32 devices in a mesh: ctx: 8 (over z, core), heads: 4 (over y, x).
Axes of the slice: x: 2, y: 2, z: 4, core: 2. Of those that a mesh axis runs over, the one named last changes fastest.
Arguments:
- queries: bfloat16 [2048, 8192], P('ctx', 'heads'), may hold values from -6 to 6
- keys: bfloat16 [2048, 8192], P('ctx', 'heads'), may hold values from -6 to 6
- values: bfloat16 [2048, 8192], P('ctx', 'heads'), may hold values from -60 to 60
- hyena_inputs: bfloat16 [3, 2048, 8192], P(None, 'ctx', 'heads'), may hold values from -6 to 6
- hyena_filter: float32 [7, 8192], P(None, 'heads'), may hold values from -2.4 to 2.4
- norm_gain: float32 [8192], P('heads'), may hold values from 0.5 to 1.5
Outputs:
- mixed: bfloat16 [2048, 8192], P('ctx', 'heads')
The draws below stay inside these ranges and needn't reach their ends.
All inputs are finite; a program needn't handle non-finite values.
Results may differ from the reference program's by a relative error of at most 0.009.
Values may be sent and summed in bfloat16 or wider, within the bound.
A program may use at most 64 MiB of HBM per device.

```python
import math
import jax
import jax.numpy as jnp
from jax import lax

HEADS = 64
DH = 128
FILT = 7
WIDTH = 8192
SEQ = 2048


def base_draw(key):
    return jnp.clip(jax.random.normal(key, (SEQ, WIDTH), jnp.float32), -5.0, 5.0)


def draw_queries(key, part):
    result = base_draw(jax.random.fold_in(key, 1))
    return result.astype(jnp.bfloat16)


def draw_keys(key, part):
    result = base_draw(jax.random.fold_in(key, 2))
    return result.astype(jnp.bfloat16)


def draw_values(key, part):
    result = base_draw(jax.random.fold_in(key, 3))
    column_place = jnp.arange(WIDTH, dtype=jnp.float32)[None, :] / WIDTH
    row_level = jax.random.uniform(jax.random.fold_in(key, 4), (SEQ, 1), jnp.float32, 0.0, 1.0)
    column_scale = jnp.power(10.0, column_place - 0.5)
    row_scale = jnp.power(10.0, row_level - 0.5)
    return (result * column_scale * row_scale).astype(jnp.bfloat16)


def block_scale(stream_key, extent, pieces, least, largest):
    gain = 1.0
    for axis_at, parts in pieces:
        heights = jax.random.uniform(jax.random.fold_in(jax.random.fold_in(stream_key, 6), axis_at), (parts,), jnp.float32, least / len(pieces), largest / len(pieces))
        gain = gain * jnp.repeat(jnp.exp(heights), extent[axis_at] // parts).reshape((-1,) + (1,) * (len(extent) - 1 - axis_at))
    return gain


def normal_values(stream_key, shape, scale, limit, split=(), kind=jnp.bfloat16):
    values = jax.random.normal(stream_key, shape, jnp.float32) * scale
    if len(split) > 0:
        values = block_scale(stream_key, shape, split, -0.22, 0.18) * values
    return jnp.clip(values, min=-limit, max=limit).astype(kind)


def setup_inputs(seed: int = 0) -> dict:
    key_list = jax.random.split(jax.random.key(seed), 7)
    return {
        "queries": draw_queries(jax.random.fold_in(key_list[6], 71), 0),
        "keys": draw_keys(jax.random.fold_in(key_list[6], 71), 0),
        "values": draw_values(jax.random.fold_in(key_list[6], 71), 0),
        "hyena_inputs": normal_values(key_list[3], (3, SEQ, WIDTH), 1.0, 6.0, ((1, 8), (2, 4))),
        "hyena_filter": normal_values(key_list[4], (FILT, WIDTH), 0.4, 2.4, ((1, 4),), jnp.float32),
        "norm_gain": jnp.clip(1.0 + 0.1 * jax.random.normal(key_list[5], (WIDTH,), jnp.float32), 0.5, 1.5),
    }


def head_attention(query_head, key_head, value_head):
    block_rows = math.gcd(SEQ, 1024)
    key_place = jnp.arange(SEQ, dtype=jnp.int32)
    score_scale = 1.0 / math.sqrt(DH)

    def one_block(block_start):
        query_block = lax.dynamic_slice_in_dim(query_head, block_start, block_rows, 0)
        scores = jnp.dot(query_block, key_head.T, preferred_element_type=jnp.float32) * score_scale
        query_place = block_start + jnp.arange(block_rows, dtype=jnp.int32)
        visible = key_place[None, :] <= query_place[:, None]
        scores = jnp.where(visible, scores, -1e+30)
        row_top = lax.optimization_barrier(jnp.max(scores, axis=1, keepdims=True))
        weights = jnp.where(visible, jnp.exp(scores - row_top), 0.0)
        totals = lax.optimization_barrier(jnp.sum(weights, axis=1, keepdims=True))
        summed = jnp.dot(weights.astype(jnp.bfloat16), value_head, preferred_element_type=jnp.float32)
        return summed / totals
    starts = (jnp.arange(SEQ // block_rows, dtype=jnp.int32) * block_rows).astype(jnp.int32)
    return lax.map(one_block, starts).reshape(SEQ, DH)

def reference(queries, keys, values, hyena_inputs, hyena_filter, norm_gain):

    def split_heads(array):
        return jnp.transpose(array.reshape(SEQ, HEADS, DH), (1, 0, 2))
    per_head = lax.map(lambda triple: head_attention(triple[0], triple[1], triple[2]), (split_heads(queries), split_heads(keys), split_heads(values)))
    attention = jnp.transpose(per_head, (1, 0, 2)).reshape(SEQ, WIDTH).astype(jnp.bfloat16)
    attention_wide = lax.optimization_barrier(attention).astype(jnp.float32)
    square_mean = lax.optimization_barrier(jnp.sum(attention_wide * attention_wide, axis=1)) / WIDTH
    product = hyena_inputs[1].astype(jnp.float32) * hyena_inputs[2].astype(jnp.float32)
    padded = jnp.concatenate([jnp.zeros((FILT - 1, WIDTH), jnp.float32), product], axis=0)
    convolved = jnp.zeros((SEQ, WIDTH), jnp.float32)
    for filter_tap in range(FILT):
        convolved = convolved + hyena_filter[filter_tap][None, :] * padded[FILT - 1 - filter_tap:FILT - 1 - filter_tap + SEQ]
    hyena_out = hyena_inputs[0].astype(jnp.float32) * convolved
    normed = attention_wide * lax.rsqrt(square_mean + 1e-06)[:, None] * norm_gain[None, :]
    return (normed + hyena_out).astype(jnp.bfloat16)
```

```python
import functools
import math

import jax
import jax.numpy as jnp
from jax import lax
from jax.experimental import pallas as pl
from jax.experimental.pallas import tpu as pltpu
from jax.sharding import PartitionSpec as P

DH = 128
WIDTH = 8192
MESH = pl.DeviceIdType.MESH
LOG2E = 1.4426950408889634
CHUNK_HEADS = 2
RIM = 16
K_UP, V_UP, K_SIDE, V_SIDE, Q_NEAR, Q_FAR, O_NEAR, O_FAR, S_NEAR, S_FAR, SINGLES, SQUARES = range(12)


def from_behind(array, axis, by):
    size = lax.axis_size(axis)
    pairs = [(i, i + by) for i in range(size) if 0 <= i + by < size]
    return lax.ppermute(array, axis, pairs)


def attend(half_state, query_block, query_place, key_block, value_block, key_place):
    numerator, maxima, totals = half_state
    score_scale = 1.0 / math.sqrt(query_block.shape[2])
    scores = (
        jnp.einsum("qhd,khd->qhk", query_block, key_block, preferred_element_type=jnp.float32)
        * score_scale
    )
    visible = key_place[None, None, :] <= query_place[:, None, None]
    scores = jnp.where(visible, scores, -1e30)
    row_top = jnp.maximum(maxima, jnp.max(scores, axis=2))
    rescale = jnp.exp(maxima - row_top)
    weights = jnp.where(visible, jnp.exp(scores - row_top[:, :, None]), 0.0)
    totals = totals * rescale + jnp.sum(weights, axis=2)
    summed = jnp.einsum(
        "qhk,khd->qhd",
        weights.astype(jnp.bfloat16),
        value_block,
        preferred_element_type=jnp.float32,
    )
    numerator = numerator * rescale[:, :, None] + summed
    return (numerator, row_top, totals)


def fresh_state(row_total, head_total, head_size):
    return (
        jnp.zeros((row_total, head_total, head_size), jnp.float32),
        jnp.full((row_total, head_total), -1e30, jnp.float32),
        jnp.zeros((row_total, head_total), jnp.float32),
    )


def cycle_attention(queries, keys, values):
    row_count, col_count = queries.shape
    head_count = col_count // DH
    half_rows = row_count // 2
    ctx_index = lax.axis_index("ctx")
    query_starts = (ctx_index * row_count, ctx_index * row_count + half_rows)
    query_heads = queries.reshape(row_count, head_count, DH)
    query_halves = (query_heads[:half_rows], query_heads[half_rows:])
    query_places = tuple(
        (query_starts[number] + jnp.arange(half_rows, dtype=jnp.int32) for number in range(2))
    )
    empty_state = fresh_state(half_rows, head_count, DH)
    key_rows = lax.all_gather(keys, "ctx", axis=0, tiled=True)
    value_rows = lax.all_gather(values, "ctx", axis=0, tiled=True)
    count = key_rows.shape[0]
    block_rows = math.gcd(count, half_rows)
    key_heads = key_rows.reshape(count, head_count, DH)
    value_heads = value_rows.reshape(count, head_count, DH)

    def inner(block_index, state):
        first = block_index * block_rows
        key_block = lax.dynamic_slice_in_dim(key_heads, first, block_rows, 0)
        value_block = lax.dynamic_slice_in_dim(value_heads, first, block_rows, 0)
        key_place = first + jnp.arange(block_rows, dtype=jnp.int32)
        updated = []
        for number in range(2):
            query_block = query_halves[number]
            query_place = query_places[number]

            def update(half_state):
                return attend(
                    half_state, query_block, query_place, key_block, value_block, key_place
                )

            needed = key_place[0] <= query_place[half_rows - 1]
            updated.append(lax.cond(needed, update, lambda half_state: half_state, state[number]))
        return tuple(updated)

    finished = lax.fori_loop(0, count // block_rows, inner, (empty_state, empty_state))
    halves_out = [finished[number][0] / finished[number][2][:, :, None] for number in range(2)]
    return jnp.concatenate(halves_out, axis=0).reshape(row_count, col_count).astype(jnp.bfloat16)


def fused_kernel(
    ctx_size, heads_size,
    q_any, k_any, v_any, hy_any, filt, gain, out,
    k_all, v_all, q_own, q_far, o_got, s_got, o_put, s_put, o_home, s_home,
    att, hy, halo, prod, hyena, squares,
    send_sem, recv_sem, local_sem,
):
    rows, cols = out.shape
    chunks = cols // DH // CHUNK_HEADS
    wide = CHUNK_HEADS * DH
    ctx = lax.axis_index("ctx")
    mine = lax.axis_index("heads")
    core = lax.rem(ctx, 2)
    place = ctx // 2
    side = ctx + 1 - 2 * core
    factor = LOG2E / math.sqrt(DH)

    barrier = pltpu.get_barrier_semaphore()
    for step in range(1, ctx_size):
        pl.semaphore_signal(
            barrier, inc=1, device_id={"ctx": lax.rem(ctx + step, ctx_size)}, device_id_type=MESH
        )
    for step in range(1, heads_size):
        pl.semaphore_signal(
            barrier, inc=1, device_id={"heads": lax.rem(mine + step, heads_size)}, device_id_type=MESH
        )
    pl.semaphore_wait(barrier, ctx_size + heads_size - 2)

    def remote(src, dst, kind, at, target):
        return pltpu.make_async_remote_copy(
            src_ref=src, dst_ref=dst, send_sem=send_sem.at[kind, at], recv_sem=recv_sem.at[kind, at],
            device_id={"ctx": target}, device_id_type=MESH,
        )

    def arrived(dst, kind, at):
        remote(dst, dst, kind, at, side).wait_recv()

    def sent(src, kind, at):
        remote(src, src, kind, at, side).wait_send()

    def lanes(chunk):
        return pl.ds(pl.multiple_of(chunk * wide, wide), wide)

    def head_lanes(head):
        return pl.ds(pl.multiple_of(head * DH, DH), DH)

    def each_chunk(body):
        def step(chunk, carry):
            body(chunk)
            return carry

        lax.fori_loop(0, chunks, step, 0)

    tail = hy_any.at[pl.ds(1, 2), pl.ds(rows - RIM, RIM), :]

    @pl.when(ctx < ctx_size - 1)
    def _():
        remote(tail, halo, SINGLES, 2, ctx + 1).start()

    remote(k_any, k_all.at[2 + core], SINGLES, 0, side).start()
    remote(v_any, v_all.at[2 + core], SINGLES, 1, side).start()

    @pl.when(place == 0)
    def _():
        @each_chunk
        def _(chunk):
            at = lanes(chunk)
            remote(k_any.at[:, at], k_all.at[core, :, at], K_UP, chunk, ctx + 2).start()
            remote(v_any.at[:, at], v_all.at[core, :, at], V_UP, chunk, ctx + 2).start()

    @pl.when(place == 2)
    def _():
        @each_chunk
        def _(chunk):
            at = lanes(chunk)
            remote(q_any.at[:, at], q_far.at[0, :, at], Q_NEAR, chunk, ctx - 2).start()

    @pl.when(place == 3)
    def _():
        @each_chunk
        def _(chunk):
            at = lanes(chunk)
            remote(q_any.at[:, at], q_far.at[1, :, at], Q_FAR, chunk, ctx - 4).start()
            remote(q_any.at[:, at], q_far.at[0, :, at], Q_NEAR, chunk, ctx - 2).start()

    local = [
        pltpu.make_async_copy(hy_any, hy, local_sem.at[0]),
        pltpu.make_async_copy(k_any, k_all.at[2 + core], local_sem.at[1]),
        pltpu.make_async_copy(v_any, v_all.at[2 + core], local_sem.at[2]),
        pltpu.make_async_copy(q_any, q_own, local_sem.at[3]),
    ]
    for copy in local:
        copy.start()

    @pl.when(ctx == 0)
    def _():
        halo[...] = jnp.zeros_like(halo)

    @pl.when(ctx > 0)
    def _():
        arrived(halo, SINGLES, 2)

    local[0].wait()

    @each_chunk
    def _(chunk):
        at = lanes(chunk)
        prod[:RIM] = halo[0, :, at].astype(jnp.float32) * halo[1, :, at].astype(jnp.float32)
        prod[RIM:] = hy[1, :, at].astype(jnp.float32) * hy[2, :, at].astype(jnp.float32)
        taps = filt[:, at]
        summed = taps[0:1] * prod[RIM : RIM + rows]
        for tap in range(1, filt.shape[0]):
            summed = summed + taps[tap : tap + 1] * prod[RIM - tap : RIM - tap + rows]
        hyena[:, at] = hy[0, :, at].astype(jnp.float32) * summed

    for copy in local[1:]:
        copy.wait()
    arrived(k_all.at[2], SINGLES, 0)
    arrived(v_all.at[2], SINGLES, 1)
    squares[mine] = jnp.zeros_like(squares[mine])

    key_place = lax.broadcasted_iota(jnp.int32, (rows, rows), 0)
    query_place = lax.broadcasted_iota(jnp.int32, (rows, rows), 1) + core * rows

    def scores(slot, head, query):
        return lax.dot_general(
            k_all[slot, :, head_lanes(head)], query, (((1,), (1,)), ((), ())),
            preferred_element_type=jnp.float32,
        )

    def turned(slot, head):
        return v_all[slot, :, head_lanes(head)].T

    def attend_some(head, query, slots, turned_values, masked):
        tiles = [scores(slot, head, query) for slot in slots]
        if masked:
            tiles = [
                jnp.where(key_place + (slot - 2) * rows <= query_place, tile, -1e30) if slot >= 2 else tile
                for slot, tile in zip(slots, tiles)
            ]
        top = functools.reduce(jnp.maximum, [jnp.max(tile, axis=0, keepdims=True) for tile in tiles])
        total, numerator = 0.0, 0.0
        for tile, value in zip(tiles, turned_values):
            weights = jnp.exp2((tile - top) * factor)
            total = total + jnp.sum(weights, axis=0, keepdims=True)
            numerator = numerator + jnp.dot(
                value, weights.astype(jnp.bfloat16), preferred_element_type=jnp.float32
            )
        return numerator / total, top * factor + jnp.log(total) * LOG2E

    def finish(head, value):
        rounded = value.astype(jnp.bfloat16).astype(jnp.float32)
        squares[mine] += jnp.sum((rounded * rounded).reshape(DH // 8, 8, rows), axis=0)
        att[:, head_lanes(head)] = rounded.T.astype(jnp.bfloat16)

    def head_rows(head):
        return pl.ds(pl.multiple_of(head * DH, DH), DH)

    def chunk_rows(chunk):
        return pl.ds(pl.multiple_of(chunk * wide, wide), wide)

    def partial_out(slot, chunk, index, head, result):
        value, log_total = result
        o_put[slot, head_rows(head), :] = value.astype(jnp.bfloat16)
        s_put[slot, chunk, index : index + 1, :] = log_total

    def send_out(slot, chunk, to_slot, target):
        at = chunk_rows(chunk)
        remote(o_put.at[slot, at], o_got.at[to_slot, at], O_NEAR + to_slot, chunk, target).start()
        remote(s_put.at[slot, chunk], s_got.at[to_slot, chunk], S_NEAR + to_slot, chunk, target).start()

    def own_query(head):
        return q_own[:, head_lanes(head)]

    @pl.when(place == 0)
    def _():
        @each_chunk
        def _(chunk):
            for index in range(CHUNK_HEADS):
                head = chunk * CHUNK_HEADS + index
                values = [turned(slot, head) for slot in (2, 3)]
                finish(head, attend_some(head, own_query(head), (2, 3), values, True)[0])

    @pl.when(place == 1)
    def _():
        s_put[...] = jnp.zeros_like(s_put)

        @each_chunk
        def _(chunk):
            at = lanes(chunk)
            arrived(k_all.at[core, :, at], K_UP, chunk)
            remote(k_all.at[core, :, at], k_all.at[core, :, at], K_SIDE, chunk, side).start()
            arrived(v_all.at[core, :, at], V_UP, chunk)
            remote(v_all.at[core, :, at], v_all.at[core, :, at], V_SIDE, chunk, side).start()
            arrived(q_far.at[0, :, at], Q_NEAR, chunk)
            arrived(q_far.at[1, :, at], Q_FAR, chunk)
            arrived(k_all.at[1 - core, :, at], K_SIDE, chunk)
            arrived(v_all.at[1 - core, :, at], V_SIDE, chunk)
            slots = (0, 1, 2, 3)
            for index in range(CHUNK_HEADS):
                head = chunk * CHUNK_HEADS + index
                values = [turned(slot, head) for slot in slots]
                for far in range(2):
                    query = q_far[far, :, head_lanes(head)]
                    partial_out(far, chunk, index, head, attend_some(head, query, slots, values, False))
                finish(head, attend_some(head, own_query(head), slots, values, True)[0])
            send_out(0, chunk, 0, ctx + 2)
            send_out(1, chunk, 1, ctx + 4)

    @pl.when(place == 2)
    def _():
        s_put[...] = jnp.zeros_like(s_put)

        @each_chunk
        def _(chunk):
            arrived(q_far.at[0, :, lanes(chunk)], Q_NEAR, chunk)
            for index in range(CHUNK_HEADS):
                head = chunk * CHUNK_HEADS + index
                values = [turned(slot, head) for slot in (2, 3)]
                query = q_far[0, :, head_lanes(head)]
                partial_out(0, chunk, index, head, attend_some(head, query, (2, 3), values, False))
                value, log_total = attend_some(head, own_query(head), (2, 3), values, True)
                o_home[head_rows(head), :] = value
                s_home[chunk, index : index + 1, :] = log_total
            send_out(0, chunk, 0, ctx + 2)

    @pl.when(place == 3)
    def _():
        @each_chunk
        def _(chunk):
            for index in range(CHUNK_HEADS):
                head = chunk * CHUNK_HEADS + index
                values = [turned(slot, head) for slot in (2, 3)]
                value, log_total = attend_some(head, own_query(head), (2, 3), values, True)
                o_home[head_rows(head), :] = value
                s_home[chunk, index : index + 1, :] = log_total

    def merge(slots):
        @each_chunk
        def _(chunk):
            for slot in slots:
                arrived(o_got.at[slot, chunk_rows(chunk)], O_NEAR + slot, chunk)
                arrived(s_got.at[slot, chunk], S_NEAR + slot, chunk)
            for index in range(CHUNK_HEADS):
                head = chunk * CHUNK_HEADS + index
                logs = [s_home[chunk, index : index + 1, :]]
                parts = [o_home[head_rows(head), :]]
                for slot in slots:
                    logs.append(s_got[slot, chunk, index : index + 1, :])
                    parts.append(o_got[slot, head_rows(head), :].astype(jnp.float32))
                top = functools.reduce(jnp.maximum, logs)
                shares = [jnp.exp2(log - top) for log in logs]
                inverse = 1.0 / sum(shares)
                finish(head, sum(part * (share * inverse) for part, share in zip(parts, shares)))

    pl.when(place == 2)(lambda: merge((0,)))
    pl.when(place == 3)(lambda: merge((0, 1)))

    def square_copy(step, slot):
        return pltpu.make_async_remote_copy(
            src_ref=squares.at[slot], dst_ref=squares.at[slot],
            send_sem=send_sem.at[SQUARES, step], recv_sem=recv_sem.at[SQUARES, slot],
            device_id={"heads": lax.rem(mine + step, heads_size)}, device_id_type=MESH,
        )

    for step in range(1, heads_size):
        square_copy(step, mine).start()
    for step in range(1, heads_size):
        square_copy(step, lax.rem(mine + step, heads_size)).wait_recv()
    square_total = squares[0]
    for slot in range(1, heads_size):
        square_total = square_total + squares[slot]
    square_mean = jnp.sum(square_total, axis=0, keepdims=True) / (cols * heads_size)
    scale = jnp.broadcast_to(lax.rsqrt(square_mean + 1e-06), (DH, rows)).T

    def last(head, carry):
        at = head_lanes(head)
        out[:, at] = (att[:, at].astype(jnp.float32) * scale * gain[:, at] + hyena[:, at]).astype(jnp.bfloat16)
        return carry

    lax.fori_loop(0, cols // DH, last, 0)

    for step in range(1, heads_size):
        square_copy(step, mine).wait_send()

    @pl.when(ctx < ctx_size - 1)
    def _():
        sent(tail, SINGLES, 2)

    sent(k_any, SINGLES, 0)
    sent(v_any, SINGLES, 1)

    def sent_lanes(kinds):
        @each_chunk
        def _(chunk):
            for kind in kinds:
                sent(q_any.at[:, lanes(chunk)], kind, chunk)

    def sent_out(slots):
        @each_chunk
        def _(chunk):
            for slot in slots:
                sent(o_put.at[slot, chunk_rows(chunk)], O_NEAR + slot, chunk)
                sent(s_put.at[slot, chunk], S_NEAR + slot, chunk)

    pl.when(place == 0)(lambda: sent_lanes((K_UP, V_UP)))
    pl.when(place == 2)(lambda: sent_lanes((Q_NEAR,)))
    pl.when(place == 3)(lambda: sent_lanes((Q_NEAR, Q_FAR)))
    pl.when(place == 2)(lambda: sent_out((0,)))

    @pl.when(place == 1)
    def _():
        sent_out((0, 1))
        sent_lanes((K_SIDE, V_SIDE))


def four_places(queries, keys, values, hyena_inputs, hyena_filter, norm_gain):
    rows, cols = queries.shape
    ctx_size, heads_size = lax.axis_size("ctx"), lax.axis_size("heads")
    chunks = cols // DH // CHUNK_HEADS
    bf16, f32 = jnp.bfloat16, jnp.float32
    count = max(chunks, heads_size, 3)
    return pl.pallas_call(
        functools.partial(fused_kernel, ctx_size, heads_size),
        out_shape=jax.ShapeDtypeStruct((rows, cols), bf16),
        in_specs=[pl.BlockSpec(memory_space=pl.ANY)] * 4 + [pl.BlockSpec(memory_space=pltpu.VMEM)] * 2,
        out_specs=pl.BlockSpec(memory_space=pltpu.VMEM),
        scratch_shapes=[
            pltpu.VMEM((4, rows, cols), bf16),
            pltpu.VMEM((4, rows, cols), bf16),
            pltpu.VMEM((rows, cols), bf16),
            pltpu.VMEM((2, rows, cols), bf16),
            pltpu.VMEM((2, cols, rows), bf16),
            pltpu.VMEM((2, chunks, 8, rows), f32),
            pltpu.VMEM((2, cols, rows), bf16),
            pltpu.VMEM((2, chunks, 8, rows), f32),
            pltpu.VMEM((cols, rows), f32),
            pltpu.VMEM((chunks, 8, rows), f32),
            pltpu.VMEM((rows, cols), bf16),
            pltpu.VMEM(hyena_inputs.shape, bf16),
            pltpu.VMEM((2, RIM, cols), bf16),
            pltpu.VMEM((RIM + rows, CHUNK_HEADS * DH), f32),
            pltpu.VMEM((rows, cols), f32),
            pltpu.VMEM((heads_size, 8, rows), f32),
            pltpu.SemaphoreType.DMA((12, count)),
            pltpu.SemaphoreType.DMA((12, count)),
            pltpu.SemaphoreType.DMA((4,)),
        ],
        compiler_params=pltpu.CompilerParams(
            collective_id=0, has_side_effects=True, vmem_limit_bytes=50 * 1024 * 1024
        ),
    )(queries, keys, values, hyena_inputs, hyena_filter, norm_gain[None, :])


def on_device(queries, keys, values, hyena_inputs, hyena_filter, norm_gain):
    if lax.axis_size("ctx") == 2 * 4:
        return four_places(queries, keys, values, hyena_inputs, hyena_filter, norm_gain)
    row_count, col_count = queries.shape
    rim_rows = hyena_filter.shape[0] - 1
    tail_rows = hyena_inputs[1:, row_count - rim_rows :, :]
    earlier = from_behind(tail_rows, "ctx", 1)
    joined = jnp.concatenate([earlier, hyena_inputs[1:]], axis=1)
    product = joined[0].astype(jnp.float32) * joined[1].astype(jnp.float32)
    convolved = jnp.zeros((row_count, col_count), jnp.float32)
    for filter_tap in range(rim_rows + 1):
        convolved = (
            convolved
            + hyena_filter[filter_tap][None, :]
            * product[rim_rows - filter_tap : rim_rows - filter_tap + row_count]
        )
    hyena_out = hyena_inputs[0].astype(jnp.float32) * convolved
    attention = cycle_attention(queries, keys, values)
    attention_wide = lax.optimization_barrier(attention).astype(jnp.float32)
    local_squares = jnp.sum(attention_wide * attention_wide, axis=1)
    square_total = lax.psum(local_squares, "heads")
    square_mean = square_total / WIDTH
    normed = attention_wide * lax.rsqrt(square_mean + 1e-06)[:, None] * norm_gain[None, :]
    return (normed + hyena_out).astype(jnp.bfloat16)


def solution(mesh):
    placed = (
        P("ctx", "heads"),
        P("ctx", "heads"),
        P("ctx", "heads"),
        P(None, "ctx", "heads"),
        P(None, "heads"),
        P("heads"),
    )
    return jax.shard_map(
        on_device, mesh=mesh, in_specs=placed, out_specs=P("ctx", "heads"), check_vma=False
    )
```

```python
import functools
import math

import jax
import jax.numpy as jnp
from jax import lax
from jax.experimental import pallas as pl
from jax.experimental.pallas import tpu as pltpu
from jax.sharding import PartitionSpec as P

DH = 128
WIDTH = 8192
MESH = pl.DeviceIdType.MESH
LOG2E = 1.4426950408889634
CHUNK_HEADS = 2
DEPTH = 2
RIM = 16
K_UP, V_UP, K_SIDE, V_SIDE, Q_NEAR, Q_FAR, O_NEAR, O_FAR, S_NEAR, S_FAR, SINGLES, SQUARES = range(12)


def from_behind(array, axis, by):
    size = lax.axis_size(axis)
    pairs = [(i, i + by) for i in range(size) if 0 <= i + by < size]
    return lax.ppermute(array, axis, pairs)


def attend(half_state, query_block, query_place, key_block, value_block, key_place):
    numerator, maxima, totals = half_state
    score_scale = 1.0 / math.sqrt(query_block.shape[2])
    scores = (
        jnp.einsum("qhd,khd->qhk", query_block, key_block, preferred_element_type=jnp.float32)
        * score_scale
    )
    visible = key_place[None, None, :] <= query_place[:, None, None]
    scores = jnp.where(visible, scores, -1e30)
    row_top = jnp.maximum(maxima, jnp.max(scores, axis=2))
    rescale = jnp.exp(maxima - row_top)
    weights = jnp.where(visible, jnp.exp(scores - row_top[:, :, None]), 0.0)
    totals = totals * rescale + jnp.sum(weights, axis=2)
    summed = jnp.einsum(
        "qhk,khd->qhd",
        weights.astype(jnp.bfloat16),
        value_block,
        preferred_element_type=jnp.float32,
    )
    numerator = numerator * rescale[:, :, None] + summed
    return (numerator, row_top, totals)


def fresh_state(row_total, head_total, head_size):
    return (
        jnp.zeros((row_total, head_total, head_size), jnp.float32),
        jnp.full((row_total, head_total), -1e30, jnp.float32),
        jnp.zeros((row_total, head_total), jnp.float32),
    )


def cycle_attention(queries, keys, values):
    row_count, col_count = queries.shape
    head_count = col_count // DH
    half_rows = row_count // 2
    ctx_index = lax.axis_index("ctx")
    query_starts = (ctx_index * row_count, ctx_index * row_count + half_rows)
    query_heads = queries.reshape(row_count, head_count, DH)
    query_halves = (query_heads[:half_rows], query_heads[half_rows:])
    query_places = tuple(
        (query_starts[number] + jnp.arange(half_rows, dtype=jnp.int32) for number in range(2))
    )
    empty_state = fresh_state(half_rows, head_count, DH)
    key_rows = lax.all_gather(keys, "ctx", axis=0, tiled=True)
    value_rows = lax.all_gather(values, "ctx", axis=0, tiled=True)
    count = key_rows.shape[0]
    block_rows = math.gcd(count, half_rows)
    key_heads = key_rows.reshape(count, head_count, DH)
    value_heads = value_rows.reshape(count, head_count, DH)

    def inner(block_index, state):
        first = block_index * block_rows
        key_block = lax.dynamic_slice_in_dim(key_heads, first, block_rows, 0)
        value_block = lax.dynamic_slice_in_dim(value_heads, first, block_rows, 0)
        key_place = first + jnp.arange(block_rows, dtype=jnp.int32)
        updated = []
        for number in range(2):
            query_block = query_halves[number]
            query_place = query_places[number]

            def update(half_state):
                return attend(
                    half_state, query_block, query_place, key_block, value_block, key_place
                )

            needed = key_place[0] <= query_place[half_rows - 1]
            updated.append(lax.cond(needed, update, lambda half_state: half_state, state[number]))
        return tuple(updated)

    finished = lax.fori_loop(0, count // block_rows, inner, (empty_state, empty_state))
    halves_out = [finished[number][0] / finished[number][2][:, :, None] for number in range(2)]
    return jnp.concatenate(halves_out, axis=0).reshape(row_count, col_count).astype(jnp.bfloat16)


def fused_kernel(
    ctx_size, heads_size,
    q_any, k_any, v_any, hy_any, filt_any, gain_any, out,
    k_all, v_all, q_own, q_far, o_got, s_got, o_put, s_put, o_home, s_home,
    att, hy, halo, prod, hyena, squares, filt, gain,
    send_sem, recv_sem, local_sem,
):
    rows, cols = out.shape
    chunks = cols // DH // CHUNK_HEADS
    wide = CHUNK_HEADS * DH
    ctx = lax.axis_index("ctx")
    mine = lax.axis_index("heads")
    core = lax.rem(ctx, 2)
    place = ctx // 2
    side = ctx + 1 - 2 * core
    factor = LOG2E / math.sqrt(DH)

    local = [
        pltpu.make_async_copy(hy_any, hy, local_sem.at[0]),
        pltpu.make_async_copy(filt_any, filt, local_sem.at[1]),
        pltpu.make_async_copy(k_any, k_all.at[2 + core], local_sem.at[2]),
        pltpu.make_async_copy(v_any, v_all.at[2 + core], local_sem.at[3]),
        pltpu.make_async_copy(q_any, q_own, local_sem.at[4]),
        pltpu.make_async_copy(gain_any, gain, local_sem.at[5]),
    ]
    barrier = pltpu.get_barrier_semaphore()
    for step in range(1, ctx_size):
        pl.semaphore_signal(
            barrier, inc=1, device_id={"ctx": lax.rem(ctx + step, ctx_size)}, device_id_type=MESH
        )
    for step in range(1, heads_size):
        pl.semaphore_signal(
            barrier, inc=1, device_id={"heads": lax.rem(mine + step, heads_size)}, device_id_type=MESH
        )
    for copy in local:
        copy.start()
    pl.semaphore_wait(barrier, ctx_size + heads_size - 2)

    def remote(src, dst, kind, at, target):
        return pltpu.make_async_remote_copy(
            src_ref=src, dst_ref=dst, send_sem=send_sem.at[kind, at], recv_sem=recv_sem.at[kind, at],
            device_id={"ctx": target}, device_id_type=MESH,
        )

    def arrived(dst, kind, at):
        remote(dst, dst, kind, at, side).wait_recv()

    def sent(src, kind, at):
        remote(src, src, kind, at, side).wait_send()

    def lanes(chunk):
        return pl.ds(pl.multiple_of(chunk * wide, wide), wide)

    def head_lanes(head):
        return pl.ds(pl.multiple_of(head * DH, DH), DH)

    def each_chunk(body):
        def step(chunk, carry):
            body(chunk)
            return carry

        lax.fori_loop(0, chunks, step, 0)

    tail = hy_any.at[pl.ds(1, 2), pl.ds(rows - RIM, RIM), :]

    @pl.when(ctx < ctx_size - 1)
    def _():
        remote(tail, halo, SINGLES, 2, ctx + 1).start()

    remote(k_any, k_all.at[2 + core], SINGLES, 0, side).start()
    remote(v_any, v_all.at[2 + core], SINGLES, 1, side).start()

    def up_copies(chunk):
        at = lanes(chunk)
        return (
            remote(k_any.at[:, at], k_all.at[core, :, at], K_UP, chunk, ctx + 2),
            remote(v_any.at[:, at], v_all.at[core, :, at], V_UP, chunk, ctx + 2),
        )

    def near_copies(chunk):
        at = lanes(chunk)
        return (remote(q_any.at[:, at], q_far.at[0, :, at], Q_NEAR, chunk, ctx - 2),)

    def far_copies(chunk):
        at = lanes(chunk)
        return (remote(q_any.at[:, at], q_far.at[1, :, at], Q_FAR, chunk, ctx - 4),) + near_copies(chunk)

    def begin(copies, depth):
        for chunk in range(depth):
            for copy in copies(chunk):
                copy.start()

    def follow(copies, depth, chunk):
        for copy in copies(chunk):
            copy.wait_send()

        @pl.when(chunk + depth < chunks)
        def _():
            for copy in copies(chunk + depth):
                copy.start()

    pl.when(place == 0)(lambda: begin(up_copies, DEPTH))
    pl.when(place == 2)(lambda: begin(near_copies, 2 * DEPTH))
    pl.when(place == 3)(lambda: begin(far_copies, DEPTH))

    @pl.when(ctx == 0)
    def _():
        halo[...] = jnp.zeros_like(halo)

    @pl.when(ctx > 0)
    def _():
        arrived(halo, SINGLES, 2)

    for copy in local[:2]:
        copy.wait()

    @each_chunk
    def _(chunk):
        at = lanes(chunk)
        prod[:RIM] = halo[0, :, at].astype(jnp.float32) * halo[1, :, at].astype(jnp.float32)
        prod[RIM:] = hy[1, :, at].astype(jnp.float32) * hy[2, :, at].astype(jnp.float32)
        taps = filt[:, at]
        summed = taps[0:1] * prod[RIM : RIM + rows]
        for tap in range(1, filt.shape[0]):
            summed = summed + taps[tap : tap + 1] * prod[RIM - tap : RIM - tap + rows]
        hyena[:, at] = hy[0, :, at].astype(jnp.float32) * summed

    for copy in local[2:]:
        copy.wait()
    arrived(k_all.at[2], SINGLES, 0)
    arrived(v_all.at[2], SINGLES, 1)
    squares[mine] = jnp.zeros_like(squares[mine])

    key_place = lax.broadcasted_iota(jnp.int32, (rows, rows), 0)
    query_place = lax.broadcasted_iota(jnp.int32, (rows, rows), 1) + core * rows

    def scores(slot, head, query):
        return lax.dot_general(
            k_all[slot, :, head_lanes(head)], query, (((1,), (1,)), ((), ())),
            preferred_element_type=jnp.float32,
        )

    def turned(slot, head):
        return v_all[slot, :, head_lanes(head)].T

    def attend_some(head, query, slots, turned_values, masked):
        tiles = [scores(slot, head, query) for slot in slots]
        if masked:
            tiles = [
                jnp.where(key_place + (slot - 2) * rows <= query_place, tile, -1e30) if slot >= 2 else tile
                for slot, tile in zip(slots, tiles)
            ]
        top = functools.reduce(jnp.maximum, [jnp.max(tile, axis=0, keepdims=True) for tile in tiles])
        total, numerator = 0.0, 0.0
        for tile, value in zip(tiles, turned_values):
            weights = jnp.exp2((tile - top) * factor)
            total = total + jnp.sum(weights, axis=0, keepdims=True)
            numerator = numerator + jnp.dot(
                value, weights.astype(jnp.bfloat16), preferred_element_type=jnp.float32
            )
        return numerator / total, top * factor + jnp.log(total) * LOG2E

    def finish(head, value):
        rounded = value.astype(jnp.bfloat16).astype(jnp.float32)
        squares[mine] += jnp.sum((rounded * rounded).reshape(DH // 8, 8, rows), axis=0)
        att[:, head_lanes(head)] = rounded.T.astype(jnp.bfloat16)

    def head_rows(head):
        return pl.ds(pl.multiple_of(head * DH, DH), DH)

    def chunk_rows(chunk):
        return pl.ds(pl.multiple_of(chunk * wide, wide), wide)

    def partial_out(slot, chunk, index, head, result):
        value, log_total = result
        o_put[slot, head_rows(head), :] = value.astype(jnp.bfloat16)
        s_put[slot, chunk, index : index + 1, :] = log_total

    def send_out(slot, chunk, to_slot, target):
        at = chunk_rows(chunk)
        remote(o_put.at[slot, at], o_got.at[to_slot, at], O_NEAR + to_slot, chunk, target).start()
        remote(s_put.at[slot, chunk], s_got.at[to_slot, chunk], S_NEAR + to_slot, chunk, target).start()

    def own_query(head):
        return q_own[:, head_lanes(head)]

    @pl.when(place == 0)
    def _():
        @each_chunk
        def _(chunk):
            follow(up_copies, DEPTH, chunk)
            for index in range(CHUNK_HEADS):
                head = chunk * CHUNK_HEADS + index
                values = [turned(slot, head) for slot in (2, 3)]
                finish(head, attend_some(head, own_query(head), (2, 3), values, True)[0])

    @pl.when(place == 1)
    def _():
        s_put[...] = jnp.zeros_like(s_put)

        @each_chunk
        def _(chunk):
            at = lanes(chunk)
            arrived(k_all.at[core, :, at], K_UP, chunk)
            remote(k_all.at[core, :, at], k_all.at[core, :, at], K_SIDE, chunk, side).start()
            arrived(v_all.at[core, :, at], V_UP, chunk)
            remote(v_all.at[core, :, at], v_all.at[core, :, at], V_SIDE, chunk, side).start()
            arrived(q_far.at[0, :, at], Q_NEAR, chunk)
            arrived(q_far.at[1, :, at], Q_FAR, chunk)
            arrived(k_all.at[1 - core, :, at], K_SIDE, chunk)
            arrived(v_all.at[1 - core, :, at], V_SIDE, chunk)
            slots = (0, 1, 2, 3)
            heads = [chunk * CHUNK_HEADS + index for index in range(CHUNK_HEADS)]
            values = [[turned(slot, head) for slot in slots] for head in heads]
            for far in (1, 0):
                for index, head in enumerate(heads):
                    query = q_far[far, :, head_lanes(head)]
                    result = attend_some(head, query, slots, values[index], False)
                    partial_out(far, chunk, index, head, result)
                send_out(far, chunk, far, ctx + 2 + 2 * far)
            for index, head in enumerate(heads):
                finish(head, attend_some(head, own_query(head), slots, values[index], True)[0])

    @pl.when(place == 2)
    def _():
        s_put[...] = jnp.zeros_like(s_put)

        @each_chunk
        def _(chunk):
            follow(near_copies, 2 * DEPTH, chunk)
            arrived(q_far.at[0, :, lanes(chunk)], Q_NEAR, chunk)
            for index in range(CHUNK_HEADS):
                head = chunk * CHUNK_HEADS + index
                values = [turned(slot, head) for slot in (2, 3)]
                query = q_far[0, :, head_lanes(head)]
                partial_out(0, chunk, index, head, attend_some(head, query, (2, 3), values, False))
                value, log_total = attend_some(head, own_query(head), (2, 3), values, True)
                o_home[head_rows(head), :] = value
                s_home[chunk, index : index + 1, :] = log_total
            send_out(0, chunk, 0, ctx + 2)

    @pl.when(place == 3)
    def _():
        @each_chunk
        def _(chunk):
            follow(far_copies, DEPTH, chunk)
            for index in range(CHUNK_HEADS):
                head = chunk * CHUNK_HEADS + index
                values = [turned(slot, head) for slot in (2, 3)]
                value, log_total = attend_some(head, own_query(head), (2, 3), values, True)
                o_home[head_rows(head), :] = value
                s_home[chunk, index : index + 1, :] = log_total

    def merge(slots):
        @each_chunk
        def _(chunk):
            for slot in slots:
                arrived(o_got.at[slot, chunk_rows(chunk)], O_NEAR + slot, chunk)
                arrived(s_got.at[slot, chunk], S_NEAR + slot, chunk)
            for index in range(CHUNK_HEADS):
                head = chunk * CHUNK_HEADS + index
                logs = [s_home[chunk, index : index + 1, :]]
                parts = [o_home[head_rows(head), :]]
                for slot in slots:
                    logs.append(s_got[slot, chunk, index : index + 1, :])
                    parts.append(o_got[slot, head_rows(head), :].astype(jnp.float32))
                top = functools.reduce(jnp.maximum, logs)
                shares = [jnp.exp2(log - top) for log in logs]
                inverse = 1.0 / sum(shares)
                finish(head, sum(part * (share * inverse) for part, share in zip(parts, shares)))

    pl.when(place == 2)(lambda: merge((0,)))
    pl.when(place == 3)(lambda: merge((0, 1)))

    def square_copy(step, slot):
        return pltpu.make_async_remote_copy(
            src_ref=squares.at[slot], dst_ref=squares.at[slot],
            send_sem=send_sem.at[SQUARES, step], recv_sem=recv_sem.at[SQUARES, slot],
            device_id={"heads": lax.rem(mine + step, heads_size)}, device_id_type=MESH,
        )

    for step in range(1, heads_size):
        square_copy(step, mine).start()
    for step in range(1, heads_size):
        square_copy(step, lax.rem(mine + step, heads_size)).wait_recv()
    square_total = squares[0]
    for slot in range(1, heads_size):
        square_total = square_total + squares[slot]
    square_mean = jnp.sum(square_total, axis=0, keepdims=True) / (cols * heads_size)
    scale = jnp.broadcast_to(lax.rsqrt(square_mean + 1e-06), (DH, rows)).T

    def last(head, carry):
        at = head_lanes(head)
        out[:, at] = (att[:, at].astype(jnp.float32) * scale * gain[:, at] + hyena[:, at]).astype(jnp.bfloat16)
        return carry

    lax.fori_loop(0, cols // DH, last, 0)

    for step in range(1, heads_size):
        square_copy(step, mine).wait_send()

    @pl.when(ctx < ctx_size - 1)
    def _():
        sent(tail, SINGLES, 2)

    sent(k_any, SINGLES, 0)
    sent(v_any, SINGLES, 1)

    def sent_lanes(kinds):
        @each_chunk
        def _(chunk):
            for kind in kinds:
                sent(q_any.at[:, lanes(chunk)], kind, chunk)

    def sent_out(slots):
        @each_chunk
        def _(chunk):
            for slot in slots:
                sent(o_put.at[slot, chunk_rows(chunk)], O_NEAR + slot, chunk)
                sent(s_put.at[slot, chunk], S_NEAR + slot, chunk)

    pl.when(place == 2)(lambda: sent_out((0,)))

    @pl.when(place == 1)
    def _():
        sent_out((0, 1))
        sent_lanes((K_SIDE, V_SIDE))


def four_places(queries, keys, values, hyena_inputs, hyena_filter, norm_gain):
    rows, cols = queries.shape
    ctx_size, heads_size = lax.axis_size("ctx"), lax.axis_size("heads")
    chunks = cols // DH // CHUNK_HEADS
    bf16, f32 = jnp.bfloat16, jnp.float32
    count = max(chunks, heads_size, 3)
    return pl.pallas_call(
        functools.partial(fused_kernel, ctx_size, heads_size),
        out_shape=jax.ShapeDtypeStruct((rows, cols), bf16),
        in_specs=[pl.BlockSpec(memory_space=pltpu.HBM)] * 6,
        out_specs=pl.BlockSpec(memory_space=pltpu.VMEM),
        scratch_shapes=[
            pltpu.VMEM((4, rows, cols), bf16),
            pltpu.VMEM((4, rows, cols), bf16),
            pltpu.VMEM((rows, cols), bf16),
            pltpu.VMEM((2, rows, cols), bf16),
            pltpu.VMEM((2, cols, rows), bf16),
            pltpu.VMEM((2, chunks, 8, rows), f32),
            pltpu.VMEM((2, cols, rows), bf16),
            pltpu.VMEM((2, chunks, 8, rows), f32),
            pltpu.VMEM((cols, rows), f32),
            pltpu.VMEM((chunks, 8, rows), f32),
            pltpu.VMEM((rows, cols), bf16),
            pltpu.VMEM(hyena_inputs.shape, bf16),
            pltpu.VMEM((2, RIM, cols), bf16),
            pltpu.VMEM((RIM + rows, CHUNK_HEADS * DH), f32),
            pltpu.VMEM((rows, cols), f32),
            pltpu.VMEM((heads_size, 8, rows), f32),
            pltpu.VMEM(hyena_filter.shape, f32),
            pltpu.VMEM((1, cols), f32),
            pltpu.SemaphoreType.DMA((12, count)),
            pltpu.SemaphoreType.DMA((12, count)),
            pltpu.SemaphoreType.DMA((6,)),
        ],
        compiler_params=pltpu.CompilerParams(
            collective_id=0, has_side_effects=True, vmem_limit_bytes=63 * 1024 * 1024
        ),
    )(queries, keys, values, hyena_inputs, hyena_filter, norm_gain[None, :])


def on_device(queries, keys, values, hyena_inputs, hyena_filter, norm_gain):
    if lax.axis_size("ctx") == 2 * 4:
        return four_places(queries, keys, values, hyena_inputs, hyena_filter, norm_gain)
    row_count, col_count = queries.shape
    rim_rows = hyena_filter.shape[0] - 1
    tail_rows = hyena_inputs[1:, row_count - rim_rows :, :]
    earlier = from_behind(tail_rows, "ctx", 1)
    joined = jnp.concatenate([earlier, hyena_inputs[1:]], axis=1)
    product = joined[0].astype(jnp.float32) * joined[1].astype(jnp.float32)
    convolved = jnp.zeros((row_count, col_count), jnp.float32)
    for filter_tap in range(rim_rows + 1):
        convolved = (
            convolved
            + hyena_filter[filter_tap][None, :]
            * product[rim_rows - filter_tap : rim_rows - filter_tap + row_count]
        )
    hyena_out = hyena_inputs[0].astype(jnp.float32) * convolved
    attention = cycle_attention(queries, keys, values)
    attention_wide = lax.optimization_barrier(attention).astype(jnp.float32)
    local_squares = jnp.sum(attention_wide * attention_wide, axis=1)
    square_total = lax.psum(local_squares, "heads")
    square_mean = square_total / WIDTH
    normed = attention_wide * lax.rsqrt(square_mean + 1e-06)[:, None] * norm_gain[None, :]
    return (normed + hyena_out).astype(jnp.bfloat16)


def solution(mesh):
    placed = (
        P("ctx", "heads"),
        P("ctx", "heads"),
        P("ctx", "heads"),
        P(None, "ctx", "heads"),
        P(None, "heads"),
        P("heads"),
    )
    return jax.shard_map(
        on_device, mesh=mesh, in_specs=placed, out_specs=P("ctx", "heads"), check_vma=False
    )
```

```python
import functools
import math

import jax
import jax.numpy as jnp
from jax import lax
from jax.experimental import pallas as pl
from jax.experimental.pallas import tpu as pltpu
from jax.sharding import PartitionSpec as P

DH = 128
WIDTH = 8192
MESH = pl.DeviceIdType.MESH
LOG2E = 1.4426950408889634
CHUNK_HEADS = 2
DEPTH = 4
RIM = 16
K_UP, V_UP, K_SIDE, V_SIDE, Q_NEAR, Q_FAR, O_NEAR, O_FAR, S_NEAR, S_FAR, SINGLES, SQUARES = range(12)


def from_behind(array, axis, by):
    size = lax.axis_size(axis)
    pairs = [(i, i + by) for i in range(size) if 0 <= i + by < size]
    return lax.ppermute(array, axis, pairs)


def attend(half_state, query_block, query_place, key_block, value_block, key_place):
    numerator, maxima, totals = half_state
    score_scale = 1.0 / math.sqrt(query_block.shape[2])
    scores = (
        jnp.einsum("qhd,khd->qhk", query_block, key_block, preferred_element_type=jnp.float32)
        * score_scale
    )
    visible = key_place[None, None, :] <= query_place[:, None, None]
    scores = jnp.where(visible, scores, -1e30)
    row_top = jnp.maximum(maxima, jnp.max(scores, axis=2))
    rescale = jnp.exp(maxima - row_top)
    weights = jnp.where(visible, jnp.exp(scores - row_top[:, :, None]), 0.0)
    totals = totals * rescale + jnp.sum(weights, axis=2)
    summed = jnp.einsum(
        "qhk,khd->qhd",
        weights.astype(jnp.bfloat16),
        value_block,
        preferred_element_type=jnp.float32,
    )
    numerator = numerator * rescale[:, :, None] + summed
    return (numerator, row_top, totals)


def fresh_state(row_total, head_total, head_size):
    return (
        jnp.zeros((row_total, head_total, head_size), jnp.float32),
        jnp.full((row_total, head_total), -1e30, jnp.float32),
        jnp.zeros((row_total, head_total), jnp.float32),
    )


def cycle_attention(queries, keys, values):
    row_count, col_count = queries.shape
    head_count = col_count // DH
    half_rows = row_count // 2
    ctx_index = lax.axis_index("ctx")
    query_starts = (ctx_index * row_count, ctx_index * row_count + half_rows)
    query_heads = queries.reshape(row_count, head_count, DH)
    query_halves = (query_heads[:half_rows], query_heads[half_rows:])
    query_places = tuple(
        (query_starts[number] + jnp.arange(half_rows, dtype=jnp.int32) for number in range(2))
    )
    empty_state = fresh_state(half_rows, head_count, DH)
    key_rows = lax.all_gather(keys, "ctx", axis=0, tiled=True)
    value_rows = lax.all_gather(values, "ctx", axis=0, tiled=True)
    count = key_rows.shape[0]
    block_rows = math.gcd(count, half_rows)
    key_heads = key_rows.reshape(count, head_count, DH)
    value_heads = value_rows.reshape(count, head_count, DH)

    def inner(block_index, state):
        first = block_index * block_rows
        key_block = lax.dynamic_slice_in_dim(key_heads, first, block_rows, 0)
        value_block = lax.dynamic_slice_in_dim(value_heads, first, block_rows, 0)
        key_place = first + jnp.arange(block_rows, dtype=jnp.int32)
        updated = []
        for number in range(2):
            query_block = query_halves[number]
            query_place = query_places[number]

            def update(half_state):
                return attend(
                    half_state, query_block, query_place, key_block, value_block, key_place
                )

            needed = key_place[0] <= query_place[half_rows - 1]
            updated.append(lax.cond(needed, update, lambda half_state: half_state, state[number]))
        return tuple(updated)

    finished = lax.fori_loop(0, count // block_rows, inner, (empty_state, empty_state))
    halves_out = [finished[number][0] / finished[number][2][:, :, None] for number in range(2)]
    return jnp.concatenate(halves_out, axis=0).reshape(row_count, col_count).astype(jnp.bfloat16)


def fused_kernel(
    ctx_size, heads_size,
    q_any, k_any, v_any, hy_any, filt_any, gain_any, out,
    k_all, v_all, q_own, q_far, o_got, s_got, o_put, s_put, o_home, s_home,
    att, hy, halo, prod, hyena, squares, filt, gain,
    send_sem, recv_sem, local_sem,
):
    rows, cols = out.shape
    chunks = cols // DH // CHUNK_HEADS
    wide = CHUNK_HEADS * DH
    ctx = lax.axis_index("ctx")
    mine = lax.axis_index("heads")
    core = lax.rem(ctx, 2)
    place = ctx // 2
    side = ctx + 1 - 2 * core
    factor = LOG2E / math.sqrt(DH)

    local = [
        pltpu.make_async_copy(hy_any, hy, local_sem.at[0]),
        pltpu.make_async_copy(filt_any, filt, local_sem.at[1]),
        pltpu.make_async_copy(k_any, k_all.at[2 + core], local_sem.at[2]),
        pltpu.make_async_copy(v_any, v_all.at[2 + core], local_sem.at[3]),
        pltpu.make_async_copy(q_any, q_own, local_sem.at[4]),
        pltpu.make_async_copy(gain_any, gain, local_sem.at[5]),
    ]
    barrier = pltpu.get_barrier_semaphore()
    for step in range(1, ctx_size):
        pl.semaphore_signal(
            barrier, inc=1, device_id={"ctx": lax.rem(ctx + step, ctx_size)}, device_id_type=MESH
        )
    for step in range(1, heads_size):
        pl.semaphore_signal(
            barrier, inc=1, device_id={"heads": lax.rem(mine + step, heads_size)}, device_id_type=MESH
        )
    for copy in local:
        copy.start()
    pl.semaphore_wait(barrier, ctx_size + heads_size - 2)

    def remote(src, dst, kind, at, target):
        return pltpu.make_async_remote_copy(
            src_ref=src, dst_ref=dst, send_sem=send_sem.at[kind, at], recv_sem=recv_sem.at[kind, at],
            device_id={"ctx": target}, device_id_type=MESH,
        )

    def arrived(dst, kind, at):
        remote(dst, dst, kind, at, side).wait_recv()

    def sent(src, kind, at):
        remote(src, src, kind, at, side).wait_send()

    def lanes(chunk):
        return pl.ds(pl.multiple_of(chunk * wide, wide), wide)

    def head_lanes(head):
        return pl.ds(pl.multiple_of(head * DH, DH), DH)

    def each_chunk(body):
        def step(chunk, carry):
            body(chunk)
            return carry

        lax.fori_loop(0, chunks, step, 0)

    tail = hy_any.at[pl.ds(1, 2), pl.ds(rows - RIM, RIM), :]

    @pl.when(ctx < ctx_size - 1)
    def _():
        remote(tail, halo, SINGLES, 2, ctx + 1).start()

    remote(k_any, k_all.at[2 + core], SINGLES, 0, side).start()
    remote(v_any, v_all.at[2 + core], SINGLES, 1, side).start()

    def up_copies(chunk):
        at = lanes(chunk)
        return (
            remote(k_any.at[:, at], k_all.at[core, :, at], K_UP, chunk, ctx + 2),
            remote(v_any.at[:, at], v_all.at[core, :, at], V_UP, chunk, ctx + 2),
        )

    def near_copies(chunk):
        at = lanes(chunk)
        return (remote(q_any.at[:, at], q_far.at[0, :, at], Q_NEAR, chunk, ctx - 2),)

    def far_copies(chunk):
        at = lanes(chunk)
        return (remote(q_any.at[:, at], q_far.at[1, :, at], Q_FAR, chunk, ctx - 4),) + near_copies(chunk)

    def begin(copies, depth):
        for chunk in range(depth):
            for copy in copies(chunk):
                copy.start()

    def follow(copies, depth, chunk):
        for copy in copies(chunk):
            copy.wait_send()

        @pl.when(chunk + depth < chunks)
        def _():
            for copy in copies(chunk + depth):
                copy.start()

    pl.when(place == 0)(lambda: begin(up_copies, DEPTH))
    pl.when(place == 2)(lambda: begin(near_copies, 2 * DEPTH))
    pl.when(place == 3)(lambda: begin(far_copies, DEPTH))

    @pl.when(ctx == 0)
    def _():
        halo[...] = jnp.zeros_like(halo)

    @pl.when(ctx > 0)
    def _():
        arrived(halo, SINGLES, 2)

    for copy in local[:2]:
        copy.wait()

    @each_chunk
    def _(chunk):
        at = lanes(chunk)
        prod[:RIM] = halo[0, :, at].astype(jnp.float32) * halo[1, :, at].astype(jnp.float32)
        prod[RIM:] = hy[1, :, at].astype(jnp.float32) * hy[2, :, at].astype(jnp.float32)
        taps = filt[:, at]
        summed = taps[0:1] * prod[RIM : RIM + rows]
        for tap in range(1, filt.shape[0]):
            summed = summed + taps[tap : tap + 1] * prod[RIM - tap : RIM - tap + rows]
        hyena[:, at] = hy[0, :, at].astype(jnp.float32) * summed

    for copy in local[2:]:
        copy.wait()
    arrived(k_all.at[2], SINGLES, 0)
    arrived(v_all.at[2], SINGLES, 1)
    squares[mine] = jnp.zeros_like(squares[mine])

    key_place = lax.broadcasted_iota(jnp.int32, (rows, rows), 0)
    query_place = lax.broadcasted_iota(jnp.int32, (rows, rows), 1) + core * rows

    def scores(slot, head, query):
        return lax.dot_general(
            k_all[slot, :, head_lanes(head)], query, (((1,), (1,)), ((), ())),
            preferred_element_type=jnp.float32,
        )

    def turned(slot, head):
        return v_all[slot, :, head_lanes(head)].T

    def masked_scores(head, query, slots, masked):
        tiles = [scores(slot, head, query) for slot in slots]
        if masked:
            tiles = [
                jnp.where(key_place + (slot - 2) * rows <= query_place, tile, -1e30) if slot >= 2 else tile
                for slot, tile in zip(slots, tiles)
            ]
        return tiles, functools.reduce(jnp.maximum, [jnp.max(tile, axis=0, keepdims=True) for tile in tiles])

    def weigh(tiles, top, turned_values):
        total, numerator = 0.0, 0.0
        for tile, value in zip(tiles, turned_values):
            weights = jnp.exp2((tile - top) * factor)
            total = total + jnp.sum(weights, axis=0, keepdims=True)
            numerator = numerator + jnp.dot(
                value, weights.astype(jnp.bfloat16), preferred_element_type=jnp.float32
            )
        return numerator / total, top * factor + jnp.log(total) * LOG2E

    def attend_some(head, query, slots, turned_values, masked):
        return weigh(*masked_scores(head, query, slots, masked), turned_values)

    def finish(head, value):
        rounded = value.astype(jnp.bfloat16).astype(jnp.float32)
        squares[mine] += jnp.sum((rounded * rounded).reshape(DH // 8, 8, rows), axis=0)
        att[:, head_lanes(head)] = rounded.T.astype(jnp.bfloat16)

    def head_rows(head):
        return pl.ds(pl.multiple_of(head * DH, DH), DH)

    def chunk_rows(chunk):
        return pl.ds(pl.multiple_of(chunk * wide, wide), wide)

    def partial_out(slot, chunk, index, head, result):
        value, log_total = result
        o_put[slot, head_rows(head), :] = value.astype(jnp.bfloat16)
        s_put[slot, chunk, index : index + 1, :] = log_total

    def send_out(slot, chunk, to_slot, target):
        at = chunk_rows(chunk)
        remote(o_put.at[slot, at], o_got.at[to_slot, at], O_NEAR + to_slot, chunk, target).start()
        remote(s_put.at[slot, chunk], s_got.at[to_slot, chunk], S_NEAR + to_slot, chunk, target).start()

    def own_query(head):
        return q_own[:, head_lanes(head)]

    @pl.when(place == 0)
    def _():
        @each_chunk
        def _(chunk):
            follow(up_copies, DEPTH, chunk)
            for index in range(CHUNK_HEADS):
                head = chunk * CHUNK_HEADS + index
                values = [turned(slot, head) for slot in (2, 3)]
                finish(head, attend_some(head, own_query(head), (2, 3), values, True)[0])

    @pl.when(place == 1)
    def _():
        s_put[...] = jnp.zeros_like(s_put)

        @each_chunk
        def _(chunk):
            at = lanes(chunk)
            arrived(k_all.at[core, :, at], K_UP, chunk)
            remote(k_all.at[core, :, at], k_all.at[core, :, at], K_SIDE, chunk, side).start()
            arrived(v_all.at[core, :, at], V_UP, chunk)
            remote(v_all.at[core, :, at], v_all.at[core, :, at], V_SIDE, chunk, side).start()
            arrived(q_far.at[0, :, at], Q_NEAR, chunk)
            arrived(q_far.at[1, :, at], Q_FAR, chunk)
            arrived(k_all.at[1 - core, :, at], K_SIDE, chunk)
            arrived(v_all.at[1 - core, :, at], V_SIDE, chunk)
            slots = (0, 1, 2, 3)
            heads = [chunk * CHUNK_HEADS + index for index in range(CHUNK_HEADS)]
            values = [[turned(slot, head) for slot in slots] for head in heads]
            works = [(far, index) for far in (1, 0, None) for index in range(CHUNK_HEADS)]

            def begin_work(far, index):
                head = heads[index]
                query = own_query(head) if far is None else q_far[far, :, head_lanes(head)]
                return masked_scores(head, query, slots, far is None)

            ready = begin_work(*works[0])
            for number, (far, index) in enumerate(works):
                current = ready
                if number + 1 < len(works):
                    ready = begin_work(*works[number + 1])
                result = weigh(*current, values[index])
                if far is None:
                    finish(heads[index], result[0])
                    continue
                partial_out(far, chunk, index, heads[index], result)
                if index == CHUNK_HEADS - 1:
                    send_out(far, chunk, far, ctx + 2 + 2 * far)

    @pl.when(place == 2)
    def _():
        s_put[...] = jnp.zeros_like(s_put)

        @each_chunk
        def _(chunk):
            follow(near_copies, 2 * DEPTH, chunk)
            arrived(q_far.at[0, :, lanes(chunk)], Q_NEAR, chunk)
            for index in range(CHUNK_HEADS):
                head = chunk * CHUNK_HEADS + index
                values = [turned(slot, head) for slot in (2, 3)]
                query = q_far[0, :, head_lanes(head)]
                partial_out(0, chunk, index, head, attend_some(head, query, (2, 3), values, False))
                value, log_total = attend_some(head, own_query(head), (2, 3), values, True)
                o_home[head_rows(head), :] = value
                s_home[chunk, index : index + 1, :] = log_total
            send_out(0, chunk, 0, ctx + 2)

    @pl.when(place == 3)
    def _():
        @each_chunk
        def _(chunk):
            follow(far_copies, DEPTH, chunk)
            for index in range(CHUNK_HEADS):
                head = chunk * CHUNK_HEADS + index
                values = [turned(slot, head) for slot in (2, 3)]
                value, log_total = attend_some(head, own_query(head), (2, 3), values, True)
                o_home[head_rows(head), :] = value
                s_home[chunk, index : index + 1, :] = log_total

    def merge(slots):
        @each_chunk
        def _(chunk):
            for slot in slots:
                arrived(o_got.at[slot, chunk_rows(chunk)], O_NEAR + slot, chunk)
                arrived(s_got.at[slot, chunk], S_NEAR + slot, chunk)
            for index in range(CHUNK_HEADS):
                head = chunk * CHUNK_HEADS + index
                logs = [s_home[chunk, index : index + 1, :]]
                parts = [o_home[head_rows(head), :]]
                for slot in slots:
                    logs.append(s_got[slot, chunk, index : index + 1, :])
                    parts.append(o_got[slot, head_rows(head), :].astype(jnp.float32))
                top = functools.reduce(jnp.maximum, logs)
                shares = [jnp.exp2(log - top) for log in logs]
                inverse = 1.0 / sum(shares)
                finish(head, sum(part * (share * inverse) for part, share in zip(parts, shares)))

    pl.when(place == 2)(lambda: merge((0,)))
    pl.when(place == 3)(lambda: merge((0, 1)))

    def square_copy(step, slot):
        return pltpu.make_async_remote_copy(
            src_ref=squares.at[slot], dst_ref=squares.at[slot],
            send_sem=send_sem.at[SQUARES, step], recv_sem=recv_sem.at[SQUARES, slot],
            device_id={"heads": lax.rem(mine + step, heads_size)}, device_id_type=MESH,
        )

    for step in range(1, heads_size):
        square_copy(step, mine).start()
    for step in range(1, heads_size):
        square_copy(step, lax.rem(mine + step, heads_size)).wait_recv()
    square_total = squares[0]
    for slot in range(1, heads_size):
        square_total = square_total + squares[slot]
    square_mean = jnp.sum(square_total, axis=0, keepdims=True) / (cols * heads_size)
    scale = jnp.broadcast_to(lax.rsqrt(square_mean + 1e-06), (DH, rows)).T

    def last(head, carry):
        at = head_lanes(head)
        out[:, at] = (att[:, at].astype(jnp.float32) * scale * gain[:, at] + hyena[:, at]).astype(jnp.bfloat16)
        return carry

    lax.fori_loop(0, cols // DH, last, 0)

    for step in range(1, heads_size):
        square_copy(step, mine).wait_send()

    @pl.when(ctx < ctx_size - 1)
    def _():
        sent(tail, SINGLES, 2)

    sent(k_any, SINGLES, 0)
    sent(v_any, SINGLES, 1)

    def sent_lanes(kinds):
        @each_chunk
        def _(chunk):
            for kind in kinds:
                sent(q_any.at[:, lanes(chunk)], kind, chunk)

    def sent_out(slots):
        @each_chunk
        def _(chunk):
            for slot in slots:
                sent(o_put.at[slot, chunk_rows(chunk)], O_NEAR + slot, chunk)
                sent(s_put.at[slot, chunk], S_NEAR + slot, chunk)

    pl.when(place == 2)(lambda: sent_out((0,)))

    @pl.when(place == 1)
    def _():
        sent_out((0, 1))
        sent_lanes((K_SIDE, V_SIDE))


def four_places(queries, keys, values, hyena_inputs, hyena_filter, norm_gain):
    rows, cols = queries.shape
    ctx_size, heads_size = lax.axis_size("ctx"), lax.axis_size("heads")
    chunks = cols // DH // CHUNK_HEADS
    bf16, f32 = jnp.bfloat16, jnp.float32
    count = max(chunks, heads_size, 3)
    return pl.pallas_call(
        functools.partial(fused_kernel, ctx_size, heads_size),
        out_shape=jax.ShapeDtypeStruct((rows, cols), bf16),
        in_specs=[pl.BlockSpec(memory_space=pltpu.HBM)] * 6,
        out_specs=pl.BlockSpec(memory_space=pltpu.VMEM),
        scratch_shapes=[
            pltpu.VMEM((4, rows, cols), bf16),
            pltpu.VMEM((4, rows, cols), bf16),
            pltpu.VMEM((rows, cols), bf16),
            pltpu.VMEM((2, rows, cols), bf16),
            pltpu.VMEM((2, cols, rows), bf16),
            pltpu.VMEM((2, chunks, 8, rows), f32),
            pltpu.VMEM((2, cols, rows), bf16),
            pltpu.VMEM((2, chunks, 8, rows), f32),
            pltpu.VMEM((cols, rows), f32),
            pltpu.VMEM((chunks, 8, rows), f32),
            pltpu.VMEM((rows, cols), bf16),
            pltpu.VMEM(hyena_inputs.shape, bf16),
            pltpu.VMEM((2, RIM, cols), bf16),
            pltpu.VMEM((RIM + rows, CHUNK_HEADS * DH), f32),
            pltpu.VMEM((rows, cols), f32),
            pltpu.VMEM((heads_size, 8, rows), f32),
            pltpu.VMEM(hyena_filter.shape, f32),
            pltpu.VMEM((1, cols), f32),
            pltpu.SemaphoreType.DMA((12, count)),
            pltpu.SemaphoreType.DMA((12, count)),
            pltpu.SemaphoreType.DMA((6,)),
        ],
        compiler_params=pltpu.CompilerParams(
            collective_id=0, has_side_effects=True, vmem_limit_bytes=63 * 1024 * 1024
        ),
    )(queries, keys, values, hyena_inputs, hyena_filter, norm_gain[None, :])


def on_device(queries, keys, values, hyena_inputs, hyena_filter, norm_gain):
    if lax.axis_size("ctx") == 2 * 4:
        return four_places(queries, keys, values, hyena_inputs, hyena_filter, norm_gain)
    row_count, col_count = queries.shape
    rim_rows = hyena_filter.shape[0] - 1
    tail_rows = hyena_inputs[1:, row_count - rim_rows :, :]
    earlier = from_behind(tail_rows, "ctx", 1)
    joined = jnp.concatenate([earlier, hyena_inputs[1:]], axis=1)
    product = joined[0].astype(jnp.float32) * joined[1].astype(jnp.float32)
    convolved = jnp.zeros((row_count, col_count), jnp.float32)
    for filter_tap in range(rim_rows + 1):
        convolved = (
            convolved
            + hyena_filter[filter_tap][None, :]
            * product[rim_rows - filter_tap : rim_rows - filter_tap + row_count]
        )
    hyena_out = hyena_inputs[0].astype(jnp.float32) * convolved
    attention = cycle_attention(queries, keys, values)
    attention_wide = lax.optimization_barrier(attention).astype(jnp.float32)
    local_squares = jnp.sum(attention_wide * attention_wide, axis=1)
    square_total = lax.psum(local_squares, "heads")
    square_mean = square_total / WIDTH
    normed = attention_wide * lax.rsqrt(square_mean + 1e-06)[:, None] * norm_gain[None, :]
    return (normed + hyena_out).astype(jnp.bfloat16)


def solution(mesh):
    placed = (
        P("ctx", "heads"),
        P("ctx", "heads"),
        P("ctx", "heads"),
        P(None, "ctx", "heads"),
        P(None, "heads"),
        P("heads"),
    )
    return jax.shard_map(
        on_device, mesh=mesh, in_specs=placed, out_specs=P("ctx", "heads"), check_vma=False
    )
```

```python
import functools
import math

import jax
import jax.numpy as jnp
from jax import lax
from jax.experimental import pallas as pl
from jax.experimental.pallas import tpu as pltpu
from jax.sharding import PartitionSpec as P

DH = 128
WIDTH = 8192
MESH = pl.DeviceIdType.MESH
LOG2E = 1.4426950408889634
CHUNK_HEADS = 1
DEPTH = 4
LAG = 6
RIM = 16
K_UP, V_UP, K_SIDE, V_SIDE, Q_NEAR, Q_FAR, O_NEAR, O_FAR, S_NEAR, S_FAR, SINGLES, SQUARES = range(12)


def from_behind(array, axis, by):
    size = lax.axis_size(axis)
    pairs = [(i, i + by) for i in range(size) if 0 <= i + by < size]
    return lax.ppermute(array, axis, pairs)


def attend(half_state, query_block, query_place, key_block, value_block, key_place):
    numerator, maxima, totals = half_state
    score_scale = 1.0 / math.sqrt(query_block.shape[2])
    scores = (
        jnp.einsum("qhd,khd->qhk", query_block, key_block, preferred_element_type=jnp.float32)
        * score_scale
    )
    visible = key_place[None, None, :] <= query_place[:, None, None]
    scores = jnp.where(visible, scores, -1e30)
    row_top = jnp.maximum(maxima, jnp.max(scores, axis=2))
    rescale = jnp.exp(maxima - row_top)
    weights = jnp.where(visible, jnp.exp(scores - row_top[:, :, None]), 0.0)
    totals = totals * rescale + jnp.sum(weights, axis=2)
    summed = jnp.einsum(
        "qhk,khd->qhd",
        weights.astype(jnp.bfloat16),
        value_block,
        preferred_element_type=jnp.float32,
    )
    numerator = numerator * rescale[:, :, None] + summed
    return (numerator, row_top, totals)


def fresh_state(row_total, head_total, head_size):
    return (
        jnp.zeros((row_total, head_total, head_size), jnp.float32),
        jnp.full((row_total, head_total), -1e30, jnp.float32),
        jnp.zeros((row_total, head_total), jnp.float32),
    )


def cycle_attention(queries, keys, values):
    row_count, col_count = queries.shape
    head_count = col_count // DH
    half_rows = row_count // 2
    ctx_index = lax.axis_index("ctx")
    query_starts = (ctx_index * row_count, ctx_index * row_count + half_rows)
    query_heads = queries.reshape(row_count, head_count, DH)
    query_halves = (query_heads[:half_rows], query_heads[half_rows:])
    query_places = tuple(
        (query_starts[number] + jnp.arange(half_rows, dtype=jnp.int32) for number in range(2))
    )
    empty_state = fresh_state(half_rows, head_count, DH)
    key_rows = lax.all_gather(keys, "ctx", axis=0, tiled=True)
    value_rows = lax.all_gather(values, "ctx", axis=0, tiled=True)
    count = key_rows.shape[0]
    block_rows = math.gcd(count, half_rows)
    key_heads = key_rows.reshape(count, head_count, DH)
    value_heads = value_rows.reshape(count, head_count, DH)

    def inner(block_index, state):
        first = block_index * block_rows
        key_block = lax.dynamic_slice_in_dim(key_heads, first, block_rows, 0)
        value_block = lax.dynamic_slice_in_dim(value_heads, first, block_rows, 0)
        key_place = first + jnp.arange(block_rows, dtype=jnp.int32)
        updated = []
        for number in range(2):
            query_block = query_halves[number]
            query_place = query_places[number]

            def update(half_state):
                return attend(
                    half_state, query_block, query_place, key_block, value_block, key_place
                )

            needed = key_place[0] <= query_place[half_rows - 1]
            updated.append(lax.cond(needed, update, lambda half_state: half_state, state[number]))
        return tuple(updated)

    finished = lax.fori_loop(0, count // block_rows, inner, (empty_state, empty_state))
    halves_out = [finished[number][0] / finished[number][2][:, :, None] for number in range(2)]
    return jnp.concatenate(halves_out, axis=0).reshape(row_count, col_count).astype(jnp.bfloat16)


def fused_kernel(
    ctx_size, heads_size,
    q_any, k_any, v_any, hy_any, filt_any, gain_any, out,
    k_all, v_all, q_own, q_far, o_got, s_got, o_put, s_put, o_home, s_home,
    att, hy, halo, prod, hyena, squares, filt, gain,
    send_sem, recv_sem, local_sem,
):
    rows, cols = out.shape
    chunks = cols // DH // CHUNK_HEADS
    wide = CHUNK_HEADS * DH
    ctx = lax.axis_index("ctx")
    mine = lax.axis_index("heads")
    core = lax.rem(ctx, 2)
    place = ctx // 2
    side = ctx + 1 - 2 * core
    factor = LOG2E / math.sqrt(DH)

    local = [
        pltpu.make_async_copy(hy_any, hy, local_sem.at[0]),
        pltpu.make_async_copy(filt_any, filt, local_sem.at[1]),
        pltpu.make_async_copy(k_any, k_all.at[2 + core], local_sem.at[2]),
        pltpu.make_async_copy(v_any, v_all.at[2 + core], local_sem.at[3]),
        pltpu.make_async_copy(q_any, q_own, local_sem.at[4]),
        pltpu.make_async_copy(gain_any, gain, local_sem.at[5]),
    ]
    for copy in local[2:5] + local[:2] + local[5:]:
        copy.start()
    barrier = pltpu.get_barrier_semaphore()
    for step in range(1, ctx_size):
        pl.semaphore_signal(
            barrier, inc=1, device_id={"ctx": lax.rem(ctx + step, ctx_size)}, device_id_type=MESH
        )
    for step in range(1, heads_size):
        pl.semaphore_signal(
            barrier, inc=1, device_id={"heads": lax.rem(mine + step, heads_size)}, device_id_type=MESH
        )
    pl.semaphore_wait(barrier, ctx_size + heads_size - 2)
    for copy in local[2:5]:
        copy.wait()

    def remote(src, dst, kind, at, target):
        return pltpu.make_async_remote_copy(
            src_ref=src, dst_ref=dst, send_sem=send_sem.at[kind, at], recv_sem=recv_sem.at[kind, at],
            device_id={"ctx": target}, device_id_type=MESH,
        )

    def arrived(dst, kind, at):
        remote(dst, dst, kind, at, side).wait_recv()

    def sent(src, kind, at):
        remote(src, src, kind, at, side).wait_send()

    def lanes(chunk):
        return pl.ds(pl.multiple_of(chunk * wide, wide), wide)

    def head_lanes(head):
        return pl.ds(pl.multiple_of(head * DH, DH), DH)

    def each_chunk(body):
        def step(chunk, carry):
            body(chunk)
            return carry

        lax.fori_loop(0, chunks, step, 0)

    tail = hy_any.at[pl.ds(1, 2), pl.ds(rows - RIM, RIM), :]

    def send_tail():
        remote(tail, halo, SINGLES, 2, ctx + 1).start()

    pl.when((ctx < ctx_size - 1) & (ctx != 1))(send_tail)
    remote(k_any, k_all.at[2 + core], SINGLES, 0, side).start()
    remote(v_any, v_all.at[2 + core], SINGLES, 1, side).start()

    def up_copies(chunk):
        at = lanes(chunk)
        return (
            remote(k_all.at[2 + core, :, at], k_all.at[core, :, at], K_UP, chunk, ctx + 2),
            remote(v_all.at[2 + core, :, at], v_all.at[core, :, at], V_UP, chunk, ctx + 2),
        )

    def near_copies(chunk):
        at = lanes(chunk)
        return (remote(q_own.at[:, at], q_far.at[0, :, at], Q_NEAR, chunk, ctx - 2),)

    def far_copies(chunk):
        at = lanes(chunk)
        return (remote(q_own.at[:, at], q_far.at[1, :, at], Q_FAR, chunk, ctx - 4),) + near_copies(chunk)

    def begin(copies, depth):
        for chunk in range(depth):
            for copy in copies(chunk):
                copy.start()

    def follow(copies, depth, chunk):
        for copy in copies(chunk):
            copy.wait_send()

        @pl.when(chunk + depth < chunks)
        def _():
            for copy in copies(chunk + depth):
                copy.start()

    pl.when(place == 0)(lambda: begin(up_copies, DEPTH))
    pl.when(place == 2)(lambda: begin(near_copies, 2 * DEPTH))
    pl.when(place == 3)(lambda: begin(far_copies, 2 * DEPTH))

    def gate():
        @pl.when(ctx == 0)
        def _():
            halo[...] = jnp.zeros_like(halo)

        @pl.when(ctx > 0)
        def _():
            arrived(halo, SINGLES, 2)

        for copy in local[:2]:
            copy.wait()

        @each_chunk
        def _(chunk):
            at = lanes(chunk)
            prod[:RIM] = halo[0, :, at].astype(jnp.float32) * halo[1, :, at].astype(jnp.float32)
            prod[RIM:] = hy[1, :, at].astype(jnp.float32) * hy[2, :, at].astype(jnp.float32)
            taps = filt[:, at]
            summed = taps[0:1] * prod[RIM : RIM + rows]
            for tap in range(1, filt.shape[0]):
                summed = summed + taps[tap : tap + 1] * prod[RIM - tap : RIM - tap + rows]
            hyena[:, at] = hy[0, :, at].astype(jnp.float32) * summed

    pl.when(place != 1)(gate)

    local[5].wait()
    arrived(k_all.at[2], SINGLES, 0)
    arrived(v_all.at[2], SINGLES, 1)
    squares[mine] = jnp.zeros_like(squares[mine])

    key_place = lax.broadcasted_iota(jnp.int32, (rows, rows), 0)
    query_place = lax.broadcasted_iota(jnp.int32, (rows, rows), 1) + core * rows

    def scores(slot, head, query):
        return lax.dot_general(
            k_all[slot, :, head_lanes(head)], query, (((1,), (1,)), ((), ())),
            preferred_element_type=jnp.float32,
        )

    def turned(slot, head):
        return v_all[slot, :, head_lanes(head)].T

    def masked_scores(head, query, slots, masked):
        tiles = [scores(slot, head, query) for slot in slots]
        if masked:
            tiles = [
                jnp.where(key_place + (slot - 2) * rows <= query_place, tile, -1e30) if slot >= 2 else tile
                for slot, tile in zip(slots, tiles)
            ]
        return tiles, functools.reduce(jnp.maximum, [jnp.max(tile, axis=0, keepdims=True) for tile in tiles])

    def weigh(tiles, top, turned_values):
        total, numerator = 0.0, 0.0
        for tile, value in zip(tiles, turned_values):
            weights = jnp.exp2((tile - top) * factor)
            total = total + jnp.sum(weights, axis=0, keepdims=True)
            numerator = numerator + jnp.dot(
                value, weights.astype(jnp.bfloat16), preferred_element_type=jnp.float32
            )
        return numerator / total, top * factor + jnp.log(total) * LOG2E

    def attend_some(head, query, slots, turned_values, masked):
        return weigh(*masked_scores(head, query, slots, masked), turned_values)

    def finish(head, value):
        rounded = value.astype(jnp.bfloat16).astype(jnp.float32)
        squares[mine] += jnp.sum((rounded * rounded).reshape(DH // 8, 8, rows), axis=0)
        att[:, head_lanes(head)] = rounded.T.astype(jnp.bfloat16)

    def head_rows(head):
        return pl.ds(pl.multiple_of(head * DH, DH), DH)

    def chunk_rows(chunk):
        return pl.ds(pl.multiple_of(chunk * wide, wide), wide)

    def partial_out(slot, chunk, index, head, result):
        value, log_total = result
        o_put[slot, head_rows(head), :] = value.astype(jnp.bfloat16)
        s_put[slot, chunk, index : index + 1, :] = log_total

    def send_out(slot, chunk, to_slot, target):
        at = chunk_rows(chunk)
        remote(o_put.at[slot, at], o_got.at[to_slot, at], O_NEAR + to_slot, chunk, target).start()
        remote(s_put.at[slot, chunk], s_got.at[to_slot, chunk], S_NEAR + to_slot, chunk, target).start()

    def merge(slots, chunk):
        for slot in slots:
            arrived(o_got.at[slot, chunk_rows(chunk)], O_NEAR + slot, chunk)
            arrived(s_got.at[slot, chunk], S_NEAR + slot, chunk)
        for index in range(CHUNK_HEADS):
            head = chunk * CHUNK_HEADS + index
            logs = [s_home[chunk, index : index + 1, :]]
            parts = [o_home[head_rows(head), :]]
            for slot in slots:
                logs.append(s_got[slot, chunk, index : index + 1, :])
                parts.append(o_got[slot, head_rows(head), :].astype(jnp.float32))
            top = functools.reduce(jnp.maximum, logs)
            shares = [jnp.exp2(log - top) for log in logs]
            inverse = 1.0 / sum(shares)
            finish(head, sum(part * (share * inverse) for part, share in zip(parts, shares)))

    def merge_behind(slots, chunk):
        pl.when(chunk >= LAG)(lambda: merge(slots, chunk - LAG))

    def merge_rest(slots):
        def step(chunk, carry):
            merge(slots, chunk)
            return carry

        lax.fori_loop(max(chunks - LAG, 0), chunks, step, 0)

    def own_query(head):
        return q_own[:, head_lanes(head)]

    @pl.when(place == 0)
    def _():
        @each_chunk
        def _(chunk):
            follow(up_copies, DEPTH, chunk)
            for index in range(CHUNK_HEADS):
                head = chunk * CHUNK_HEADS + index
                values = [turned(slot, head) for slot in (2, 3)]
                finish(head, attend_some(head, own_query(head), (2, 3), values, True)[0])

        pl.when(core == 1)(send_tail)

    @pl.when(place == 1)
    def _():
        @each_chunk
        def _(chunk):
            at = lanes(chunk)
            arrived(k_all.at[core, :, at], K_UP, chunk)
            remote(k_all.at[core, :, at], k_all.at[core, :, at], K_SIDE, chunk, side).start()
            arrived(v_all.at[core, :, at], V_UP, chunk)
            remote(v_all.at[core, :, at], v_all.at[core, :, at], V_SIDE, chunk, side).start()
            arrived(q_far.at[0, :, at], Q_NEAR, chunk)
            arrived(q_far.at[1, :, at], Q_FAR, chunk)
            arrived(k_all.at[1 - core, :, at], K_SIDE, chunk)
            arrived(v_all.at[1 - core, :, at], V_SIDE, chunk)
            slots = (0, 1, 2, 3)
            heads = [chunk * CHUNK_HEADS + index for index in range(CHUNK_HEADS)]
            values = [[turned(slot, head) for slot in slots] for head in heads]
            works = [(far, index) for far in (1, 0, None) for index in range(CHUNK_HEADS)]

            def begin_work(far, index):
                head = heads[index]
                query = own_query(head) if far is None else q_far[far, :, head_lanes(head)]
                return masked_scores(head, query, slots, far is None)

            ready = begin_work(*works[0])
            for number, (far, index) in enumerate(works):
                current = ready
                if number + 1 < len(works):
                    ready = begin_work(*works[number + 1])
                result = weigh(*current, values[index])
                if far is None:
                    finish(heads[index], result[0])
                    continue
                partial_out(far, chunk, index, heads[index], result)
                if index == CHUNK_HEADS - 1:
                    send_out(far, chunk, far, ctx + 2 + 2 * far)

        gate()

    @pl.when(place == 2)
    def _():
        @each_chunk
        def _(chunk):
            follow(near_copies, 2 * DEPTH, chunk)
            arrived(q_far.at[0, :, lanes(chunk)], Q_NEAR, chunk)
            for index in range(CHUNK_HEADS):
                head = chunk * CHUNK_HEADS + index
                values = [turned(slot, head) for slot in (2, 3)]
                query = q_far[0, :, head_lanes(head)]
                partial_out(0, chunk, index, head, attend_some(head, query, (2, 3), values, False))
                value, log_total = attend_some(head, own_query(head), (2, 3), values, True)
                o_home[head_rows(head), :] = value
                s_home[chunk, index : index + 1, :] = log_total
            send_out(0, chunk, 0, ctx + 2)
            merge_behind((0,), chunk)

        merge_rest((0,))

    @pl.when(place == 3)
    def _():
        @each_chunk
        def _(chunk):
            follow(far_copies, 2 * DEPTH, chunk)
            for index in range(CHUNK_HEADS):
                head = chunk * CHUNK_HEADS + index
                values = [turned(slot, head) for slot in (2, 3)]
                value, log_total = attend_some(head, own_query(head), (2, 3), values, True)
                o_home[head_rows(head), :] = value
                s_home[chunk, index : index + 1, :] = log_total
            merge_behind((0, 1), chunk)

        merge_rest((0, 1))

    def square_copy(step, slot):
        return pltpu.make_async_remote_copy(
            src_ref=squares.at[slot], dst_ref=squares.at[slot],
            send_sem=send_sem.at[SQUARES, step], recv_sem=recv_sem.at[SQUARES, slot],
            device_id={"heads": lax.rem(mine + step, heads_size)}, device_id_type=MESH,
        )

    for step in range(1, heads_size):
        square_copy(step, mine).start()
    for step in range(1, heads_size):
        square_copy(step, lax.rem(mine + step, heads_size)).wait_recv()
    square_total = squares[0]
    for slot in range(1, heads_size):
        square_total = square_total + squares[slot]
    square_mean = jnp.sum(square_total, axis=0, keepdims=True) / (cols * heads_size)
    scale = jnp.broadcast_to(lax.rsqrt(square_mean + 1e-06), (DH, rows)).T

    def last(head, carry):
        at = head_lanes(head)
        out[:, at] = (att[:, at].astype(jnp.float32) * scale * gain[:, at] + hyena[:, at]).astype(jnp.bfloat16)
        return carry

    lax.fori_loop(0, cols // DH, last, 0)

    for step in range(1, heads_size):
        square_copy(step, mine).wait_send()

    @pl.when(ctx < ctx_size - 1)
    def _():
        sent(tail, SINGLES, 2)

    sent(k_any, SINGLES, 0)
    sent(v_any, SINGLES, 1)

    def sent_lanes(kinds):
        @each_chunk
        def _(chunk):
            for kind in kinds:
                sent(q_any.at[:, lanes(chunk)], kind, chunk)

    def sent_out(slots):
        @each_chunk
        def _(chunk):
            for slot in slots:
                sent(o_put.at[slot, chunk_rows(chunk)], O_NEAR + slot, chunk)
                sent(s_put.at[slot, chunk], S_NEAR + slot, chunk)

    pl.when(place == 2)(lambda: sent_out((0,)))

    @pl.when(place == 1)
    def _():
        sent_out((0, 1))
        sent_lanes((K_SIDE, V_SIDE))


def four_places(queries, keys, values, hyena_inputs, hyena_filter, norm_gain):
    rows, cols = queries.shape
    ctx_size, heads_size = lax.axis_size("ctx"), lax.axis_size("heads")
    chunks = cols // DH // CHUNK_HEADS
    bf16, f32 = jnp.bfloat16, jnp.float32
    count = max(chunks, heads_size, 3)
    return pl.pallas_call(
        functools.partial(fused_kernel, ctx_size, heads_size),
        out_shape=jax.ShapeDtypeStruct((rows, cols), bf16),
        in_specs=[pl.BlockSpec(memory_space=pltpu.HBM)] * 6,
        out_specs=pl.BlockSpec(memory_space=pltpu.VMEM),
        scratch_shapes=[
            pltpu.VMEM((4, rows, cols), bf16),
            pltpu.VMEM((4, rows, cols), bf16),
            pltpu.VMEM((rows, cols), bf16),
            pltpu.VMEM((2, rows, cols), bf16),
            pltpu.VMEM((2, cols, rows), bf16),
            pltpu.VMEM((2, chunks, CHUNK_HEADS, rows), f32),
            pltpu.VMEM((2, cols, rows), bf16),
            pltpu.VMEM((2, chunks, CHUNK_HEADS, rows), f32),
            pltpu.VMEM((cols, rows), f32),
            pltpu.VMEM((chunks, CHUNK_HEADS, rows), f32),
            pltpu.VMEM((rows, cols), bf16),
            pltpu.VMEM(hyena_inputs.shape, bf16),
            pltpu.VMEM((2, RIM, cols), bf16),
            pltpu.VMEM((RIM + rows, CHUNK_HEADS * DH), f32),
            pltpu.VMEM((rows, cols), f32),
            pltpu.VMEM((heads_size, 8, rows), f32),
            pltpu.VMEM(hyena_filter.shape, f32),
            pltpu.VMEM((1, cols), f32),
            pltpu.SemaphoreType.DMA((12, count)),
            pltpu.SemaphoreType.DMA((12, count)),
            pltpu.SemaphoreType.DMA((6,)),
        ],
        compiler_params=pltpu.CompilerParams(
            collective_id=0, has_side_effects=True, vmem_limit_bytes=63 * 1024 * 1024
        ),
    )(queries, keys, values, hyena_inputs, hyena_filter, norm_gain[None, :])


def on_device(queries, keys, values, hyena_inputs, hyena_filter, norm_gain):
    if lax.axis_size("ctx") == 2 * 4:
        return four_places(queries, keys, values, hyena_inputs, hyena_filter, norm_gain)
    row_count, col_count = queries.shape
    rim_rows = hyena_filter.shape[0] - 1
    tail_rows = hyena_inputs[1:, row_count - rim_rows :, :]
    earlier = from_behind(tail_rows, "ctx", 1)
    joined = jnp.concatenate([earlier, hyena_inputs[1:]], axis=1)
    product = joined[0].astype(jnp.float32) * joined[1].astype(jnp.float32)
    convolved = jnp.zeros((row_count, col_count), jnp.float32)
    for filter_tap in range(rim_rows + 1):
        convolved = (
            convolved
            + hyena_filter[filter_tap][None, :]
            * product[rim_rows - filter_tap : rim_rows - filter_tap + row_count]
        )
    hyena_out = hyena_inputs[0].astype(jnp.float32) * convolved
    attention = cycle_attention(queries, keys, values)
    attention_wide = lax.optimization_barrier(attention).astype(jnp.float32)
    local_squares = jnp.sum(attention_wide * attention_wide, axis=1)
    square_total = lax.psum(local_squares, "heads")
    square_mean = square_total / WIDTH
    normed = attention_wide * lax.rsqrt(square_mean + 1e-06)[:, None] * norm_gain[None, :]
    return (normed + hyena_out).astype(jnp.bfloat16)


def solution(mesh):
    placed = (
        P("ctx", "heads"),
        P("ctx", "heads"),
        P("ctx", "heads"),
        P(None, "ctx", "heads"),
        P(None, "heads"),
        P("heads"),
    )
    return jax.shard_map(
        on_device, mesh=mesh, in_specs=placed, out_specs=P("ctx", "heads"), check_vma=False
    )
```

```python
import functools
import math

import jax
import jax.numpy as jnp
from jax import lax
from jax.experimental import pallas as pl
from jax.experimental.pallas import tpu as pltpu
from jax.sharding import PartitionSpec as P

DH = 128
WIDTH = 8192
MESH = pl.DeviceIdType.MESH
LOG2E = 1.4426950408889634
CHUNK_HEADS = 1
DEPTH = 16
LAG = 6
RIM = 16
K_UP, V_UP, K_SIDE, V_SIDE, Q_NEAR, Q_FAR, O_NEAR, O_FAR, S_NEAR, S_FAR, SINGLES, SQUARES = range(12)


def from_behind(array, axis, by):
    size = lax.axis_size(axis)
    pairs = [(i, i + by) for i in range(size) if 0 <= i + by < size]
    return lax.ppermute(array, axis, pairs)


def attend(half_state, query_block, query_place, key_block, value_block, key_place):
    numerator, maxima, totals = half_state
    score_scale = 1.0 / math.sqrt(query_block.shape[2])
    scores = (
        jnp.einsum("qhd,khd->qhk", query_block, key_block, preferred_element_type=jnp.float32)
        * score_scale
    )
    visible = key_place[None, None, :] <= query_place[:, None, None]
    scores = jnp.where(visible, scores, -1e30)
    row_top = jnp.maximum(maxima, jnp.max(scores, axis=2))
    rescale = jnp.exp(maxima - row_top)
    weights = jnp.where(visible, jnp.exp(scores - row_top[:, :, None]), 0.0)
    totals = totals * rescale + jnp.sum(weights, axis=2)
    summed = jnp.einsum(
        "qhk,khd->qhd",
        weights.astype(jnp.bfloat16),
        value_block,
        preferred_element_type=jnp.float32,
    )
    numerator = numerator * rescale[:, :, None] + summed
    return (numerator, row_top, totals)


def fresh_state(row_total, head_total, head_size):
    return (
        jnp.zeros((row_total, head_total, head_size), jnp.float32),
        jnp.full((row_total, head_total), -1e30, jnp.float32),
        jnp.zeros((row_total, head_total), jnp.float32),
    )


def cycle_attention(queries, keys, values):
    row_count, col_count = queries.shape
    head_count = col_count // DH
    half_rows = row_count // 2
    ctx_index = lax.axis_index("ctx")
    query_starts = (ctx_index * row_count, ctx_index * row_count + half_rows)
    query_heads = queries.reshape(row_count, head_count, DH)
    query_halves = (query_heads[:half_rows], query_heads[half_rows:])
    query_places = tuple(
        (query_starts[number] + jnp.arange(half_rows, dtype=jnp.int32) for number in range(2))
    )
    empty_state = fresh_state(half_rows, head_count, DH)
    key_rows = lax.all_gather(keys, "ctx", axis=0, tiled=True)
    value_rows = lax.all_gather(values, "ctx", axis=0, tiled=True)
    count = key_rows.shape[0]
    block_rows = math.gcd(count, half_rows)
    key_heads = key_rows.reshape(count, head_count, DH)
    value_heads = value_rows.reshape(count, head_count, DH)

    def inner(block_index, state):
        first = block_index * block_rows
        key_block = lax.dynamic_slice_in_dim(key_heads, first, block_rows, 0)
        value_block = lax.dynamic_slice_in_dim(value_heads, first, block_rows, 0)
        key_place = first + jnp.arange(block_rows, dtype=jnp.int32)
        updated = []
        for number in range(2):
            query_block = query_halves[number]
            query_place = query_places[number]

            def update(half_state):
                return attend(
                    half_state, query_block, query_place, key_block, value_block, key_place
                )

            needed = key_place[0] <= query_place[half_rows - 1]
            updated.append(lax.cond(needed, update, lambda half_state: half_state, state[number]))
        return tuple(updated)

    finished = lax.fori_loop(0, count // block_rows, inner, (empty_state, empty_state))
    halves_out = [finished[number][0] / finished[number][2][:, :, None] for number in range(2)]
    return jnp.concatenate(halves_out, axis=0).reshape(row_count, col_count).astype(jnp.bfloat16)


def fused_kernel(
    ctx_size, heads_size,
    q_any, k_any, v_any, hy_any, filt_any, gain_any, out,
    k_all, v_all, q_own, q_far, o_got, s_got, o_put, s_put, o_home, s_home,
    att, hy, halo, prod, hyena, squares, filt, gain,
    send_sem, recv_sem, local_sem,
):
    rows, cols = out.shape
    chunks = cols // DH // CHUNK_HEADS
    wide = CHUNK_HEADS * DH
    ctx = lax.axis_index("ctx")
    mine = lax.axis_index("heads")
    core = lax.rem(ctx, 2)
    place = ctx // 2
    side = ctx + 1 - 2 * core
    factor = LOG2E / math.sqrt(DH)

    local = [
        pltpu.make_async_copy(hy_any, hy, local_sem.at[0]),
        pltpu.make_async_copy(filt_any, filt, local_sem.at[1]),
        pltpu.make_async_copy(k_any, k_all.at[2 + core], local_sem.at[2]),
        pltpu.make_async_copy(v_any, v_all.at[2 + core], local_sem.at[3]),
        pltpu.make_async_copy(q_any, q_own, local_sem.at[4]),
        pltpu.make_async_copy(gain_any, gain, local_sem.at[5]),
    ]
    for copy in local[2:5] + local[:2] + local[5:]:
        copy.start()
    barrier = pltpu.get_barrier_semaphore()
    for step in range(1, ctx_size):
        pl.semaphore_signal(
            barrier, inc=1, device_id={"ctx": lax.rem(ctx + step, ctx_size)}, device_id_type=MESH
        )
    for step in range(1, heads_size):
        pl.semaphore_signal(
            barrier, inc=1, device_id={"heads": lax.rem(mine + step, heads_size)}, device_id_type=MESH
        )
    pl.semaphore_wait(barrier, ctx_size + heads_size - 2)
    for copy in local[2:5]:
        copy.wait()

    def remote(src, dst, kind, at, target):
        return pltpu.make_async_remote_copy(
            src_ref=src, dst_ref=dst, send_sem=send_sem.at[kind, at], recv_sem=recv_sem.at[kind, at],
            device_id={"ctx": target}, device_id_type=MESH,
        )

    def arrived(dst, kind, at):
        remote(dst, dst, kind, at, side).wait_recv()

    def sent(src, kind, at):
        remote(src, src, kind, at, side).wait_send()

    def lanes(chunk):
        return pl.ds(pl.multiple_of(chunk * wide, wide), wide)

    def head_lanes(head):
        return pl.ds(pl.multiple_of(head * DH, DH), DH)

    def each_chunk(body):
        def step(chunk, carry):
            body(chunk)
            return carry

        lax.fori_loop(0, chunks, step, 0)

    tail = hy_any.at[pl.ds(1, 2), pl.ds(rows - RIM, RIM), :]

    def send_tail():
        remote(tail, halo, SINGLES, 2, ctx + 1).start()

    pl.when((ctx < ctx_size - 1) & (ctx != 1))(send_tail)
    remote(k_any, k_all.at[2 + core], SINGLES, 0, side).start()
    remote(v_any, v_all.at[2 + core], SINGLES, 1, side).start()

    def up_copies(chunk):
        at = lanes(chunk)
        return (
            remote(k_all.at[2 + core, :, at], k_all.at[core, :, at], K_UP, chunk, ctx + 2),
            remote(v_all.at[2 + core, :, at], v_all.at[core, :, at], V_UP, chunk, ctx + 2),
        )

    def near_copies(chunk):
        at = lanes(chunk)
        return (remote(q_own.at[:, at], q_far.at[0, :, at], Q_NEAR, chunk, ctx - 2),)

    def far_copies(chunk):
        at = lanes(chunk)
        return (remote(q_own.at[:, at], q_far.at[1, :, at], Q_FAR, chunk, ctx - 4),) + near_copies(chunk)

    def begin(copies, depth):
        def step(chunk, carry):
            for copy in copies(chunk):
                copy.start()
            return carry

        lax.fori_loop(0, min(depth, chunks), step, 0)

    def follow(copies, depth, chunk):
        for copy in copies(chunk):
            copy.wait_send()

        @pl.when(chunk + depth < chunks)
        def _():
            for copy in copies(chunk + depth):
                copy.start()

    pl.when(place == 0)(lambda: begin(up_copies, DEPTH))
    pl.when(place == 2)(lambda: begin(near_copies, DEPTH))
    pl.when(place == 3)(lambda: begin(far_copies, DEPTH))

    def gate():
        @pl.when(ctx == 0)
        def _():
            halo[...] = jnp.zeros_like(halo)

        @pl.when(ctx > 0)
        def _():
            arrived(halo, SINGLES, 2)

        for copy in local[:2]:
            copy.wait()

        @each_chunk
        def _(chunk):
            at = lanes(chunk)
            prod[:RIM] = halo[0, :, at].astype(jnp.float32) * halo[1, :, at].astype(jnp.float32)
            prod[RIM:] = hy[1, :, at].astype(jnp.float32) * hy[2, :, at].astype(jnp.float32)
            taps = filt[:, at]
            summed = taps[0:1] * prod[RIM : RIM + rows]
            for tap in range(1, filt.shape[0]):
                summed = summed + taps[tap : tap + 1] * prod[RIM - tap : RIM - tap + rows]
            hyena[:, at] = hy[0, :, at].astype(jnp.float32) * summed

    pl.when(place != 1)(gate)

    local[5].wait()
    arrived(k_all.at[2], SINGLES, 0)
    arrived(v_all.at[2], SINGLES, 1)
    squares[mine] = jnp.zeros_like(squares[mine])

    key_place = lax.broadcasted_iota(jnp.int32, (rows, rows), 0)
    query_place = lax.broadcasted_iota(jnp.int32, (rows, rows), 1) + core * rows

    def scores(slot, head, query):
        return lax.dot_general(
            k_all[slot, :, head_lanes(head)], query, (((1,), (1,)), ((), ())),
            preferred_element_type=jnp.float32,
        )

    def turned(slot, head):
        return v_all[slot, :, head_lanes(head)].T

    def masked_scores(head, query, slots, masked):
        tiles = [scores(slot, head, query) for slot in slots]
        if masked:
            tiles = [
                jnp.where(key_place + (slot - 2) * rows <= query_place, tile, -1e30) if slot >= 2 else tile
                for slot, tile in zip(slots, tiles)
            ]
        return tiles, functools.reduce(jnp.maximum, [jnp.max(tile, axis=0, keepdims=True) for tile in tiles])

    def weigh(tiles, top, turned_values):
        total, numerator = 0.0, 0.0
        for tile, value in zip(tiles, turned_values):
            weights = jnp.exp2((tile - top) * factor)
            total = total + jnp.sum(weights, axis=0, keepdims=True)
            numerator = numerator + jnp.dot(
                value, weights.astype(jnp.bfloat16), preferred_element_type=jnp.float32
            )
        return numerator / total, top * factor + jnp.log(total) * LOG2E

    def attend_some(head, query, slots, turned_values, masked):
        return weigh(*masked_scores(head, query, slots, masked), turned_values)

    def finish(head, value):
        rounded = value.astype(jnp.bfloat16).astype(jnp.float32)
        squares[mine] += jnp.sum((rounded * rounded).reshape(DH // 8, 8, rows), axis=0)
        att[:, head_lanes(head)] = rounded.T.astype(jnp.bfloat16)

    def head_rows(head):
        return pl.ds(pl.multiple_of(head * DH, DH), DH)

    def chunk_rows(chunk):
        return pl.ds(pl.multiple_of(chunk * wide, wide), wide)

    def partial_out(slot, chunk, index, head, result):
        value, log_total = result
        o_put[slot, head_rows(head), :] = value.astype(jnp.bfloat16)
        s_put[slot, chunk, index : index + 1, :] = log_total

    def send_out(slot, chunk, to_slot, target):
        at = chunk_rows(chunk)
        remote(o_put.at[slot, at], o_got.at[to_slot, at], O_NEAR + to_slot, chunk, target).start()
        remote(s_put.at[slot, chunk], s_got.at[to_slot, chunk], S_NEAR + to_slot, chunk, target).start()

    def merge(slots, chunk):
        for slot in slots:
            arrived(o_got.at[slot, chunk_rows(chunk)], O_NEAR + slot, chunk)
            arrived(s_got.at[slot, chunk], S_NEAR + slot, chunk)
        for index in range(CHUNK_HEADS):
            head = chunk * CHUNK_HEADS + index
            logs = [s_home[chunk, index : index + 1, :]]
            parts = [o_home[head_rows(head), :]]
            for slot in slots:
                logs.append(s_got[slot, chunk, index : index + 1, :])
                parts.append(o_got[slot, head_rows(head), :].astype(jnp.float32))
            top = functools.reduce(jnp.maximum, logs)
            shares = [jnp.exp2(log - top) for log in logs]
            inverse = 1.0 / sum(shares)
            finish(head, sum(part * (share * inverse) for part, share in zip(parts, shares)))

    def merge_behind(slots, chunk):
        pl.when(chunk >= LAG)(lambda: merge(slots, chunk - LAG))

    def merge_rest(slots):
        def step(chunk, carry):
            merge(slots, chunk)
            return carry

        lax.fori_loop(max(chunks - LAG, 0), chunks, step, 0)

    def own_query(head):
        return q_own[:, head_lanes(head)]

    @pl.when(place == 0)
    def _():
        @each_chunk
        def _(chunk):
            follow(up_copies, DEPTH, chunk)
            for index in range(CHUNK_HEADS):
                head = chunk * CHUNK_HEADS + index
                values = [turned(slot, head) for slot in (2, 3)]
                finish(head, attend_some(head, own_query(head), (2, 3), values, True)[0])

        pl.when(core == 1)(send_tail)

    @pl.when(place == 1)
    def _():
        @each_chunk
        def _(chunk):
            at = lanes(chunk)
            arrived(k_all.at[core, :, at], K_UP, chunk)
            remote(k_all.at[core, :, at], k_all.at[core, :, at], K_SIDE, chunk, side).start()
            arrived(v_all.at[core, :, at], V_UP, chunk)
            remote(v_all.at[core, :, at], v_all.at[core, :, at], V_SIDE, chunk, side).start()
            arrived(q_far.at[0, :, at], Q_NEAR, chunk)
            arrived(q_far.at[1, :, at], Q_FAR, chunk)
            arrived(k_all.at[1 - core, :, at], K_SIDE, chunk)
            arrived(v_all.at[1 - core, :, at], V_SIDE, chunk)
            slots = (0, 1, 2, 3)
            heads = [chunk * CHUNK_HEADS + index for index in range(CHUNK_HEADS)]
            values = [[turned(slot, head) for slot in slots] for head in heads]
            works = [(far, index) for far in (1, 0, None) for index in range(CHUNK_HEADS)]

            def begin_work(far, index):
                head = heads[index]
                query = own_query(head) if far is None else q_far[far, :, head_lanes(head)]
                return masked_scores(head, query, slots, far is None)

            ready = begin_work(*works[0])
            for number, (far, index) in enumerate(works):
                current = ready
                if number + 1 < len(works):
                    ready = begin_work(*works[number + 1])
                result = weigh(*current, values[index])
                if far is None:
                    finish(heads[index], result[0])
                    continue
                partial_out(far, chunk, index, heads[index], result)
                if index == CHUNK_HEADS - 1:
                    send_out(far, chunk, far, ctx + 2 + 2 * far)

        gate()

    @pl.when(place == 2)
    def _():
        @each_chunk
        def _(chunk):
            follow(near_copies, DEPTH, chunk)
            arrived(q_far.at[0, :, lanes(chunk)], Q_NEAR, chunk)
            for index in range(CHUNK_HEADS):
                head = chunk * CHUNK_HEADS + index
                values = [turned(slot, head) for slot in (2, 3)]
                query = q_far[0, :, head_lanes(head)]
                partial_out(0, chunk, index, head, attend_some(head, query, (2, 3), values, False))
                value, log_total = attend_some(head, own_query(head), (2, 3), values, True)
                o_home[head_rows(head), :] = value
                s_home[chunk, index : index + 1, :] = log_total
            send_out(0, chunk, 0, ctx + 2)
            merge_behind((0,), chunk)

        merge_rest((0,))

    @pl.when(place == 3)
    def _():
        @each_chunk
        def _(chunk):
            follow(far_copies, DEPTH, chunk)
            for index in range(CHUNK_HEADS):
                head = chunk * CHUNK_HEADS + index
                values = [turned(slot, head) for slot in (2, 3)]
                value, log_total = attend_some(head, own_query(head), (2, 3), values, True)
                o_home[head_rows(head), :] = value
                s_home[chunk, index : index + 1, :] = log_total
            merge_behind((0, 1), chunk)

        merge_rest((0, 1))

    def square_copy(step, slot):
        return pltpu.make_async_remote_copy(
            src_ref=squares.at[slot], dst_ref=squares.at[slot],
            send_sem=send_sem.at[SQUARES, step], recv_sem=recv_sem.at[SQUARES, slot],
            device_id={"heads": lax.rem(mine + step, heads_size)}, device_id_type=MESH,
        )

    for step in range(1, heads_size):
        square_copy(step, mine).start()
    for step in range(1, heads_size):
        square_copy(step, lax.rem(mine + step, heads_size)).wait_recv()
    square_total = squares[0]
    for slot in range(1, heads_size):
        square_total = square_total + squares[slot]
    square_mean = jnp.sum(square_total, axis=0, keepdims=True) / (cols * heads_size)
    scale = jnp.broadcast_to(lax.rsqrt(square_mean + 1e-06), (DH, rows)).T

    def last(head, carry):
        at = head_lanes(head)
        out[:, at] = (att[:, at].astype(jnp.float32) * scale * gain[:, at] + hyena[:, at]).astype(jnp.bfloat16)
        return carry

    lax.fori_loop(0, cols // DH, last, 0)

    for step in range(1, heads_size):
        square_copy(step, mine).wait_send()

    @pl.when(ctx < ctx_size - 1)
    def _():
        sent(tail, SINGLES, 2)

    sent(k_any, SINGLES, 0)
    sent(v_any, SINGLES, 1)

    def sent_lanes(kinds):
        @each_chunk
        def _(chunk):
            for kind in kinds:
                sent(q_any.at[:, lanes(chunk)], kind, chunk)

    def sent_out(slots):
        @each_chunk
        def _(chunk):
            for slot in slots:
                sent(o_put.at[slot, chunk_rows(chunk)], O_NEAR + slot, chunk)
                sent(s_put.at[slot, chunk], S_NEAR + slot, chunk)

    pl.when(place == 2)(lambda: sent_out((0,)))

    @pl.when(place == 1)
    def _():
        sent_out((0, 1))
        sent_lanes((K_SIDE, V_SIDE))


def four_places(queries, keys, values, hyena_inputs, hyena_filter, norm_gain):
    rows, cols = queries.shape
    ctx_size, heads_size = lax.axis_size("ctx"), lax.axis_size("heads")
    chunks = cols // DH // CHUNK_HEADS
    bf16, f32 = jnp.bfloat16, jnp.float32
    count = max(chunks, heads_size, 3)
    return pl.pallas_call(
        functools.partial(fused_kernel, ctx_size, heads_size),
        out_shape=jax.ShapeDtypeStruct((rows, cols), bf16),
        in_specs=[pl.BlockSpec(memory_space=pltpu.HBM)] * 6,
        out_specs=pl.BlockSpec(memory_space=pltpu.VMEM),
        scratch_shapes=[
            pltpu.VMEM((4, rows, cols), bf16),
            pltpu.VMEM((4, rows, cols), bf16),
            pltpu.VMEM((rows, cols), bf16),
            pltpu.VMEM((2, rows, cols), bf16),
            pltpu.VMEM((2, cols, rows), bf16),
            pltpu.VMEM((2, chunks, CHUNK_HEADS, rows), f32),
            pltpu.VMEM((2, cols, rows), bf16),
            pltpu.VMEM((2, chunks, CHUNK_HEADS, rows), f32),
            pltpu.VMEM((cols, rows), f32),
            pltpu.VMEM((chunks, CHUNK_HEADS, rows), f32),
            pltpu.VMEM((rows, cols), bf16),
            pltpu.VMEM(hyena_inputs.shape, bf16),
            pltpu.VMEM((2, RIM, cols), bf16),
            pltpu.VMEM((RIM + rows, CHUNK_HEADS * DH), f32),
            pltpu.VMEM((rows, cols), f32),
            pltpu.VMEM((heads_size, 8, rows), f32),
            pltpu.VMEM(hyena_filter.shape, f32),
            pltpu.VMEM((1, cols), f32),
            pltpu.SemaphoreType.DMA((12, count)),
            pltpu.SemaphoreType.DMA((12, count)),
            pltpu.SemaphoreType.DMA((6,)),
        ],
        compiler_params=pltpu.CompilerParams(
            collective_id=0, has_side_effects=True, vmem_limit_bytes=63 * 1024 * 1024
        ),
    )(queries, keys, values, hyena_inputs, hyena_filter, norm_gain[None, :])


def on_device(queries, keys, values, hyena_inputs, hyena_filter, norm_gain):
    if lax.axis_size("ctx") == 2 * 4:
        return four_places(queries, keys, values, hyena_inputs, hyena_filter, norm_gain)
    row_count, col_count = queries.shape
    rim_rows = hyena_filter.shape[0] - 1
    tail_rows = hyena_inputs[1:, row_count - rim_rows :, :]
    earlier = from_behind(tail_rows, "ctx", 1)
    joined = jnp.concatenate([earlier, hyena_inputs[1:]], axis=1)
    product = joined[0].astype(jnp.float32) * joined[1].astype(jnp.float32)
    convolved = jnp.zeros((row_count, col_count), jnp.float32)
    for filter_tap in range(rim_rows + 1):
        convolved = (
            convolved
            + hyena_filter[filter_tap][None, :]
            * product[rim_rows - filter_tap : rim_rows - filter_tap + row_count]
        )
    hyena_out = hyena_inputs[0].astype(jnp.float32) * convolved
    attention = cycle_attention(queries, keys, values)
    attention_wide = lax.optimization_barrier(attention).astype(jnp.float32)
    local_squares = jnp.sum(attention_wide * attention_wide, axis=1)
    square_total = lax.psum(local_squares, "heads")
    square_mean = square_total / WIDTH
    normed = attention_wide * lax.rsqrt(square_mean + 1e-06)[:, None] * norm_gain[None, :]
    return (normed + hyena_out).astype(jnp.bfloat16)


def solution(mesh):
    placed = (
        P("ctx", "heads"),
        P("ctx", "heads"),
        P("ctx", "heads"),
        P(None, "ctx", "heads"),
        P(None, "heads"),
        P("heads"),
    )
    return jax.shard_map(
        on_device, mesh=mesh, in_specs=placed, out_specs=P("ctx", "heads"), check_vma=False
    )
```

```python
import functools
import math

import jax
import jax.numpy as jnp
from jax import lax
from jax.experimental import pallas as pl
from jax.experimental.pallas import tpu as pltpu
from jax.sharding import PartitionSpec as P

DH = 128
WIDTH = 8192
MESH = pl.DeviceIdType.MESH
LOG2E = 1.4426950408889634
CHUNK_HEADS = 1
DEPTH = 16
LAG = 6
RIM = 16
K_UP, V_UP, K_SIDE, V_SIDE, Q_NEAR, Q_FAR, O_NEAR, O_FAR, S_NEAR, S_FAR, SINGLES, SQUARES = range(12)


def from_behind(array, axis, by):
    size = lax.axis_size(axis)
    pairs = [(i, i + by) for i in range(size) if 0 <= i + by < size]
    return lax.ppermute(array, axis, pairs)


def attend(half_state, query_block, query_place, key_block, value_block, key_place):
    numerator, maxima, totals = half_state
    score_scale = 1.0 / math.sqrt(query_block.shape[2])
    scores = (
        jnp.einsum("qhd,khd->qhk", query_block, key_block, preferred_element_type=jnp.float32)
        * score_scale
    )
    visible = key_place[None, None, :] <= query_place[:, None, None]
    scores = jnp.where(visible, scores, -1e30)
    row_top = jnp.maximum(maxima, jnp.max(scores, axis=2))
    rescale = jnp.exp(maxima - row_top)
    weights = jnp.where(visible, jnp.exp(scores - row_top[:, :, None]), 0.0)
    totals = totals * rescale + jnp.sum(weights, axis=2)
    summed = jnp.einsum(
        "qhk,khd->qhd",
        weights.astype(jnp.bfloat16),
        value_block,
        preferred_element_type=jnp.float32,
    )
    numerator = numerator * rescale[:, :, None] + summed
    return (numerator, row_top, totals)


def fresh_state(row_total, head_total, head_size):
    return (
        jnp.zeros((row_total, head_total, head_size), jnp.float32),
        jnp.full((row_total, head_total), -1e30, jnp.float32),
        jnp.zeros((row_total, head_total), jnp.float32),
    )


def cycle_attention(queries, keys, values):
    row_count, col_count = queries.shape
    head_count = col_count // DH
    half_rows = row_count // 2
    ctx_index = lax.axis_index("ctx")
    query_starts = (ctx_index * row_count, ctx_index * row_count + half_rows)
    query_heads = queries.reshape(row_count, head_count, DH)
    query_halves = (query_heads[:half_rows], query_heads[half_rows:])
    query_places = tuple(
        (query_starts[number] + jnp.arange(half_rows, dtype=jnp.int32) for number in range(2))
    )
    empty_state = fresh_state(half_rows, head_count, DH)
    key_rows = lax.all_gather(keys, "ctx", axis=0, tiled=True)
    value_rows = lax.all_gather(values, "ctx", axis=0, tiled=True)
    count = key_rows.shape[0]
    block_rows = math.gcd(count, half_rows)
    key_heads = key_rows.reshape(count, head_count, DH)
    value_heads = value_rows.reshape(count, head_count, DH)

    def inner(block_index, state):
        first = block_index * block_rows
        key_block = lax.dynamic_slice_in_dim(key_heads, first, block_rows, 0)
        value_block = lax.dynamic_slice_in_dim(value_heads, first, block_rows, 0)
        key_place = first + jnp.arange(block_rows, dtype=jnp.int32)
        updated = []
        for number in range(2):
            query_block = query_halves[number]
            query_place = query_places[number]

            def update(half_state):
                return attend(
                    half_state, query_block, query_place, key_block, value_block, key_place
                )

            needed = key_place[0] <= query_place[half_rows - 1]
            updated.append(lax.cond(needed, update, lambda half_state: half_state, state[number]))
        return tuple(updated)

    finished = lax.fori_loop(0, count // block_rows, inner, (empty_state, empty_state))
    halves_out = [finished[number][0] / finished[number][2][:, :, None] for number in range(2)]
    return jnp.concatenate(halves_out, axis=0).reshape(row_count, col_count).astype(jnp.bfloat16)


def fused_kernel(
    ctx_size, heads_size,
    q_any, k_any, v_any, hy_any, filt_any, gain_any, out,
    k_all, v_all, q_own, q_far, o_got, s_got, o_put, s_put, o_home, s_home,
    att, hy, halo, prod, hyena, squares, filt, gain,
    send_sem, recv_sem, local_sem,
):
    rows, cols = out.shape
    chunks = cols // DH // CHUNK_HEADS
    wide = CHUNK_HEADS * DH
    ctx = lax.axis_index("ctx")
    mine = lax.axis_index("heads")
    core = lax.rem(ctx, 2)
    place = ctx // 2
    side = ctx + 1 - 2 * core
    factor = LOG2E / math.sqrt(DH)

    local = [
        pltpu.make_async_copy(hy_any, hy, local_sem.at[0]),
        pltpu.make_async_copy(filt_any, filt, local_sem.at[1]),
        pltpu.make_async_copy(k_any, k_all.at[2 + core], local_sem.at[2]),
        pltpu.make_async_copy(v_any, v_all.at[2 + core], local_sem.at[3]),
        pltpu.make_async_copy(q_any, q_own, local_sem.at[4]),
        pltpu.make_async_copy(gain_any, gain, local_sem.at[5]),
    ]
    for copy in local[2:5] + local[:2] + local[5:]:
        copy.start()
    barrier = pltpu.get_barrier_semaphore()
    for step in range(1, ctx_size):
        pl.semaphore_signal(
            barrier, inc=1, device_id={"ctx": lax.rem(ctx + step, ctx_size)}, device_id_type=MESH
        )
    for step in range(1, heads_size):
        pl.semaphore_signal(
            barrier, inc=1, device_id={"heads": lax.rem(mine + step, heads_size)}, device_id_type=MESH
        )
    pl.semaphore_wait(barrier, ctx_size + heads_size - 2)
    for copy in local[2:5]:
        copy.wait()

    def remote(src, dst, kind, at, target):
        return pltpu.make_async_remote_copy(
            src_ref=src, dst_ref=dst, send_sem=send_sem.at[kind, at], recv_sem=recv_sem.at[kind, at],
            device_id={"ctx": target}, device_id_type=MESH,
        )

    def arrived(dst, kind, at):
        remote(dst, dst, kind, at, side).wait_recv()

    def sent(src, kind, at):
        remote(src, src, kind, at, side).wait_send()

    def lanes(chunk):
        return pl.ds(pl.multiple_of(chunk * wide, wide), wide)

    def head_lanes(head):
        return pl.ds(pl.multiple_of(head * DH, DH), DH)

    def each_chunk(body):
        def step(chunk, carry):
            body(chunk)
            return carry

        lax.fori_loop(0, chunks, step, 0)

    tail = hy_any.at[pl.ds(1, 2), pl.ds(rows - RIM, RIM), :]

    def send_tail():
        remote(tail, halo, SINGLES, 2, ctx + 1).start()

    pl.when((ctx < ctx_size - 1) & (ctx != 1))(send_tail)
    remote(k_any, k_all.at[2 + core], SINGLES, 0, side).start()
    remote(v_any, v_all.at[2 + core], SINGLES, 1, side).start()

    def up_copies(chunk):
        at = lanes(chunk)
        return (
            remote(k_all.at[2 + core, :, at], k_all.at[core, :, at], K_UP, chunk, ctx + 2),
            remote(v_all.at[2 + core, :, at], v_all.at[core, :, at], V_UP, chunk, ctx + 2),
        )

    def near_copies(chunk):
        at = lanes(chunk)
        return (remote(q_own.at[:, at], q_far.at[0, :, at], Q_NEAR, chunk, ctx - 2),)

    def far_copies(chunk):
        at = lanes(chunk)
        return (remote(q_own.at[:, at], q_far.at[1, :, at], Q_FAR, chunk, ctx - 4),) + near_copies(chunk)

    def begin(copies, depth):
        def step(chunk, carry):
            for copy in copies(chunk):
                copy.start()
            return carry

        lax.fori_loop(0, min(depth, chunks), step, 0)

    def follow(copies, depth, chunk):
        for copy in copies(chunk):
            copy.wait_send()

        @pl.when(chunk + depth < chunks)
        def _():
            for copy in copies(chunk + depth):
                copy.start()

    pl.when(place == 0)(lambda: begin(up_copies, DEPTH))
    pl.when(place == 2)(lambda: begin(near_copies, DEPTH))
    pl.when(place == 3)(lambda: begin(far_copies, DEPTH))

    def gate(count, rim):
        @each_chunk
        def _(chunk):
            at = lanes(chunk)
            part = pl.ds(0, count)
            if rim:
                prod[:RIM] = halo[0, :, at].astype(jnp.float32) * halo[1, :, at].astype(jnp.float32)
            else:
                prod[:RIM] = jnp.zeros((RIM, wide), jnp.float32)
            prod[RIM : RIM + count] = hy[1, part, at].astype(jnp.float32) * hy[2, part, at].astype(jnp.float32)
            taps = filt[:, at]
            summed = taps[0:1] * prod[RIM : RIM + count]
            for tap in range(1, filt.shape[0]):
                summed = summed + taps[tap : tap + 1] * prod[RIM - tap : RIM - tap + count]
            hyena[part, at] = hy[0, part, at].astype(jnp.float32) * summed

    def redo_rim():
        arrived(halo, SINGLES, 2)
        gate(RIM, True)

    for copy in local[:2]:
        copy.wait()
    gate(rows, False)
    pl.when(place >= 2)(redo_rim)

    local[5].wait()
    arrived(k_all.at[2], SINGLES, 0)
    arrived(v_all.at[2], SINGLES, 1)
    squares[mine] = jnp.zeros_like(squares[mine])

    key_place = lax.broadcasted_iota(jnp.int32, (rows, rows), 0)
    query_place = lax.broadcasted_iota(jnp.int32, (rows, rows), 1) + core * rows

    def scores(slot, head, query):
        return lax.dot_general(
            k_all[slot, :, head_lanes(head)], query, (((1,), (1,)), ((), ())),
            preferred_element_type=jnp.float32,
        )

    def turned(slot, head):
        return v_all[slot, :, head_lanes(head)].T

    def masked_scores(head, query, slots, masked):
        tiles = [scores(slot, head, query) for slot in slots]
        if masked:
            tiles = [
                jnp.where(key_place + (slot - 2) * rows <= query_place, tile, -1e30) if slot >= 2 else tile
                for slot, tile in zip(slots, tiles)
            ]
        return tiles, functools.reduce(jnp.maximum, [jnp.max(tile, axis=0, keepdims=True) for tile in tiles])

    def weigh(tiles, top, turned_values):
        total, numerator = 0.0, 0.0
        for tile, value in zip(tiles, turned_values):
            weights = jnp.exp2((tile - top) * factor)
            total = total + jnp.sum(weights, axis=0, keepdims=True)
            numerator = numerator + jnp.dot(
                value, weights.astype(jnp.bfloat16), preferred_element_type=jnp.float32
            )
        return numerator / total, top * factor + jnp.log(total) * LOG2E

    def attend_some(head, query, slots, turned_values, masked):
        return weigh(*masked_scores(head, query, slots, masked), turned_values)

    def finish(head, value):
        rounded = value.astype(jnp.bfloat16).astype(jnp.float32)
        squares[mine] += jnp.sum((rounded * rounded).reshape(DH // 8, 8, rows), axis=0)
        att[:, head_lanes(head)] = rounded.T.astype(jnp.bfloat16)

    def head_rows(head):
        return pl.ds(pl.multiple_of(head * DH, DH), DH)

    def chunk_rows(chunk):
        return pl.ds(pl.multiple_of(chunk * wide, wide), wide)

    def partial_out(slot, chunk, index, head, result):
        value, log_total = result
        o_put[slot, head_rows(head), :] = value.astype(jnp.bfloat16)
        s_put[slot, chunk, index : index + 1, :] = log_total

    def send_out(slot, chunk, to_slot, target):
        at = chunk_rows(chunk)
        remote(o_put.at[slot, at], o_got.at[to_slot, at], O_NEAR + to_slot, chunk, target).start()
        remote(s_put.at[slot, chunk], s_got.at[to_slot, chunk], S_NEAR + to_slot, chunk, target).start()

    def merge(slots, chunk):
        for slot in slots:
            arrived(o_got.at[slot, chunk_rows(chunk)], O_NEAR + slot, chunk)
            arrived(s_got.at[slot, chunk], S_NEAR + slot, chunk)
        for index in range(CHUNK_HEADS):
            head = chunk * CHUNK_HEADS + index
            logs = [s_home[chunk, index : index + 1, :]]
            parts = [o_home[head_rows(head), :]]
            for slot in slots:
                logs.append(s_got[slot, chunk, index : index + 1, :])
                parts.append(o_got[slot, head_rows(head), :].astype(jnp.float32))
            top = functools.reduce(jnp.maximum, logs)
            shares = [jnp.exp2(log - top) for log in logs]
            inverse = 1.0 / sum(shares)
            finish(head, sum(part * (share * inverse) for part, share in zip(parts, shares)))

    def merge_behind(slots, chunk):
        pl.when(chunk >= LAG)(lambda: merge(slots, chunk - LAG))

    def merge_rest(slots):
        def step(chunk, carry):
            merge(slots, chunk)
            return carry

        lax.fori_loop(max(chunks - LAG, 0), chunks, step, 0)

    def own_query(head):
        return q_own[:, head_lanes(head)]

    @pl.when(place == 0)
    def _():
        @each_chunk
        def _(chunk):
            follow(up_copies, DEPTH, chunk)
            for index in range(CHUNK_HEADS):
                head = chunk * CHUNK_HEADS + index
                values = [turned(slot, head) for slot in (2, 3)]
                finish(head, attend_some(head, own_query(head), (2, 3), values, True)[0])

        pl.when(core == 1)(send_tail)
        pl.when(core == 1)(redo_rim)

    @pl.when(place == 1)
    def _():
        def forward(chunk):
            at = lanes(chunk)
            arrived(k_all.at[core, :, at], K_UP, chunk)
            remote(k_all.at[core, :, at], k_all.at[core, :, at], K_SIDE, chunk, side).start()
            arrived(v_all.at[core, :, at], V_UP, chunk)
            remote(v_all.at[core, :, at], v_all.at[core, :, at], V_SIDE, chunk, side).start()

        forward(0)

        @each_chunk
        def _(chunk):
            at = lanes(chunk)
            arrived(q_far.at[1, :, at], Q_FAR, chunk)
            arrived(q_far.at[0, :, at], Q_NEAR, chunk)
            arrived(k_all.at[1 - core, :, at], K_SIDE, chunk)
            arrived(v_all.at[1 - core, :, at], V_SIDE, chunk)
            slots = (0, 1, 2, 3)
            heads = [chunk * CHUNK_HEADS + index for index in range(CHUNK_HEADS)]
            values = [[turned(slot, head) for slot in slots] for head in heads]
            works = [(far, index) for far in (1, 0, None) for index in range(CHUNK_HEADS)]

            def begin_work(far, index):
                head = heads[index]
                query = own_query(head) if far is None else q_far[far, :, head_lanes(head)]
                return masked_scores(head, query, slots, far is None)

            ready = begin_work(*works[0])
            for number, (far, index) in enumerate(works):
                current = ready
                if number + 1 < len(works):
                    ready = begin_work(*works[number + 1])
                result = weigh(*current, values[index])
                if far is None:
                    finish(heads[index], result[0])
                    continue
                partial_out(far, chunk, index, heads[index], result)
                if index == CHUNK_HEADS - 1:
                    send_out(far, chunk, far, ctx + 2 + 2 * far)
                    if far == 0:
                        pl.when(chunk + 1 < chunks)(lambda: forward(chunk + 1))

        redo_rim()

    @pl.when(place == 2)
    def _():
        @each_chunk
        def _(chunk):
            follow(near_copies, DEPTH, chunk)
            arrived(q_far.at[0, :, lanes(chunk)], Q_NEAR, chunk)
            for index in range(CHUNK_HEADS):
                head = chunk * CHUNK_HEADS + index
                values = [turned(slot, head) for slot in (2, 3)]
                query = q_far[0, :, head_lanes(head)]
                partial_out(0, chunk, index, head, attend_some(head, query, (2, 3), values, False))
                value, log_total = attend_some(head, own_query(head), (2, 3), values, True)
                o_home[head_rows(head), :] = value
                s_home[chunk, index : index + 1, :] = log_total
            send_out(0, chunk, 0, ctx + 2)
            merge_behind((0,), chunk)

        merge_rest((0,))

    @pl.when(place == 3)
    def _():
        @each_chunk
        def _(chunk):
            follow(far_copies, DEPTH, chunk)
            for index in range(CHUNK_HEADS):
                head = chunk * CHUNK_HEADS + index
                values = [turned(slot, head) for slot in (2, 3)]
                value, log_total = attend_some(head, own_query(head), (2, 3), values, True)
                o_home[head_rows(head), :] = value
                s_home[chunk, index : index + 1, :] = log_total
            merge_behind((0, 1), chunk)

        merge_rest((0, 1))

    def square_copy(step, slot):
        return pltpu.make_async_remote_copy(
            src_ref=squares.at[slot], dst_ref=squares.at[slot],
            send_sem=send_sem.at[SQUARES, step], recv_sem=recv_sem.at[SQUARES, slot],
            device_id={"heads": lax.rem(mine + step, heads_size)}, device_id_type=MESH,
        )

    for step in range(1, heads_size):
        square_copy(step, mine).start()
    for step in range(1, heads_size):
        square_copy(step, lax.rem(mine + step, heads_size)).wait_recv()
    square_total = squares[0]
    for slot in range(1, heads_size):
        square_total = square_total + squares[slot]
    square_mean = jnp.sum(square_total, axis=0, keepdims=True) / (cols * heads_size)
    scale = jnp.broadcast_to(lax.rsqrt(square_mean + 1e-06), (DH, rows)).T

    def last(head, carry):
        at = head_lanes(head)
        out[:, at] = (att[:, at].astype(jnp.float32) * scale * gain[:, at] + hyena[:, at]).astype(jnp.bfloat16)
        return carry

    lax.fori_loop(0, cols // DH, last, 0)

    for step in range(1, heads_size):
        square_copy(step, mine).wait_send()

    @pl.when(ctx < ctx_size - 1)
    def _():
        sent(tail, SINGLES, 2)

    sent(k_any, SINGLES, 0)
    sent(v_any, SINGLES, 1)

    def sent_lanes(kinds):
        @each_chunk
        def _(chunk):
            for kind in kinds:
                sent(q_any.at[:, lanes(chunk)], kind, chunk)

    def sent_out(slots):
        @each_chunk
        def _(chunk):
            for slot in slots:
                sent(o_put.at[slot, chunk_rows(chunk)], O_NEAR + slot, chunk)
                sent(s_put.at[slot, chunk], S_NEAR + slot, chunk)

    pl.when(place == 2)(lambda: sent_out((0,)))

    @pl.when(place == 1)
    def _():
        sent_out((0, 1))
        sent_lanes((K_SIDE, V_SIDE))


def four_places(queries, keys, values, hyena_inputs, hyena_filter, norm_gain):
    rows, cols = queries.shape
    ctx_size, heads_size = lax.axis_size("ctx"), lax.axis_size("heads")
    chunks = cols // DH // CHUNK_HEADS
    bf16, f32 = jnp.bfloat16, jnp.float32
    count = max(chunks, heads_size, 3)
    return pl.pallas_call(
        functools.partial(fused_kernel, ctx_size, heads_size),
        out_shape=jax.ShapeDtypeStruct((rows, cols), bf16),
        in_specs=[pl.BlockSpec(memory_space=pltpu.HBM)] * 6,
        out_specs=pl.BlockSpec(memory_space=pltpu.VMEM),
        scratch_shapes=[
            pltpu.VMEM((4, rows, cols), bf16),
            pltpu.VMEM((4, rows, cols), bf16),
            pltpu.VMEM((rows, cols), bf16),
            pltpu.VMEM((2, rows, cols), bf16),
            pltpu.VMEM((2, cols, rows), bf16),
            pltpu.VMEM((2, chunks, CHUNK_HEADS, rows), f32),
            pltpu.VMEM((2, cols, rows), bf16),
            pltpu.VMEM((2, chunks, CHUNK_HEADS, rows), f32),
            pltpu.VMEM((cols, rows), f32),
            pltpu.VMEM((chunks, CHUNK_HEADS, rows), f32),
            pltpu.VMEM((rows, cols), bf16),
            pltpu.VMEM(hyena_inputs.shape, bf16),
            pltpu.VMEM((2, RIM, cols), bf16),
            pltpu.VMEM((RIM + rows, CHUNK_HEADS * DH), f32),
            pltpu.VMEM((rows, cols), f32),
            pltpu.VMEM((heads_size, 8, rows), f32),
            pltpu.VMEM(hyena_filter.shape, f32),
            pltpu.VMEM((1, cols), f32),
            pltpu.SemaphoreType.DMA((12, count)),
            pltpu.SemaphoreType.DMA((12, count)),
            pltpu.SemaphoreType.DMA((6,)),
        ],
        compiler_params=pltpu.CompilerParams(
            collective_id=0, has_side_effects=True, vmem_limit_bytes=52 * 1024 * 1024
        ),
    )(queries, keys, values, hyena_inputs, hyena_filter, norm_gain[None, :])


def on_device(queries, keys, values, hyena_inputs, hyena_filter, norm_gain):
    if lax.axis_size("ctx") == 2 * 4:
        return four_places(queries, keys, values, hyena_inputs, hyena_filter, norm_gain)
    row_count, col_count = queries.shape
    rim_rows = hyena_filter.shape[0] - 1
    tail_rows = hyena_inputs[1:, row_count - rim_rows :, :]
    earlier = from_behind(tail_rows, "ctx", 1)
    joined = jnp.concatenate([earlier, hyena_inputs[1:]], axis=1)
    product = joined[0].astype(jnp.float32) * joined[1].astype(jnp.float32)
    convolved = jnp.zeros((row_count, col_count), jnp.float32)
    for filter_tap in range(rim_rows + 1):
        convolved = (
            convolved
            + hyena_filter[filter_tap][None, :]
            * product[rim_rows - filter_tap : rim_rows - filter_tap + row_count]
        )
    hyena_out = hyena_inputs[0].astype(jnp.float32) * convolved
    attention = cycle_attention(queries, keys, values)
    attention_wide = lax.optimization_barrier(attention).astype(jnp.float32)
    local_squares = jnp.sum(attention_wide * attention_wide, axis=1)
    square_total = lax.psum(local_squares, "heads")
    square_mean = square_total / WIDTH
    normed = attention_wide * lax.rsqrt(square_mean + 1e-06)[:, None] * norm_gain[None, :]
    return (normed + hyena_out).astype(jnp.bfloat16)


def solution(mesh):
    placed = (
        P("ctx", "heads"),
        P("ctx", "heads"),
        P("ctx", "heads"),
        P(None, "ctx", "heads"),
        P(None, "heads"),
        P("heads"),
    )
    return jax.shard_map(
        on_device, mesh=mesh, in_specs=placed, out_specs=P("ctx", "heads"), check_vma=False
    )
```

```python
import functools
import math

import jax
import jax.numpy as jnp
from jax import lax
from jax.experimental import pallas as pl
from jax.experimental.pallas import tpu as pltpu
from jax.sharding import PartitionSpec as P

DH = 128
WIDTH = 8192
MESH = pl.DeviceIdType.MESH
LOG2E = 1.4426950408889634
CHUNK_HEADS = 1
LAG = 6
RIM = 16
K_UP, V_UP, K_SIDE, V_SIDE, Q_NEAR, Q_FAR, O_NEAR, O_FAR, S_NEAR, S_FAR, SINGLES, SQUARES = range(12)
K_SIB, V_SIB = 12, 13


def from_behind(array, axis, by):
    size = lax.axis_size(axis)
    pairs = [(i, i + by) for i in range(size) if 0 <= i + by < size]
    return lax.ppermute(array, axis, pairs)


def attend(half_state, query_block, query_place, key_block, value_block, key_place):
    numerator, maxima, totals = half_state
    score_scale = 1.0 / math.sqrt(query_block.shape[2])
    scores = (
        jnp.einsum("qhd,khd->qhk", query_block, key_block, preferred_element_type=jnp.float32)
        * score_scale
    )
    visible = key_place[None, None, :] <= query_place[:, None, None]
    scores = jnp.where(visible, scores, -1e30)
    row_top = jnp.maximum(maxima, jnp.max(scores, axis=2))
    rescale = jnp.exp(maxima - row_top)
    weights = jnp.where(visible, jnp.exp(scores - row_top[:, :, None]), 0.0)
    totals = totals * rescale + jnp.sum(weights, axis=2)
    summed = jnp.einsum(
        "qhk,khd->qhd",
        weights.astype(jnp.bfloat16),
        value_block,
        preferred_element_type=jnp.float32,
    )
    numerator = numerator * rescale[:, :, None] + summed
    return (numerator, row_top, totals)


def fresh_state(row_total, head_total, head_size):
    return (
        jnp.zeros((row_total, head_total, head_size), jnp.float32),
        jnp.full((row_total, head_total), -1e30, jnp.float32),
        jnp.zeros((row_total, head_total), jnp.float32),
    )


def cycle_attention(queries, keys, values):
    row_count, col_count = queries.shape
    head_count = col_count // DH
    half_rows = row_count // 2
    ctx_index = lax.axis_index("ctx")
    query_starts = (ctx_index * row_count, ctx_index * row_count + half_rows)
    query_heads = queries.reshape(row_count, head_count, DH)
    query_halves = (query_heads[:half_rows], query_heads[half_rows:])
    query_places = tuple(
        (query_starts[number] + jnp.arange(half_rows, dtype=jnp.int32) for number in range(2))
    )
    empty_state = fresh_state(half_rows, head_count, DH)
    key_rows = lax.all_gather(keys, "ctx", axis=0, tiled=True)
    value_rows = lax.all_gather(values, "ctx", axis=0, tiled=True)
    count = key_rows.shape[0]
    block_rows = math.gcd(count, half_rows)
    key_heads = key_rows.reshape(count, head_count, DH)
    value_heads = value_rows.reshape(count, head_count, DH)

    def inner(block_index, state):
        first = block_index * block_rows
        key_block = lax.dynamic_slice_in_dim(key_heads, first, block_rows, 0)
        value_block = lax.dynamic_slice_in_dim(value_heads, first, block_rows, 0)
        key_place = first + jnp.arange(block_rows, dtype=jnp.int32)
        updated = []
        for number in range(2):
            query_block = query_halves[number]
            query_place = query_places[number]

            def update(half_state):
                return attend(
                    half_state, query_block, query_place, key_block, value_block, key_place
                )

            needed = key_place[0] <= query_place[half_rows - 1]
            updated.append(lax.cond(needed, update, lambda half_state: half_state, state[number]))
        return tuple(updated)

    finished = lax.fori_loop(0, count // block_rows, inner, (empty_state, empty_state))
    halves_out = [finished[number][0] / finished[number][2][:, :, None] for number in range(2)]
    return jnp.concatenate(halves_out, axis=0).reshape(row_count, col_count).astype(jnp.bfloat16)


def fused_kernel(
    ctx_size, heads_size,
    q_any, k_any, v_any, hy_any, filt_any, gain_any, out,
    k_all, v_all, q_own, q_far, o_got, s_got, o_put, s_put, o_home, s_home,
    att, hy, halo, prod, hyena, squares, filt, gain,
    send_sem, recv_sem, local_sem,
):
    rows, cols = out.shape
    chunks = cols // DH // CHUNK_HEADS
    wide = CHUNK_HEADS * DH
    ctx = lax.axis_index("ctx")
    mine = lax.axis_index("heads")
    core = lax.rem(ctx, 2)
    place = ctx // 2
    side = ctx + 1 - 2 * core
    factor = LOG2E / math.sqrt(DH)

    local = [
        pltpu.make_async_copy(hy_any, hy, local_sem.at[0]),
        pltpu.make_async_copy(filt_any, filt, local_sem.at[1]),
        pltpu.make_async_copy(k_any, k_all.at[2 + core], local_sem.at[2]),
        pltpu.make_async_copy(v_any, v_all.at[2 + core], local_sem.at[3]),
        pltpu.make_async_copy(q_any, q_own, local_sem.at[4]),
        pltpu.make_async_copy(gain_any, gain, local_sem.at[5]),
    ]
    for copy in local[2:5] + local[:2] + local[5:]:
        copy.start()
    barrier = pltpu.get_barrier_semaphore()
    for step in range(1, ctx_size):
        pl.semaphore_signal(
            barrier, inc=1, device_id={"ctx": lax.rem(ctx + step, ctx_size)}, device_id_type=MESH
        )
    for step in range(1, heads_size):
        pl.semaphore_signal(
            barrier, inc=1, device_id={"heads": lax.rem(mine + step, heads_size)}, device_id_type=MESH
        )
    pl.semaphore_wait(barrier, ctx_size + heads_size - 2)
    for copy in local[2:5]:
        copy.wait()

    def remote(src, dst, kind, at, target):
        return pltpu.make_async_remote_copy(
            src_ref=src, dst_ref=dst, send_sem=send_sem.at[kind, at], recv_sem=recv_sem.at[kind, at],
            device_id={"ctx": target}, device_id_type=MESH,
        )

    def arrived(dst, kind, at):
        remote(dst, dst, kind, at, side).wait_recv()

    def sent(src, kind, at):
        remote(src, src, kind, at, side).wait_send()

    def lanes(chunk):
        return pl.ds(pl.multiple_of(chunk * wide, wide), wide)

    def head_lanes(head):
        return pl.ds(pl.multiple_of(head * DH, DH), DH)

    def each_chunk(body):
        def step(chunk, carry):
            body(chunk)
            return carry

        lax.fori_loop(0, chunks, step, 0)

    tail = hy_any.at[pl.ds(1, 2), pl.ds(rows - RIM, RIM), :]

    def send_tail():
        remote(tail, halo, SINGLES, 2, ctx + 1).start()

    def up_copies(chunk):
        at = lanes(chunk)
        return (
            remote(k_all.at[2 + core, :, at], k_all.at[core, :, at], K_UP, chunk, ctx + 2),
            remote(v_all.at[2 + core, :, at], v_all.at[core, :, at], V_UP, chunk, ctx + 2),
        )

    def near_copies(chunk):
        at = lanes(chunk)
        return (remote(q_own.at[:, at], q_far.at[0, :, at], Q_NEAR, chunk, ctx - 2),)

    def far_copies(chunk):
        at = lanes(chunk)
        return (remote(q_own.at[:, at], q_far.at[1, :, at], Q_FAR, chunk, ctx - 4),) + near_copies(chunk)

    def sibling_copies(chunk):
        at = lanes(chunk)
        return (
            remote(k_all.at[2 + core, :, at], k_all.at[2 + core, :, at], K_SIB, chunk, side),
            remote(v_all.at[2 + core, :, at], v_all.at[2 + core, :, at], V_SIB, chunk, side),
        )

    def sibling_arrived(chunk):
        arrived(k_all.at[3 - core, :, lanes(chunk)], K_SIB, chunk)
        arrived(v_all.at[3 - core, :, lanes(chunk)], V_SIB, chunk)

    @each_chunk
    def _(chunk):
        def begin(copies):
            for copy in copies(chunk):
                copy.start()

        pl.when(place == 0)(lambda: begin(up_copies))
        pl.when(place == 2)(lambda: begin(near_copies))
        pl.when(place == 3)(lambda: begin(far_copies))
        begin(sibling_copies)
        pl.when((ctx < ctx_size - 1) & (ctx != 1) & (chunk == 1))(send_tail)

    def gate(count, rim):
        @each_chunk
        def _(chunk):
            at = lanes(chunk)
            part = pl.ds(0, count)
            if rim:
                prod[:RIM] = halo[0, :, at].astype(jnp.float32) * halo[1, :, at].astype(jnp.float32)
            else:
                prod[:RIM] = jnp.zeros((RIM, wide), jnp.float32)
            prod[RIM : RIM + count] = hy[1, part, at].astype(jnp.float32) * hy[2, part, at].astype(jnp.float32)
            taps = filt[:, at]
            summed = taps[0:1] * prod[RIM : RIM + count]
            for tap in range(1, filt.shape[0]):
                summed = summed + taps[tap : tap + 1] * prod[RIM - tap : RIM - tap + count]
            hyena[part, at] = hy[0, part, at].astype(jnp.float32) * summed

    def redo_rim():
        arrived(halo, SINGLES, 2)
        gate(RIM, True)

    for copy in local[:2]:
        copy.wait()
    gate(rows, False)

    local[5].wait()
    squares[mine] = jnp.zeros_like(squares[mine])

    key_place = lax.broadcasted_iota(jnp.int32, (rows, rows), 0)
    query_place = lax.broadcasted_iota(jnp.int32, (rows, rows), 1) + core * rows

    def scores(slot, head, query):
        return lax.dot_general(
            k_all[slot, :, head_lanes(head)], query, (((1,), (1,)), ((), ())),
            preferred_element_type=jnp.float32,
        )

    def turned(slot, head):
        return v_all[slot, :, head_lanes(head)].T

    def masked_scores(head, query, slots, masked):
        tiles = [scores(slot, head, query) for slot in slots]
        if masked:
            tiles = [
                jnp.where(key_place + (slot - 2) * rows <= query_place, tile, -1e30) if slot >= 2 else tile
                for slot, tile in zip(slots, tiles)
            ]
        return tiles, functools.reduce(jnp.maximum, [jnp.max(tile, axis=0, keepdims=True) for tile in tiles])

    def weigh(tiles, top, turned_values):
        total, numerator = 0.0, 0.0
        for tile, value in zip(tiles, turned_values):
            weights = jnp.exp2((tile - top) * factor)
            total = total + jnp.sum(weights, axis=0, keepdims=True)
            numerator = numerator + jnp.dot(
                value, weights.astype(jnp.bfloat16), preferred_element_type=jnp.float32
            )
        return numerator / total, top * factor + jnp.log(total) * LOG2E

    def attend_some(head, query, slots, turned_values, masked):
        return weigh(*masked_scores(head, query, slots, masked), turned_values)

    def finish(head, value):
        rounded = value.astype(jnp.bfloat16).astype(jnp.float32)
        squares[mine] += jnp.sum((rounded * rounded).reshape(DH // 8, 8, rows), axis=0)
        att[:, head_lanes(head)] = rounded.T.astype(jnp.bfloat16)

    def head_rows(head):
        return pl.ds(pl.multiple_of(head * DH, DH), DH)

    def chunk_rows(chunk):
        return pl.ds(pl.multiple_of(chunk * wide, wide), wide)

    def partial_out(slot, chunk, index, head, result):
        value, log_total = result
        o_put[slot, head_rows(head), :] = value.astype(jnp.bfloat16)
        s_put[slot, chunk, index : index + 1, :] = log_total

    def send_out(slot, chunk, to_slot, target):
        at = chunk_rows(chunk)
        remote(o_put.at[slot, at], o_got.at[to_slot, at], O_NEAR + to_slot, chunk, target).start()
        remote(s_put.at[slot, chunk], s_got.at[to_slot, chunk], S_NEAR + to_slot, chunk, target).start()

    def merge(slots, chunk):
        for slot in slots:
            arrived(o_got.at[slot, chunk_rows(chunk)], O_NEAR + slot, chunk)
            arrived(s_got.at[slot, chunk], S_NEAR + slot, chunk)
        for index in range(CHUNK_HEADS):
            head = chunk * CHUNK_HEADS + index
            logs = [s_home[chunk, index : index + 1, :]]
            parts = [o_home[head_rows(head), :]]
            for slot in slots:
                logs.append(s_got[slot, chunk, index : index + 1, :])
                parts.append(o_got[slot, head_rows(head), :].astype(jnp.float32))
            top = functools.reduce(jnp.maximum, logs)
            shares = [jnp.exp2(log - top) for log in logs]
            inverse = 1.0 / sum(shares)
            finish(head, sum(part * (share * inverse) for part, share in zip(parts, shares)))

    def merge_behind(slots, chunk):
        pl.when(chunk >= LAG)(lambda: merge(slots, chunk - LAG))

    def merge_rest(slots):
        def step(chunk, carry):
            merge(slots, chunk)
            return carry

        lax.fori_loop(max(chunks - LAG, 0), chunks, step, 0)

    def own_query(head):
        return q_own[:, head_lanes(head)]

    @pl.when(place == 0)
    def _():
        @each_chunk
        def _(chunk):
            sibling_arrived(chunk)
            for index in range(CHUNK_HEADS):
                head = chunk * CHUNK_HEADS + index
                values = [turned(slot, head) for slot in (2, 3)]
                finish(head, attend_some(head, own_query(head), (2, 3), values, True)[0])

        pl.when(core == 1)(send_tail)
        pl.when(core == 1)(redo_rim)

    @pl.when(place == 1)
    def _():
        def forward(chunk):
            at = lanes(chunk)
            arrived(k_all.at[core, :, at], K_UP, chunk)
            remote(k_all.at[core, :, at], k_all.at[core, :, at], K_SIDE, chunk, side).start()
            arrived(v_all.at[core, :, at], V_UP, chunk)
            remote(v_all.at[core, :, at], v_all.at[core, :, at], V_SIDE, chunk, side).start()

        forward(0)

        @each_chunk
        def _(chunk):
            at = lanes(chunk)
            sibling_arrived(chunk)
            arrived(q_far.at[1, :, at], Q_FAR, chunk)
            arrived(q_far.at[0, :, at], Q_NEAR, chunk)
            arrived(k_all.at[1 - core, :, at], K_SIDE, chunk)
            arrived(v_all.at[1 - core, :, at], V_SIDE, chunk)
            slots = (0, 1, 2, 3)
            heads = [chunk * CHUNK_HEADS + index for index in range(CHUNK_HEADS)]
            values = [[turned(slot, head) for slot in slots] for head in heads]
            works = [(far, index) for far in (1, 0, None) for index in range(CHUNK_HEADS)]

            def begin_work(far, index):
                head = heads[index]
                query = own_query(head) if far is None else q_far[far, :, head_lanes(head)]
                return masked_scores(head, query, slots, far is None)

            ready = begin_work(*works[0])
            for number, (far, index) in enumerate(works):
                current = ready
                if number + 1 < len(works):
                    ready = begin_work(*works[number + 1])
                result = weigh(*current, values[index])
                if far is None:
                    finish(heads[index], result[0])
                    continue
                partial_out(far, chunk, index, heads[index], result)
                if index == CHUNK_HEADS - 1:
                    send_out(far, chunk, far, ctx + 2 + 2 * far)
                    if far == 0:
                        pl.when(chunk + 1 < chunks)(lambda: forward(chunk + 1))

        redo_rim()

    @pl.when(place == 2)
    def _():
        @each_chunk
        def _(chunk):
            sibling_arrived(chunk)
            arrived(q_far.at[0, :, lanes(chunk)], Q_NEAR, chunk)
            for index in range(CHUNK_HEADS):
                head = chunk * CHUNK_HEADS + index
                values = [turned(slot, head) for slot in (2, 3)]
                query = q_far[0, :, head_lanes(head)]
                partial_out(0, chunk, index, head, attend_some(head, query, (2, 3), values, False))
                value, log_total = attend_some(head, own_query(head), (2, 3), values, True)
                o_home[head_rows(head), :] = value
                s_home[chunk, index : index + 1, :] = log_total
            send_out(0, chunk, 0, ctx + 2)
            merge_behind((0,), chunk)

        redo_rim()
        merge_rest((0,))

    @pl.when(place == 3)
    def _():
        @each_chunk
        def _(chunk):
            sibling_arrived(chunk)
            for index in range(CHUNK_HEADS):
                head = chunk * CHUNK_HEADS + index
                values = [turned(slot, head) for slot in (2, 3)]
                value, log_total = attend_some(head, own_query(head), (2, 3), values, True)
                o_home[head_rows(head), :] = value
                s_home[chunk, index : index + 1, :] = log_total
            merge_behind((0, 1), chunk)

        redo_rim()
        merge_rest((0, 1))

    def square_copy(step, slot):
        return pltpu.make_async_remote_copy(
            src_ref=squares.at[slot], dst_ref=squares.at[slot],
            send_sem=send_sem.at[SQUARES, step], recv_sem=recv_sem.at[SQUARES, slot],
            device_id={"heads": lax.rem(mine + step, heads_size)}, device_id_type=MESH,
        )

    for step in range(1, heads_size):
        square_copy(step, mine).start()
    for step in range(1, heads_size):
        square_copy(step, lax.rem(mine + step, heads_size)).wait_recv()
    square_total = squares[0]
    for slot in range(1, heads_size):
        square_total = square_total + squares[slot]
    square_mean = jnp.sum(square_total, axis=0, keepdims=True) / (cols * heads_size)
    scale = jnp.broadcast_to(lax.rsqrt(square_mean + 1e-06), (DH, rows)).T

    def last(head, carry):
        at = head_lanes(head)
        out[:, at] = (att[:, at].astype(jnp.float32) * scale * gain[:, at] + hyena[:, at]).astype(jnp.bfloat16)
        return carry

    lax.fori_loop(0, cols // DH, last, 0)

    for step in range(1, heads_size):
        square_copy(step, mine).wait_send()

    @pl.when(ctx < ctx_size - 1)
    def _():
        sent(tail, SINGLES, 2)

    def sent_lanes(kinds):
        @each_chunk
        def _(chunk):
            for kind in kinds:
                sent(q_any.at[:, lanes(chunk)], kind, chunk)

    def sent_out(slots):
        @each_chunk
        def _(chunk):
            for slot in slots:
                sent(o_put.at[slot, chunk_rows(chunk)], O_NEAR + slot, chunk)
                sent(s_put.at[slot, chunk], S_NEAR + slot, chunk)

    sent_lanes((K_SIB, V_SIB))
    pl.when(place == 0)(lambda: sent_lanes((K_UP, V_UP)))
    pl.when(place == 2)(lambda: sent_lanes((Q_NEAR,)))
    pl.when(place == 3)(lambda: sent_lanes((Q_NEAR, Q_FAR)))
    pl.when(place == 2)(lambda: sent_out((0,)))

    @pl.when(place == 1)
    def _():
        sent_out((0, 1))
        sent_lanes((K_SIDE, V_SIDE))


def four_places(queries, keys, values, hyena_inputs, hyena_filter, norm_gain):
    rows, cols = queries.shape
    ctx_size, heads_size = lax.axis_size("ctx"), lax.axis_size("heads")
    chunks = cols // DH // CHUNK_HEADS
    bf16, f32 = jnp.bfloat16, jnp.float32
    count = max(chunks, heads_size, 3)
    return pl.pallas_call(
        functools.partial(fused_kernel, ctx_size, heads_size),
        out_shape=jax.ShapeDtypeStruct((rows, cols), bf16),
        in_specs=[pl.BlockSpec(memory_space=pltpu.HBM)] * 6,
        out_specs=pl.BlockSpec(memory_space=pltpu.VMEM),
        scratch_shapes=[
            pltpu.VMEM((4, rows, cols), bf16),
            pltpu.VMEM((4, rows, cols), bf16),
            pltpu.VMEM((rows, cols), bf16),
            pltpu.VMEM((2, rows, cols), bf16),
            pltpu.VMEM((2, cols, rows), bf16),
            pltpu.VMEM((2, chunks, CHUNK_HEADS, rows), f32),
            pltpu.VMEM((2, cols, rows), bf16),
            pltpu.VMEM((2, chunks, CHUNK_HEADS, rows), f32),
            pltpu.VMEM((cols, rows), f32),
            pltpu.VMEM((chunks, CHUNK_HEADS, rows), f32),
            pltpu.VMEM((rows, cols), bf16),
            pltpu.VMEM(hyena_inputs.shape, bf16),
            pltpu.VMEM((2, RIM, cols), bf16),
            pltpu.VMEM((RIM + rows, CHUNK_HEADS * DH), f32),
            pltpu.VMEM((rows, cols), f32),
            pltpu.VMEM((heads_size, 8, rows), f32),
            pltpu.VMEM(hyena_filter.shape, f32),
            pltpu.VMEM((1, cols), f32),
            pltpu.SemaphoreType.DMA((14, count)),
            pltpu.SemaphoreType.DMA((14, count)),
            pltpu.SemaphoreType.DMA((6,)),
        ],
        compiler_params=pltpu.CompilerParams(
            collective_id=0, has_side_effects=True, vmem_limit_bytes=52 * 1024 * 1024
        ),
    )(queries, keys, values, hyena_inputs, hyena_filter, norm_gain[None, :])


def on_device(queries, keys, values, hyena_inputs, hyena_filter, norm_gain):
    if lax.axis_size("ctx") == 2 * 4:
        return four_places(queries, keys, values, hyena_inputs, hyena_filter, norm_gain)
    row_count, col_count = queries.shape
    rim_rows = hyena_filter.shape[0] - 1
    tail_rows = hyena_inputs[1:, row_count - rim_rows :, :]
    earlier = from_behind(tail_rows, "ctx", 1)
    joined = jnp.concatenate([earlier, hyena_inputs[1:]], axis=1)
    product = joined[0].astype(jnp.float32) * joined[1].astype(jnp.float32)
    convolved = jnp.zeros((row_count, col_count), jnp.float32)
    for filter_tap in range(rim_rows + 1):
        convolved = (
            convolved
            + hyena_filter[filter_tap][None, :]
            * product[rim_rows - filter_tap : rim_rows - filter_tap + row_count]
        )
    hyena_out = hyena_inputs[0].astype(jnp.float32) * convolved
    attention = cycle_attention(queries, keys, values)
    attention_wide = lax.optimization_barrier(attention).astype(jnp.float32)
    local_squares = jnp.sum(attention_wide * attention_wide, axis=1)
    square_total = lax.psum(local_squares, "heads")
    square_mean = square_total / WIDTH
    normed = attention_wide * lax.rsqrt(square_mean + 1e-06)[:, None] * norm_gain[None, :]
    return (normed + hyena_out).astype(jnp.bfloat16)


def solution(mesh):
    placed = (
        P("ctx", "heads"),
        P("ctx", "heads"),
        P("ctx", "heads"),
        P(None, "ctx", "heads"),
        P(None, "heads"),
        P("heads"),
    )
    return jax.shard_map(
        on_device, mesh=mesh, in_specs=placed, out_specs=P("ctx", "heads"), check_vma=False
    )
```

```python
import functools
import math

import jax
import jax.numpy as jnp
from jax import lax
from jax.experimental import pallas as pl
from jax.experimental.pallas import tpu as pltpu
from jax.sharding import PartitionSpec as P

DH = 128
WIDTH = 8192
MESH = pl.DeviceIdType.MESH
LOG2E = 1.4426950408889634
CHUNK_HEADS = 1
LAG = 6
OWN_LATE = 4
RIM = 16
K_UP, V_UP, K_SIDE, V_SIDE, Q_NEAR, Q_FAR, O_NEAR, O_FAR, S_NEAR, S_FAR, SINGLES, SQUARES = range(12)
K_SIB, V_SIB = 12, 13


def from_behind(array, axis, by):
    size = lax.axis_size(axis)
    pairs = [(i, i + by) for i in range(size) if 0 <= i + by < size]
    return lax.ppermute(array, axis, pairs)


def attend(half_state, query_block, query_place, key_block, value_block, key_place):
    numerator, maxima, totals = half_state
    score_scale = 1.0 / math.sqrt(query_block.shape[2])
    scores = (
        jnp.einsum("qhd,khd->qhk", query_block, key_block, preferred_element_type=jnp.float32)
        * score_scale
    )
    visible = key_place[None, None, :] <= query_place[:, None, None]
    scores = jnp.where(visible, scores, -1e30)
    row_top = jnp.maximum(maxima, jnp.max(scores, axis=2))
    rescale = jnp.exp(maxima - row_top)
    weights = jnp.where(visible, jnp.exp(scores - row_top[:, :, None]), 0.0)
    totals = totals * rescale + jnp.sum(weights, axis=2)
    summed = jnp.einsum(
        "qhk,khd->qhd",
        weights.astype(jnp.bfloat16),
        value_block,
        preferred_element_type=jnp.float32,
    )
    numerator = numerator * rescale[:, :, None] + summed
    return (numerator, row_top, totals)


def fresh_state(row_total, head_total, head_size):
    return (
        jnp.zeros((row_total, head_total, head_size), jnp.float32),
        jnp.full((row_total, head_total), -1e30, jnp.float32),
        jnp.zeros((row_total, head_total), jnp.float32),
    )


def cycle_attention(queries, keys, values):
    row_count, col_count = queries.shape
    head_count = col_count // DH
    half_rows = row_count // 2
    ctx_index = lax.axis_index("ctx")
    query_starts = (ctx_index * row_count, ctx_index * row_count + half_rows)
    query_heads = queries.reshape(row_count, head_count, DH)
    query_halves = (query_heads[:half_rows], query_heads[half_rows:])
    query_places = tuple(
        (query_starts[number] + jnp.arange(half_rows, dtype=jnp.int32) for number in range(2))
    )
    empty_state = fresh_state(half_rows, head_count, DH)
    key_rows = lax.all_gather(keys, "ctx", axis=0, tiled=True)
    value_rows = lax.all_gather(values, "ctx", axis=0, tiled=True)
    count = key_rows.shape[0]
    block_rows = math.gcd(count, half_rows)
    key_heads = key_rows.reshape(count, head_count, DH)
    value_heads = value_rows.reshape(count, head_count, DH)

    def inner(block_index, state):
        first = block_index * block_rows
        key_block = lax.dynamic_slice_in_dim(key_heads, first, block_rows, 0)
        value_block = lax.dynamic_slice_in_dim(value_heads, first, block_rows, 0)
        key_place = first + jnp.arange(block_rows, dtype=jnp.int32)
        updated = []
        for number in range(2):
            query_block = query_halves[number]
            query_place = query_places[number]

            def update(half_state):
                return attend(
                    half_state, query_block, query_place, key_block, value_block, key_place
                )

            needed = key_place[0] <= query_place[half_rows - 1]
            updated.append(lax.cond(needed, update, lambda half_state: half_state, state[number]))
        return tuple(updated)

    finished = lax.fori_loop(0, count // block_rows, inner, (empty_state, empty_state))
    halves_out = [finished[number][0] / finished[number][2][:, :, None] for number in range(2)]
    return jnp.concatenate(halves_out, axis=0).reshape(row_count, col_count).astype(jnp.bfloat16)


def fused_kernel(
    ctx_size, heads_size,
    q_any, k_any, v_any, hy_any, filt_any, gain_any, out,
    k_all, v_all, q_own, q_far, o_got, s_got, o_put, s_put, o_home, s_home,
    att, hy, halo, prod, hyena, squares, filt, gain,
    send_sem, recv_sem, local_sem,
):
    rows, cols = out.shape
    chunks = cols // DH // CHUNK_HEADS
    wide = CHUNK_HEADS * DH
    ctx = lax.axis_index("ctx")
    mine = lax.axis_index("heads")
    core = lax.rem(ctx, 2)
    place = ctx // 2
    side = ctx + 1 - 2 * core
    factor = LOG2E / math.sqrt(DH)

    local = [
        pltpu.make_async_copy(hy_any, hy, local_sem.at[0]),
        pltpu.make_async_copy(filt_any, filt, local_sem.at[1]),
        pltpu.make_async_copy(k_any, k_all.at[2 + core], local_sem.at[2]),
        pltpu.make_async_copy(v_any, v_all.at[2 + core], local_sem.at[3]),
        pltpu.make_async_copy(q_any, q_own, local_sem.at[4]),
        pltpu.make_async_copy(gain_any, gain, local_sem.at[5]),
    ]
    for copy in local[2:5] + local[:2] + local[5:]:
        copy.start()
    barrier = pltpu.get_barrier_semaphore()
    for step in range(1, ctx_size):
        pl.semaphore_signal(
            barrier, inc=1, device_id={"ctx": lax.rem(ctx + step, ctx_size)}, device_id_type=MESH
        )
    for step in range(1, heads_size):
        pl.semaphore_signal(
            barrier, inc=1, device_id={"heads": lax.rem(mine + step, heads_size)}, device_id_type=MESH
        )
    pl.semaphore_wait(barrier, ctx_size + heads_size - 2)
    for copy in local[2:5]:
        copy.wait()

    def remote(src, dst, kind, at, target):
        return pltpu.make_async_remote_copy(
            src_ref=src, dst_ref=dst, send_sem=send_sem.at[kind, at], recv_sem=recv_sem.at[kind, at],
            device_id={"ctx": target}, device_id_type=MESH,
        )

    def arrived(dst, kind, at):
        remote(dst, dst, kind, at, side).wait_recv()

    def sent(src, kind, at):
        remote(src, src, kind, at, side).wait_send()

    def lanes(chunk):
        return pl.ds(pl.multiple_of(chunk * wide, wide), wide)

    def head_lanes(head):
        return pl.ds(pl.multiple_of(head * DH, DH), DH)

    def each_chunk(body):
        def step(chunk, carry):
            body(chunk)
            return carry

        lax.fori_loop(0, chunks, step, 0)

    tail = hy_any.at[pl.ds(1, 2), pl.ds(rows - RIM, RIM), :]

    def send_tail():
        remote(tail, halo, SINGLES, 2, ctx + 1).start()

    def up_copies(chunk):
        at = lanes(chunk)
        return (
            remote(k_all.at[2 + core, :, at], k_all.at[core, :, at], K_UP, chunk, ctx + 2),
            remote(v_all.at[2 + core, :, at], v_all.at[core, :, at], V_UP, chunk, ctx + 2),
        )

    def near_copies(chunk):
        at = lanes(chunk)
        return (remote(q_own.at[:, at], q_far.at[0, :, at], Q_NEAR, chunk, ctx - 2),)

    def far_copies(chunk):
        at = lanes(chunk)
        return (remote(q_own.at[:, at], q_far.at[1, :, at], Q_FAR, chunk, ctx - 4),) + near_copies(chunk)

    def sibling_copies(chunk):
        at = lanes(chunk)
        return (
            remote(k_all.at[2 + core, :, at], k_all.at[2 + core, :, at], K_SIB, chunk, side),
            remote(v_all.at[2 + core, :, at], v_all.at[2 + core, :, at], V_SIB, chunk, side),
        )

    def sibling_arrived(chunk):
        arrived(k_all.at[3 - core, :, lanes(chunk)], K_SIB, chunk)
        arrived(v_all.at[3 - core, :, lanes(chunk)], V_SIB, chunk)

    @each_chunk
    def _(chunk):
        def begin(copies):
            for copy in copies(chunk):
                copy.start()

        pl.when(place == 0)(lambda: begin(up_copies))
        pl.when(place == 2)(lambda: begin(near_copies))
        pl.when(place == 3)(lambda: begin(far_copies))
        begin(sibling_copies)
        pl.when((ctx < ctx_size - 1) & (ctx != 1) & (chunk == 1))(send_tail)

    def gate(count, rim):
        @each_chunk
        def _(chunk):
            at = lanes(chunk)
            part = pl.ds(0, count)
            if rim:
                prod[:RIM] = halo[0, :, at].astype(jnp.float32) * halo[1, :, at].astype(jnp.float32)
            else:
                prod[:RIM] = jnp.zeros((RIM, wide), jnp.float32)
            prod[RIM : RIM + count] = hy[1, part, at].astype(jnp.float32) * hy[2, part, at].astype(jnp.float32)
            taps = filt[:, at]
            summed = taps[0:1] * prod[RIM : RIM + count]
            for tap in range(1, filt.shape[0]):
                summed = summed + taps[tap : tap + 1] * prod[RIM - tap : RIM - tap + count]
            hyena[part, at] = hy[0, part, at].astype(jnp.float32) * summed

    def redo_rim():
        arrived(halo, SINGLES, 2)
        gate(RIM, True)

    for copy in local[:2]:
        copy.wait()
    gate(rows, False)

    local[5].wait()
    squares[mine] = jnp.zeros_like(squares[mine])

    key_place = lax.broadcasted_iota(jnp.int32, (rows, rows), 0)
    query_place = lax.broadcasted_iota(jnp.int32, (rows, rows), 1) + core * rows

    def scores(slot, head, query):
        return lax.dot_general(
            k_all[slot, :, head_lanes(head)], query, (((1,), (1,)), ((), ())),
            preferred_element_type=jnp.float32,
        )

    def turned(slot, head):
        return v_all[slot, :, head_lanes(head)].T

    def masked_scores(head, query, slots, masked):
        tiles = [scores(slot, head, query) for slot in slots]
        if masked:
            tiles = [
                jnp.where(key_place + (slot - 2) * rows <= query_place, tile, -1e30) if slot >= 2 else tile
                for slot, tile in zip(slots, tiles)
            ]
        return tiles, functools.reduce(jnp.maximum, [jnp.max(tile, axis=0, keepdims=True) for tile in tiles])

    def weigh(tiles, top, turned_values):
        total, numerator = 0.0, 0.0
        for tile, value in zip(tiles, turned_values):
            weights = jnp.exp2((tile - top) * factor)
            total = total + jnp.sum(weights, axis=0, keepdims=True)
            numerator = numerator + jnp.dot(
                value, weights.astype(jnp.bfloat16), preferred_element_type=jnp.float32
            )
        return numerator / total, top * factor + jnp.log(total) * LOG2E

    def attend_some(head, query, slots, turned_values, masked):
        return weigh(*masked_scores(head, query, slots, masked), turned_values)

    def finish(head, value):
        rounded = value.astype(jnp.bfloat16).astype(jnp.float32)
        squares[mine] += jnp.sum((rounded * rounded).reshape(DH // 8, 8, rows), axis=0)
        att[:, head_lanes(head)] = rounded.T.astype(jnp.bfloat16)

    def head_rows(head):
        return pl.ds(pl.multiple_of(head * DH, DH), DH)

    def chunk_rows(chunk):
        return pl.ds(pl.multiple_of(chunk * wide, wide), wide)

    def partial_out(slot, chunk, index, head, result):
        value, log_total = result
        o_put[slot, head_rows(head), :] = value.astype(jnp.bfloat16)
        s_put[slot, chunk, index : index + 1, :] = log_total

    def send_out(slot, chunk, to_slot, target):
        at = chunk_rows(chunk)
        remote(o_put.at[slot, at], o_got.at[to_slot, at], O_NEAR + to_slot, chunk, target).start()
        remote(s_put.at[slot, chunk], s_got.at[to_slot, chunk], S_NEAR + to_slot, chunk, target).start()

    def merge(slots, chunk):
        for slot in slots:
            arrived(o_got.at[slot, chunk_rows(chunk)], O_NEAR + slot, chunk)
            arrived(s_got.at[slot, chunk], S_NEAR + slot, chunk)
        for index in range(CHUNK_HEADS):
            head = chunk * CHUNK_HEADS + index
            logs = [s_home[chunk, index : index + 1, :]]
            parts = [o_home[head_rows(head), :]]
            for slot in slots:
                logs.append(s_got[slot, chunk, index : index + 1, :])
                parts.append(o_got[slot, head_rows(head), :].astype(jnp.float32))
            top = functools.reduce(jnp.maximum, logs)
            shares = [jnp.exp2(log - top) for log in logs]
            inverse = 1.0 / sum(shares)
            finish(head, sum(part * (share * inverse) for part, share in zip(parts, shares)))

    def merge_behind(slots, chunk):
        pl.when(chunk >= LAG)(lambda: merge(slots, chunk - LAG))

    def merge_rest(slots):
        def step(chunk, carry):
            merge(slots, chunk)
            return carry

        lax.fori_loop(max(chunks - LAG, 0), chunks, step, 0)

    def own_query(head):
        return q_own[:, head_lanes(head)]

    @pl.when(place == 0)
    def _():
        @each_chunk
        def _(chunk):
            sibling_arrived(chunk)
            for index in range(CHUNK_HEADS):
                head = chunk * CHUNK_HEADS + index
                values = [turned(slot, head) for slot in (2, 3)]
                finish(head, attend_some(head, own_query(head), (2, 3), values, True)[0])

        pl.when(core == 1)(send_tail)
        pl.when(core == 1)(redo_rim)

    @pl.when(place == 1)
    def _():
        def forward(chunk):
            at = lanes(chunk)
            arrived(k_all.at[core, :, at], K_UP, chunk)
            remote(k_all.at[core, :, at], k_all.at[core, :, at], K_SIDE, chunk, side).start()
            arrived(v_all.at[core, :, at], V_UP, chunk)
            remote(v_all.at[core, :, at], v_all.at[core, :, at], V_SIDE, chunk, side).start()

        slots = (0, 1, 2, 3)

        def own(chunk):
            for index in range(CHUNK_HEADS):
                head = chunk * CHUNK_HEADS + index
                values = [turned(slot, head) for slot in slots]
                finish(head, attend_some(head, own_query(head), slots, values, True)[0])

        forward(0)

        @each_chunk
        def _(chunk):
            at = lanes(chunk)
            sibling_arrived(chunk)
            arrived(q_far.at[1, :, at], Q_FAR, chunk)
            arrived(q_far.at[0, :, at], Q_NEAR, chunk)
            arrived(k_all.at[1 - core, :, at], K_SIDE, chunk)
            arrived(v_all.at[1 - core, :, at], V_SIDE, chunk)
            heads = [chunk * CHUNK_HEADS + index for index in range(CHUNK_HEADS)]
            values = [[turned(slot, head) for slot in slots] for head in heads]
            works = [(far, index) for far in (1, 0) for index in range(CHUNK_HEADS)]

            def begin_work(far, index):
                return masked_scores(heads[index], q_far[far, :, head_lanes(heads[index])], slots, False)

            ready = begin_work(*works[0])
            for number, (far, index) in enumerate(works):
                current = ready
                if number + 1 < len(works):
                    ready = begin_work(*works[number + 1])
                partial_out(far, chunk, index, heads[index], weigh(*current, values[index]))
                if index == CHUNK_HEADS - 1:
                    send_out(far, chunk, far, ctx + 2 + 2 * far)
            pl.when(chunk + 1 < chunks)(lambda: forward(chunk + 1))
            pl.when(chunk < chunks - OWN_LATE)(lambda: own(chunk))

        def late(chunk, carry):
            own(chunk)
            return carry

        lax.fori_loop(max(chunks - OWN_LATE, 0), chunks, late, 0)
        redo_rim()

    @pl.when(place == 2)
    def _():
        @each_chunk
        def _(chunk):
            sibling_arrived(chunk)
            arrived(q_far.at[0, :, lanes(chunk)], Q_NEAR, chunk)
            for index in range(CHUNK_HEADS):
                head = chunk * CHUNK_HEADS + index
                values = [turned(slot, head) for slot in (2, 3)]
                query = q_far[0, :, head_lanes(head)]
                partial_out(0, chunk, index, head, attend_some(head, query, (2, 3), values, False))
                value, log_total = attend_some(head, own_query(head), (2, 3), values, True)
                o_home[head_rows(head), :] = value
                s_home[chunk, index : index + 1, :] = log_total
            send_out(0, chunk, 0, ctx + 2)
            merge_behind((0,), chunk)

        redo_rim()
        merge_rest((0,))

    @pl.when(place == 3)
    def _():
        @each_chunk
        def _(chunk):
            sibling_arrived(chunk)
            for index in range(CHUNK_HEADS):
                head = chunk * CHUNK_HEADS + index
                values = [turned(slot, head) for slot in (2, 3)]
                value, log_total = attend_some(head, own_query(head), (2, 3), values, True)
                o_home[head_rows(head), :] = value
                s_home[chunk, index : index + 1, :] = log_total
            merge_behind((0, 1), chunk)

        redo_rim()
        merge_rest((0, 1))

    def square_copy(step, slot):
        return pltpu.make_async_remote_copy(
            src_ref=squares.at[slot], dst_ref=squares.at[slot],
            send_sem=send_sem.at[SQUARES, step], recv_sem=recv_sem.at[SQUARES, slot],
            device_id={"heads": lax.rem(mine + step, heads_size)}, device_id_type=MESH,
        )

    for step in range(1, heads_size):
        square_copy(step, mine).start()
    for step in range(1, heads_size):
        square_copy(step, lax.rem(mine + step, heads_size)).wait_recv()
    square_total = squares[0]
    for slot in range(1, heads_size):
        square_total = square_total + squares[slot]
    square_mean = jnp.sum(square_total, axis=0, keepdims=True) / (cols * heads_size)
    scale = jnp.broadcast_to(lax.rsqrt(square_mean + 1e-06), (DH, rows)).T

    def last(head, carry):
        at = head_lanes(head)
        out[:, at] = (att[:, at].astype(jnp.float32) * scale * gain[:, at] + hyena[:, at]).astype(jnp.bfloat16)
        return carry

    lax.fori_loop(0, cols // DH, last, 0)

    for step in range(1, heads_size):
        square_copy(step, mine).wait_send()

    @pl.when(ctx < ctx_size - 1)
    def _():
        sent(tail, SINGLES, 2)

    def sent_lanes(kinds):
        @each_chunk
        def _(chunk):
            for kind in kinds:
                sent(q_any.at[:, lanes(chunk)], kind, chunk)

    def sent_out(slots):
        @each_chunk
        def _(chunk):
            for slot in slots:
                sent(o_put.at[slot, chunk_rows(chunk)], O_NEAR + slot, chunk)
                sent(s_put.at[slot, chunk], S_NEAR + slot, chunk)

    sent_lanes((K_SIB, V_SIB))
    pl.when(place == 0)(lambda: sent_lanes((K_UP, V_UP)))
    pl.when(place == 2)(lambda: sent_lanes((Q_NEAR,)))
    pl.when(place == 3)(lambda: sent_lanes((Q_NEAR, Q_FAR)))
    pl.when(place == 2)(lambda: sent_out((0,)))

    @pl.when(place == 1)
    def _():
        sent_out((0, 1))
        sent_lanes((K_SIDE, V_SIDE))


def four_places(queries, keys, values, hyena_inputs, hyena_filter, norm_gain):
    rows, cols = queries.shape
    ctx_size, heads_size = lax.axis_size("ctx"), lax.axis_size("heads")
    chunks = cols // DH // CHUNK_HEADS
    bf16, f32 = jnp.bfloat16, jnp.float32
    count = max(chunks, heads_size, 3)
    return pl.pallas_call(
        functools.partial(fused_kernel, ctx_size, heads_size),
        out_shape=jax.ShapeDtypeStruct((rows, cols), bf16),
        in_specs=[pl.BlockSpec(memory_space=pltpu.HBM)] * 6,
        out_specs=pl.BlockSpec(memory_space=pltpu.VMEM),
        scratch_shapes=[
            pltpu.VMEM((4, rows, cols), bf16),
            pltpu.VMEM((4, rows, cols), bf16),
            pltpu.VMEM((rows, cols), bf16),
            pltpu.VMEM((2, rows, cols), bf16),
            pltpu.VMEM((2, cols, rows), bf16),
            pltpu.VMEM((2, chunks, CHUNK_HEADS, rows), f32),
            pltpu.VMEM((2, cols, rows), bf16),
            pltpu.VMEM((2, chunks, CHUNK_HEADS, rows), f32),
            pltpu.VMEM((cols, rows), f32),
            pltpu.VMEM((chunks, CHUNK_HEADS, rows), f32),
            pltpu.VMEM((rows, cols), bf16),
            pltpu.VMEM(hyena_inputs.shape, bf16),
            pltpu.VMEM((2, RIM, cols), bf16),
            pltpu.VMEM((RIM + rows, CHUNK_HEADS * DH), f32),
            pltpu.VMEM((rows, cols), f32),
            pltpu.VMEM((heads_size, 8, rows), f32),
            pltpu.VMEM(hyena_filter.shape, f32),
            pltpu.VMEM((1, cols), f32),
            pltpu.SemaphoreType.DMA((14, count)),
            pltpu.SemaphoreType.DMA((14, count)),
            pltpu.SemaphoreType.DMA((6,)),
        ],
        compiler_params=pltpu.CompilerParams(
            collective_id=0, has_side_effects=True, vmem_limit_bytes=52 * 1024 * 1024
        ),
    )(queries, keys, values, hyena_inputs, hyena_filter, norm_gain[None, :])


def on_device(queries, keys, values, hyena_inputs, hyena_filter, norm_gain):
    if lax.axis_size("ctx") == 2 * 4:
        return four_places(queries, keys, values, hyena_inputs, hyena_filter, norm_gain)
    row_count, col_count = queries.shape
    rim_rows = hyena_filter.shape[0] - 1
    tail_rows = hyena_inputs[1:, row_count - rim_rows :, :]
    earlier = from_behind(tail_rows, "ctx", 1)
    joined = jnp.concatenate([earlier, hyena_inputs[1:]], axis=1)
    product = joined[0].astype(jnp.float32) * joined[1].astype(jnp.float32)
    convolved = jnp.zeros((row_count, col_count), jnp.float32)
    for filter_tap in range(rim_rows + 1):
        convolved = (
            convolved
            + hyena_filter[filter_tap][None, :]
            * product[rim_rows - filter_tap : rim_rows - filter_tap + row_count]
        )
    hyena_out = hyena_inputs[0].astype(jnp.float32) * convolved
    attention = cycle_attention(queries, keys, values)
    attention_wide = lax.optimization_barrier(attention).astype(jnp.float32)
    local_squares = jnp.sum(attention_wide * attention_wide, axis=1)
    square_total = lax.psum(local_squares, "heads")
    square_mean = square_total / WIDTH
    normed = attention_wide * lax.rsqrt(square_mean + 1e-06)[:, None] * norm_gain[None, :]
    return (normed + hyena_out).astype(jnp.bfloat16)


def solution(mesh):
    placed = (
        P("ctx", "heads"),
        P("ctx", "heads"),
        P("ctx", "heads"),
        P(None, "ctx", "heads"),
        P(None, "heads"),
        P("heads"),
    )
    return jax.shard_map(
        on_device, mesh=mesh, in_specs=placed, out_specs=P("ctx", "heads"), check_vma=False
    )
```

```python
import functools
import math

import jax
import jax.numpy as jnp
from jax import lax
from jax.experimental import pallas as pl
from jax.experimental.pallas import tpu as pltpu
from jax.sharding import PartitionSpec as P

DH = 128
WIDTH = 8192
MESH = pl.DeviceIdType.MESH
LOG2E = 1.4426950408889634
CHUNK_HEADS = 1
DEPTH = 16
LAG = 8
GROUP = 4
RIM = 16
K_UP, V_UP, K_SIDE, V_SIDE, Q_NEAR, Q_FAR, O_NEAR, O_FAR, S_NEAR, S_FAR, SINGLES, SQUARES = range(12)


def from_behind(array, axis, by):
    size = lax.axis_size(axis)
    pairs = [(i, i + by) for i in range(size) if 0 <= i + by < size]
    return lax.ppermute(array, axis, pairs)


def attend(half_state, query_block, query_place, key_block, value_block, key_place):
    numerator, maxima, totals = half_state
    score_scale = 1.0 / math.sqrt(query_block.shape[2])
    scores = (
        jnp.einsum("qhd,khd->qhk", query_block, key_block, preferred_element_type=jnp.float32)
        * score_scale
    )
    visible = key_place[None, None, :] <= query_place[:, None, None]
    scores = jnp.where(visible, scores, -1e30)
    row_top = jnp.maximum(maxima, jnp.max(scores, axis=2))
    rescale = jnp.exp(maxima - row_top)
    weights = jnp.where(visible, jnp.exp(scores - row_top[:, :, None]), 0.0)
    totals = totals * rescale + jnp.sum(weights, axis=2)
    summed = jnp.einsum(
        "qhk,khd->qhd",
        weights.astype(jnp.bfloat16),
        value_block,
        preferred_element_type=jnp.float32,
    )
    numerator = numerator * rescale[:, :, None] + summed
    return (numerator, row_top, totals)


def fresh_state(row_total, head_total, head_size):
    return (
        jnp.zeros((row_total, head_total, head_size), jnp.float32),
        jnp.full((row_total, head_total), -1e30, jnp.float32),
        jnp.zeros((row_total, head_total), jnp.float32),
    )


def cycle_attention(queries, keys, values):
    row_count, col_count = queries.shape
    head_count = col_count // DH
    half_rows = row_count // 2
    ctx_index = lax.axis_index("ctx")
    query_starts = (ctx_index * row_count, ctx_index * row_count + half_rows)
    query_heads = queries.reshape(row_count, head_count, DH)
    query_halves = (query_heads[:half_rows], query_heads[half_rows:])
    query_places = tuple(
        (query_starts[number] + jnp.arange(half_rows, dtype=jnp.int32) for number in range(2))
    )
    empty_state = fresh_state(half_rows, head_count, DH)
    key_rows = lax.all_gather(keys, "ctx", axis=0, tiled=True)
    value_rows = lax.all_gather(values, "ctx", axis=0, tiled=True)
    count = key_rows.shape[0]
    block_rows = math.gcd(count, half_rows)
    key_heads = key_rows.reshape(count, head_count, DH)
    value_heads = value_rows.reshape(count, head_count, DH)

    def inner(block_index, state):
        first = block_index * block_rows
        key_block = lax.dynamic_slice_in_dim(key_heads, first, block_rows, 0)
        value_block = lax.dynamic_slice_in_dim(value_heads, first, block_rows, 0)
        key_place = first + jnp.arange(block_rows, dtype=jnp.int32)
        updated = []
        for number in range(2):
            query_block = query_halves[number]
            query_place = query_places[number]

            def update(half_state):
                return attend(
                    half_state, query_block, query_place, key_block, value_block, key_place
                )

            needed = key_place[0] <= query_place[half_rows - 1]
            updated.append(lax.cond(needed, update, lambda half_state: half_state, state[number]))
        return tuple(updated)

    finished = lax.fori_loop(0, count // block_rows, inner, (empty_state, empty_state))
    halves_out = [finished[number][0] / finished[number][2][:, :, None] for number in range(2)]
    return jnp.concatenate(halves_out, axis=0).reshape(row_count, col_count).astype(jnp.bfloat16)


def fused_kernel(
    ctx_size, heads_size,
    q_any, k_any, v_any, hy_any, filt_any, gain_any, out,
    k_all, v_all, q_own, q_far, o_got, s_got, o_put, s_put, o_home, s_home,
    att, hy, halo, prod, hyena, squares, filt, gain,
    send_sem, recv_sem, local_sem,
):
    rows, cols = out.shape
    chunks = cols // DH // CHUNK_HEADS
    wide = CHUNK_HEADS * DH
    ctx = lax.axis_index("ctx")
    mine = lax.axis_index("heads")
    core = lax.rem(ctx, 2)
    place = ctx // 2
    side = ctx + 1 - 2 * core
    factor = LOG2E / math.sqrt(DH)

    local = [
        pltpu.make_async_copy(hy_any, hy, local_sem.at[0]),
        pltpu.make_async_copy(filt_any, filt, local_sem.at[1]),
        pltpu.make_async_copy(k_any, k_all.at[2 + core], local_sem.at[2]),
        pltpu.make_async_copy(v_any, v_all.at[2 + core], local_sem.at[3]),
        pltpu.make_async_copy(q_any, q_own, local_sem.at[4]),
        pltpu.make_async_copy(gain_any, gain, local_sem.at[5]),
    ]
    for copy in local[2:5] + local[:2] + local[5:]:
        copy.start()
    barrier = pltpu.get_barrier_semaphore()
    for step in range(1, ctx_size):
        pl.semaphore_signal(
            barrier, inc=1, device_id={"ctx": lax.rem(ctx + step, ctx_size)}, device_id_type=MESH
        )
    for step in range(1, heads_size):
        pl.semaphore_signal(
            barrier, inc=1, device_id={"heads": lax.rem(mine + step, heads_size)}, device_id_type=MESH
        )
    pl.semaphore_wait(barrier, ctx_size + heads_size - 2)
    for copy in local[2:5]:
        copy.wait()

    def remote(src, dst, kind, at, target):
        return pltpu.make_async_remote_copy(
            src_ref=src, dst_ref=dst, send_sem=send_sem.at[kind, at], recv_sem=recv_sem.at[kind, at],
            device_id={"ctx": target}, device_id_type=MESH,
        )

    def arrived(dst, kind, at):
        remote(dst, dst, kind, at, side).wait_recv()

    def sent(src, kind, at):
        remote(src, src, kind, at, side).wait_send()

    def lanes(chunk):
        return pl.ds(pl.multiple_of(chunk * wide, wide), wide)

    def head_lanes(head):
        return pl.ds(pl.multiple_of(head * DH, DH), DH)

    def each_chunk(body):
        def step(chunk, carry):
            body(chunk)
            return carry

        lax.fori_loop(0, chunks, step, 0)

    tail = hy_any.at[pl.ds(1, 2), pl.ds(rows - RIM, RIM), :]

    def send_tail():
        remote(tail, halo, SINGLES, 2, ctx + 1).start()

    pl.when((ctx < ctx_size - 1) & (ctx != 1))(send_tail)
    remote(k_any, k_all.at[2 + core], SINGLES, 0, side).start()
    remote(v_any, v_all.at[2 + core], SINGLES, 1, side).start()

    def up_copies(chunk):
        at = lanes(chunk)
        return (
            remote(k_all.at[2 + core, :, at], k_all.at[core, :, at], K_UP, chunk, ctx + 2),
            remote(v_all.at[2 + core, :, at], v_all.at[core, :, at], V_UP, chunk, ctx + 2),
        )

    def near_copies(chunk):
        at = lanes(chunk)
        return (remote(q_own.at[:, at], q_far.at[0, :, at], Q_NEAR, chunk, ctx - 2),)

    def far_copies(chunk):
        at = lanes(chunk)
        return (remote(q_own.at[:, at], q_far.at[1, :, at], Q_FAR, chunk, ctx - 4),) + near_copies(chunk)

    def begin(copies, depth):
        def step(chunk, carry):
            for copy in copies(chunk):
                copy.start()
            return carry

        lax.fori_loop(0, min(depth, chunks), step, 0)

    def follow(copies, depth, chunk):
        for copy in copies(chunk):
            copy.wait_send()

        @pl.when(chunk + depth < chunks)
        def _():
            for copy in copies(chunk + depth):
                copy.start()

    pl.when(place == 0)(lambda: begin(up_copies, DEPTH))
    pl.when(place == 2)(lambda: begin(near_copies, DEPTH))
    pl.when(place == 3)(lambda: begin(far_copies, DEPTH))

    def gate(count, rim):
        @each_chunk
        def _(chunk):
            at = lanes(chunk)
            part = pl.ds(0, count)
            if rim:
                prod[:RIM] = halo[0, :, at].astype(jnp.float32) * halo[1, :, at].astype(jnp.float32)
            else:
                prod[:RIM] = jnp.zeros((RIM, wide), jnp.float32)
            prod[RIM : RIM + count] = hy[1, part, at].astype(jnp.float32) * hy[2, part, at].astype(jnp.float32)
            taps = filt[:, at]
            summed = taps[0:1] * prod[RIM : RIM + count]
            for tap in range(1, filt.shape[0]):
                summed = summed + taps[tap : tap + 1] * prod[RIM - tap : RIM - tap + count]
            hyena[part, at] = hy[0, part, at].astype(jnp.float32) * summed

    def redo_rim():
        arrived(halo, SINGLES, 2)
        gate(RIM, True)

    for copy in local[:2]:
        copy.wait()
    gate(rows, False)
    pl.when(place >= 2)(redo_rim)

    local[5].wait()
    arrived(k_all.at[2], SINGLES, 0)
    arrived(v_all.at[2], SINGLES, 1)
    squares[mine] = jnp.zeros_like(squares[mine])

    key_place = lax.broadcasted_iota(jnp.int32, (rows, rows), 0)
    query_place = lax.broadcasted_iota(jnp.int32, (rows, rows), 1) + core * rows

    def scores(slot, head, query):
        return lax.dot_general(
            k_all[slot, :, head_lanes(head)], query, (((1,), (1,)), ((), ())),
            preferred_element_type=jnp.float32,
        )

    def turned(slot, head):
        return v_all[slot, :, head_lanes(head)].T

    def masked_scores(head, query, slots, masked):
        tiles = [scores(slot, head, query) for slot in slots]
        if masked:
            tiles = [
                jnp.where(key_place + (slot - 2) * rows <= query_place, tile, -1e30) if slot >= 2 else tile
                for slot, tile in zip(slots, tiles)
            ]
        return tiles, functools.reduce(jnp.maximum, [jnp.max(tile, axis=0, keepdims=True) for tile in tiles])

    def weigh(tiles, top, turned_values):
        total, numerator = 0.0, 0.0
        for tile, value in zip(tiles, turned_values):
            weights = jnp.exp2((tile - top) * factor)
            total = total + jnp.sum(weights, axis=0, keepdims=True)
            numerator = numerator + jnp.dot(
                value, weights.astype(jnp.bfloat16), preferred_element_type=jnp.float32
            )
        return numerator / total, top * factor + jnp.log(total) * LOG2E

    def attend_some(head, query, slots, turned_values, masked):
        return weigh(*masked_scores(head, query, slots, masked), turned_values)

    def finish(head, value):
        rounded = value.astype(jnp.bfloat16).astype(jnp.float32)
        squares[mine] += jnp.sum((rounded * rounded).reshape(DH // 8, 8, rows), axis=0)
        att[:, head_lanes(head)] = rounded.T.astype(jnp.bfloat16)

    def head_rows(head):
        return pl.ds(pl.multiple_of(head * DH, DH), DH)

    def chunk_rows(chunk):
        return pl.ds(pl.multiple_of(chunk * wide, wide), wide)

    def partial_out(slot, chunk, index, head, result):
        value, log_total = result
        o_put[slot, head_rows(head), :] = value.astype(jnp.bfloat16)
        s_put[slot, chunk, index : index + 1, :] = log_total

    def send_out(slot, chunk, to_slot, target):
        at = chunk_rows(chunk)
        remote(o_put.at[slot, at], o_got.at[to_slot, at], O_NEAR + to_slot, chunk, target).start()

        @pl.when(lax.rem(chunk, GROUP) == GROUP - 1)
        def _():
            logs = pl.ds(chunk - (GROUP - 1), GROUP)
            remote(
                s_put.at[slot, logs], s_got.at[to_slot, logs], S_NEAR + to_slot, chunk // GROUP, target
            ).start()

    def merge(slots, chunk):
        for slot in slots:
            arrived(o_got.at[slot, chunk_rows(chunk)], O_NEAR + slot, chunk)

            @pl.when(lax.rem(chunk, GROUP) == 0)
            def _():
                arrived(s_got.at[slot, pl.ds(chunk, GROUP)], S_NEAR + slot, chunk // GROUP)

        for index in range(CHUNK_HEADS):
            head = chunk * CHUNK_HEADS + index
            logs = [s_home[chunk, index : index + 1, :]]
            parts = [o_home[head_rows(head), :]]
            for slot in slots:
                logs.append(s_got[slot, chunk, index : index + 1, :])
                parts.append(o_got[slot, head_rows(head), :].astype(jnp.float32))
            top = functools.reduce(jnp.maximum, logs)
            shares = [jnp.exp2(log - top) for log in logs]
            inverse = 1.0 / sum(shares)
            finish(head, sum(part * (share * inverse) for part, share in zip(parts, shares)))

    def merge_behind(slots, chunk):
        pl.when(chunk >= LAG)(lambda: merge(slots, chunk - LAG))

    def merge_rest(slots):
        def step(chunk, carry):
            merge(slots, chunk)
            return carry

        lax.fori_loop(max(chunks - LAG, 0), chunks, step, 0)

    def own_query(head):
        return q_own[:, head_lanes(head)]

    @pl.when(place == 0)
    def _():
        @each_chunk
        def _(chunk):
            follow(up_copies, DEPTH, chunk)
            for index in range(CHUNK_HEADS):
                head = chunk * CHUNK_HEADS + index
                values = [turned(slot, head) for slot in (2, 3)]
                finish(head, attend_some(head, own_query(head), (2, 3), values, True)[0])

        pl.when(core == 1)(send_tail)
        pl.when(core == 1)(redo_rim)

    @pl.when(place == 1)
    def _():
        def forward(chunk):
            at = lanes(chunk)
            arrived(k_all.at[core, :, at], K_UP, chunk)
            remote(k_all.at[core, :, at], k_all.at[core, :, at], K_SIDE, chunk, side).start()
            arrived(v_all.at[core, :, at], V_UP, chunk)
            remote(v_all.at[core, :, at], v_all.at[core, :, at], V_SIDE, chunk, side).start()

        forward(0)

        @each_chunk
        def _(chunk):
            at = lanes(chunk)
            arrived(q_far.at[1, :, at], Q_FAR, chunk)
            arrived(q_far.at[0, :, at], Q_NEAR, chunk)
            arrived(k_all.at[1 - core, :, at], K_SIDE, chunk)
            arrived(v_all.at[1 - core, :, at], V_SIDE, chunk)
            slots = (0, 1, 2, 3)
            heads = [chunk * CHUNK_HEADS + index for index in range(CHUNK_HEADS)]
            values = [[turned(slot, head) for slot in slots] for head in heads]
            works = [(far, index) for far in (1, 0, None) for index in range(CHUNK_HEADS)]

            def begin_work(far, index):
                head = heads[index]
                query = own_query(head) if far is None else q_far[far, :, head_lanes(head)]
                return masked_scores(head, query, slots, far is None)

            ready = begin_work(*works[0])
            for number, (far, index) in enumerate(works):
                current = ready
                if number + 1 < len(works):
                    ready = begin_work(*works[number + 1])
                result = weigh(*current, values[index])
                if far is None:
                    finish(heads[index], result[0])
                    continue
                partial_out(far, chunk, index, heads[index], result)
                if index == CHUNK_HEADS - 1:
                    send_out(far, chunk, far, ctx + 2 + 2 * far)
                    if far == 0:
                        pl.when(chunk + 1 < chunks)(lambda: forward(chunk + 1))

        redo_rim()

    @pl.when(place == 2)
    def _():
        @each_chunk
        def _(chunk):
            follow(near_copies, DEPTH, chunk)
            arrived(q_far.at[0, :, lanes(chunk)], Q_NEAR, chunk)
            for index in range(CHUNK_HEADS):
                head = chunk * CHUNK_HEADS + index
                values = [turned(slot, head) for slot in (2, 3)]
                query = q_far[0, :, head_lanes(head)]
                partial_out(0, chunk, index, head, attend_some(head, query, (2, 3), values, False))
                value, log_total = attend_some(head, own_query(head), (2, 3), values, True)
                o_home[head_rows(head), :] = value
                s_home[chunk, index : index + 1, :] = log_total
            send_out(0, chunk, 0, ctx + 2)
            merge_behind((0,), chunk)

        merge_rest((0,))

    @pl.when(place == 3)
    def _():
        @each_chunk
        def _(chunk):
            follow(far_copies, DEPTH, chunk)
            for index in range(CHUNK_HEADS):
                head = chunk * CHUNK_HEADS + index
                values = [turned(slot, head) for slot in (2, 3)]
                value, log_total = attend_some(head, own_query(head), (2, 3), values, True)
                o_home[head_rows(head), :] = value
                s_home[chunk, index : index + 1, :] = log_total
            merge_behind((0, 1), chunk)

        merge_rest((0, 1))

    def square_copy(step, slot):
        return pltpu.make_async_remote_copy(
            src_ref=squares.at[slot], dst_ref=squares.at[slot],
            send_sem=send_sem.at[SQUARES, step], recv_sem=recv_sem.at[SQUARES, slot],
            device_id={"heads": lax.rem(mine + step, heads_size)}, device_id_type=MESH,
        )

    for step in range(1, heads_size):
        square_copy(step, mine).start()
    for step in range(1, heads_size):
        square_copy(step, lax.rem(mine + step, heads_size)).wait_recv()
    square_total = squares[0]
    for slot in range(1, heads_size):
        square_total = square_total + squares[slot]
    square_mean = jnp.sum(square_total, axis=0, keepdims=True) / (cols * heads_size)
    scale = jnp.broadcast_to(lax.rsqrt(square_mean + 1e-06), (DH, rows)).T

    def last(head, carry):
        at = head_lanes(head)
        out[:, at] = (att[:, at].astype(jnp.float32) * scale * gain[:, at] + hyena[:, at]).astype(jnp.bfloat16)
        return carry

    lax.fori_loop(0, cols // DH, last, 0)

    for step in range(1, heads_size):
        square_copy(step, mine).wait_send()

    @pl.when(ctx < ctx_size - 1)
    def _():
        sent(tail, SINGLES, 2)

    sent(k_any, SINGLES, 0)
    sent(v_any, SINGLES, 1)

    def sent_lanes(kinds):
        @each_chunk
        def _(chunk):
            for kind in kinds:
                sent(q_any.at[:, lanes(chunk)], kind, chunk)

    def sent_out(slots):
        @each_chunk
        def _(chunk):
            for slot in slots:
                sent(o_put.at[slot, chunk_rows(chunk)], O_NEAR + slot, chunk)

                @pl.when(lax.rem(chunk, GROUP) == 0)
                def _():
                    sent(s_put.at[slot, pl.ds(chunk, GROUP)], S_NEAR + slot, chunk // GROUP)


    pl.when(place == 2)(lambda: sent_out((0,)))

    @pl.when(place == 1)
    def _():
        sent_out((0, 1))
        sent_lanes((K_SIDE, V_SIDE))


def four_places(queries, keys, values, hyena_inputs, hyena_filter, norm_gain):
    rows, cols = queries.shape
    ctx_size, heads_size = lax.axis_size("ctx"), lax.axis_size("heads")
    chunks = cols // DH // CHUNK_HEADS
    bf16, f32 = jnp.bfloat16, jnp.float32
    count = max(chunks, heads_size, 3)
    return pl.pallas_call(
        functools.partial(fused_kernel, ctx_size, heads_size),
        out_shape=jax.ShapeDtypeStruct((rows, cols), bf16),
        in_specs=[pl.BlockSpec(memory_space=pltpu.HBM)] * 6,
        out_specs=pl.BlockSpec(memory_space=pltpu.VMEM),
        scratch_shapes=[
            pltpu.VMEM((4, rows, cols), bf16),
            pltpu.VMEM((4, rows, cols), bf16),
            pltpu.VMEM((rows, cols), bf16),
            pltpu.VMEM((2, rows, cols), bf16),
            pltpu.VMEM((2, cols, rows), bf16),
            pltpu.VMEM((2, chunks, CHUNK_HEADS, rows), f32),
            pltpu.VMEM((2, cols, rows), bf16),
            pltpu.VMEM((2, chunks, CHUNK_HEADS, rows), f32),
            pltpu.VMEM((cols, rows), f32),
            pltpu.VMEM((chunks, CHUNK_HEADS, rows), f32),
            pltpu.VMEM((rows, cols), bf16),
            pltpu.VMEM(hyena_inputs.shape, bf16),
            pltpu.VMEM((2, RIM, cols), bf16),
            pltpu.VMEM((RIM + rows, CHUNK_HEADS * DH), f32),
            pltpu.VMEM((rows, cols), f32),
            pltpu.VMEM((heads_size, 8, rows), f32),
            pltpu.VMEM(hyena_filter.shape, f32),
            pltpu.VMEM((1, cols), f32),
            pltpu.SemaphoreType.DMA((12, count)),
            pltpu.SemaphoreType.DMA((12, count)),
            pltpu.SemaphoreType.DMA((6,)),
        ],
        compiler_params=pltpu.CompilerParams(
            collective_id=0, has_side_effects=True, vmem_limit_bytes=52 * 1024 * 1024
        ),
    )(queries, keys, values, hyena_inputs, hyena_filter, norm_gain[None, :])


def on_device(queries, keys, values, hyena_inputs, hyena_filter, norm_gain):
    if lax.axis_size("ctx") == 2 * 4:
        return four_places(queries, keys, values, hyena_inputs, hyena_filter, norm_gain)
    row_count, col_count = queries.shape
    rim_rows = hyena_filter.shape[0] - 1
    tail_rows = hyena_inputs[1:, row_count - rim_rows :, :]
    earlier = from_behind(tail_rows, "ctx", 1)
    joined = jnp.concatenate([earlier, hyena_inputs[1:]], axis=1)
    product = joined[0].astype(jnp.float32) * joined[1].astype(jnp.float32)
    convolved = jnp.zeros((row_count, col_count), jnp.float32)
    for filter_tap in range(rim_rows + 1):
        convolved = (
            convolved
            + hyena_filter[filter_tap][None, :]
            * product[rim_rows - filter_tap : rim_rows - filter_tap + row_count]
        )
    hyena_out = hyena_inputs[0].astype(jnp.float32) * convolved
    attention = cycle_attention(queries, keys, values)
    attention_wide = lax.optimization_barrier(attention).astype(jnp.float32)
    local_squares = jnp.sum(attention_wide * attention_wide, axis=1)
    square_total = lax.psum(local_squares, "heads")
    square_mean = square_total / WIDTH
    normed = attention_wide * lax.rsqrt(square_mean + 1e-06)[:, None] * norm_gain[None, :]
    return (normed + hyena_out).astype(jnp.bfloat16)


def solution(mesh):
    placed = (
        P("ctx", "heads"),
        P("ctx", "heads"),
        P("ctx", "heads"),
        P(None, "ctx", "heads"),
        P(None, "heads"),
        P("heads"),
    )
    return jax.shard_map(
        on_device, mesh=mesh, in_specs=placed, out_specs=P("ctx", "heads"), check_vma=False
    )
```
